32 devices in a mesh: dp: 8 (over y, x, core), tensor: 4 (over z).
Axes of the slice: x: 2, y: 2, z: 4, core: 2. Of those that a mesh axis runs over, the one named last changes fastest.
Arguments:
- tokens: bfloat16 [16384, 1536], P(('dp', 'tensor')), may hold values from -6 to 6
- cotangent: bfloat16 [16384, 1536], P(('dp', 'tensor')), may hold values from -6 to 6
- lengths: int32 [8, 2], P('dp'), may hold values from 128 to 1024, as said below
- in_weight: float32 [1536, 2, 3072], P('dp', None, 'tensor'), may hold values from -0.15625 to 0.15625
- in_first: float32 [1536, 2, 3072], P('dp', None, 'tensor'), may hold values from -32 to 32
- in_second: float32 [1536, 2, 3072], P('dp', None, 'tensor'), may hold values from 107.7248 to 430.8992
- dt_weight: float32 [1536, 48], P('dp', 'tensor'), may hold values from -0.15625 to 0.15625
- dt_first: float32 [1536, 48], P('dp', 'tensor'), may hold values from -64 to 64
- dt_second: float32 [1536, 48], P('dp', 'tensor'), may hold values from 430.8992 to 1723.5968
- bc_weight: float32 [1536, 256], P(('dp', 'tensor')), may hold values from -0.15625 to 0.15625
- bc_first: float32 [1536, 256], P(('dp', 'tensor')), may hold values from -128 to 128
- bc_second: float32 [1536, 256], P(('dp', 'tensor')), may hold values from 1723.5968 to 6894.387
- out_weight: float32 [3072, 1536], P('tensor', 'dp'), may hold values from -0.109375 to 0.109375
- out_first: float32 [3072, 1536], P('tensor', 'dp'), may hold values from -64 to 64
- out_second: float32 [3072, 1536], P('tensor', 'dp'), may hold values from 430.8992 to 1723.5968
- norm_gain: float32 [1536], P(('dp', 'tensor')), may hold values from 0.5 to 1.5
- gain_first: float32 [1536], P(('dp', 'tensor')), may hold values from -40 to 40
- gain_second: float32 [1536], P(('dp', 'tensor')), may hold values from 215.4496 to 861.7984
- bc_conv: float32 [5, 256], P(None, ('dp', 'tensor')), may hold values from -3 to 3
- conv_first: float32 [5, 256], P(None, ('dp', 'tensor')), may hold values from -40 to 40
- conv_second: float32 [5, 256], P(None, ('dp', 'tensor')), may hold values from 215.4496 to 861.7984
- x_channel: float32 [6, 3072], P(None, 'tensor')
- channel_first: float32 [6, 3072], P(None, 'tensor'), may hold values from -40 to 40
- channel_second: float32 [6, 3072], P(None, 'tensor'), may hold values from 215.4496 to 861.7984
- head_params: float32 [3, 48], P(None, 'tensor')
- head_first: float32 [3, 48], P(None, 'tensor'), may hold values from -40 to 40
- head_second: float32 [3, 48], P(None, 'tensor'), may hold values from 215.4496 to 861.7984
Outputs:
- mixed: bfloat16 [16384, 1536], P(('dp', 'tensor'))
- token_grad: bfloat16 [16384, 1536], P(('dp', 'tensor'))
- in_weight_new: float32 [1536, 2, 3072], P('dp', None, 'tensor')
- in_first_new: float32 [1536, 2, 3072], P('dp', None, 'tensor')
- in_second_new: float32 [1536, 2, 3072], P('dp', None, 'tensor')
- dt_weight_new: float32 [1536, 48], P('dp', 'tensor')
- dt_first_new: float32 [1536, 48], P('dp', 'tensor')
- dt_second_new: float32 [1536, 48], P('dp', 'tensor')
- bc_weight_new: float32 [1536, 256], P(('dp', 'tensor'))
- bc_first_new: float32 [1536, 256], P(('dp', 'tensor'))
- bc_second_new: float32 [1536, 256], P(('dp', 'tensor'))
- out_weight_new: float32 [3072, 1536], P('tensor', 'dp')
- out_first_new: float32 [3072, 1536], P('tensor', 'dp')
- out_second_new: float32 [3072, 1536], P('tensor', 'dp')
- norm_gain_new: float32 [1536], P(('dp', 'tensor'))
- gain_first_new: float32 [1536], P(('dp', 'tensor'))
- gain_second_new: float32 [1536], P(('dp', 'tensor'))
- bc_conv_new: float32 [5, 256], P(None, ('dp', 'tensor'))
- conv_first_new: float32 [5, 256], P(None, ('dp', 'tensor'))
- conv_second_new: float32 [5, 256], P(None, ('dp', 'tensor'))
- x_channel_new: float32 [6, 3072], P(None, 'tensor')
- channel_first_new: float32 [6, 3072], P(None, 'tensor')
- channel_second_new: float32 [6, 3072], P(None, 'tensor')
- head_params_new: float32 [3, 48], P(None, 'tensor')
- head_first_new: float32 [3, 48], P(None, 'tensor')
- head_second_new: float32 [3, 48], P(None, 'tensor')
The draws below stay inside these ranges and needn't reach their ends.
Inputs may be any that keep to these rules, and one draw needn't show every extreme that they name: Row g holds the lengths of the 2 sequences of group g in order; the rest of the group's 2048 rows is padding. Some entry equals 1024 in every draw.
All inputs are finite; a program needn't handle non-finite values.
Results may differ from the reference program's by a relative error of at most 0.00235.
The reference program's roundings to bfloat16 on the way count: a program that leaves them out, or rounds other values in their place, can miss the bound.
Values may be sent and summed in bfloat16 or wider, within the bound.
A program may use at most 256 MiB of HBM per device.

```python
import math
import jax
import jax.numpy as jnp
from jax import lax

D = 1536
HEADS = 48
INNER = 3072
STATE = 128
KW = 4
SPAN = 256
MAXLEN = 1024
STEP = 5
CAP = 2048
GROUPS = 8
TOKENS = 16384
SEQS = 2
N_DP = 8


def draw_lengths(key, part):
    key = jax.random.fold_in(key, 11)
    first, second = jax.random.split(key)
    values = jax.random.randint(first, (GROUPS * SEQS,), MAXLEN // 8, MAXLEN + 1)
    spot = jax.random.randint(second, (), 0, GROUPS * SEQS)
    values = jnp.where(jnp.arange(GROUPS * SEQS, dtype=jnp.int32) == spot, MAXLEN, values)
    return values.reshape(GROUPS, SEQS).astype(jnp.int32)


def draw_x_channel(key, part):
    key = jax.random.fold_in(key, 5)
    first, second, third = jax.random.split(key, 3)
    kernel = 0.5 * jax.random.normal(first, (KW, INNER), jnp.float32)
    bias = 0.3 * jax.random.normal(second, (1, INNER), jnp.float32)
    places = jnp.arange(INNER, dtype=jnp.float32) / (INNER - 1)
    ramp = 1.0 + 2.0 * places
    gain = ramp * jax.random.uniform(third, (INNER,), jnp.float32, 0.8, 1.25)
    return jnp.concatenate([kernel, bias, gain[None, :]], axis=0)


def draw_head_params(key, part):
    key = jax.random.fold_in(key, 7)
    first, second, third = jax.random.split(key, 3)
    step_bias = jax.random.uniform(first, (HEADS,), jnp.float32, -2.5, -1.5)
    log_rate = jax.random.uniform(second, (HEADS,), jnp.float32, -4.5, -0.5)
    places = jnp.arange(HEADS, dtype=jnp.float32) / (HEADS - 1)
    skip_factor = (0.3 + 0.6 * places) * jax.random.uniform(third, (HEADS,), jnp.float32, 0.8, 1.25)
    return jnp.stack([step_bias, log_rate, skip_factor], axis=0)


def steps_of(stream_key, extent, cuts, low, high):
    level, own = 1.0, jax.random.fold_in(stream_key, 6)
    for position, parts in cuts:
        steps = jnp.exp(jax.random.uniform(jax.random.fold_in(own, position), (parts,), jnp.float32, low / len(cuts), high / len(cuts)))
        level = level * jnp.repeat(steps, extent[position] // parts).reshape([-1 if axis == position else 1 for axis in range(len(extent))])
    return level


def gaussian(key, dims, deviation, reach, cuts=(), held_as=jnp.bfloat16):
    drawn = deviation * jax.random.normal(key, dims, jnp.float32)
    if cuts:
        drawn = drawn * steps_of(key, dims, cuts, -0.22, 0.18)
    return jnp.clip(drawn, -reach, reach).astype(held_as)


def setup_inputs(seed: int = 0) -> dict:
    arg_keys = jax.random.split(jax.random.key(seed), 28)
    return {
        "tokens": gaussian(arg_keys[0], (TOKENS, D), 1.0, 6.0, ((0, 32),)),
        "cotangent": gaussian(arg_keys[1], (TOKENS, D), 1.0, 6.0, ((0, 32),)),
        "lengths": draw_lengths(jax.random.fold_in(arg_keys[27], 71), 0),
        "in_weight": gaussian(arg_keys[3], (D, 2, INNER), D ** -0.5, 0.15625, ((0, 8), (2, 4)), jnp.float32),
        "in_first": gaussian(arg_keys[4], (D, 2, INNER), (0.111 * (0.125 * TOKENS) ** 0.5), 32.0, ((0, 8), (2, 4)), jnp.float32),
        "in_second": jnp.clip(jnp.exp(math.log(430.8992) - 1.3862944 * jax.random.uniform(arg_keys[5], (D, 2, INNER), jnp.float32) ** steps_of(arg_keys[5], (D, 2, INNER), ((0, 8), (2, 4)), -0.2, 0.2)), 107.7248, 430.8992),
        "dt_weight": gaussian(arg_keys[6], (D, HEADS), D ** -0.5, 0.15625, ((0, 8), (1, 4)), jnp.float32),
        "dt_first": gaussian(arg_keys[7], (D, HEADS), (0.111 * (0.5 * TOKENS) ** 0.5), 64.0, ((0, 8), (1, 4)), jnp.float32),
        "dt_second": jnp.clip(jnp.exp(math.log(1723.5968) - 1.3862944 * jax.random.uniform(arg_keys[8], (D, HEADS), jnp.float32) ** steps_of(arg_keys[8], (D, HEADS), ((0, 8), (1, 4)), -0.2, 0.2)), 430.8992, 1723.5968),
        "bc_weight": gaussian(arg_keys[9], (D, 2 * STATE), D ** -0.5, 0.15625, ((0, 32),), jnp.float32),
        "bc_first": gaussian(arg_keys[10], (D, 2 * STATE), (0.111 * (2 * TOKENS) ** 0.5), 128.0, ((0, 32),), jnp.float32),
        "bc_second": jnp.clip(jnp.exp(math.log(6894.387) - 1.3862944 * jax.random.uniform(arg_keys[11], (D, 2 * STATE), jnp.float32) ** steps_of(arg_keys[11], (D, 2 * STATE), ((0, 32),), -0.2, 0.2)), 1723.5968, 6894.387),
        "out_weight": gaussian(arg_keys[12], (INNER, D), INNER ** -0.5, 0.109375, ((0, 4), (1, 8)), jnp.float32),
        "out_first": gaussian(arg_keys[13], (INNER, D), (0.111 * (0.5 * TOKENS) ** 0.5), 64.0, ((0, 4), (1, 8)), jnp.float32),
        "out_second": jnp.clip(jnp.exp(math.log(1723.5968) - 1.3862944 * jax.random.uniform(arg_keys[14], (INNER, D), jnp.float32) ** steps_of(arg_keys[14], (INNER, D), ((0, 4), (1, 8)), -0.2, 0.2)), 430.8992, 1723.5968),
        "norm_gain": jnp.clip(1.0 + 0.1 * jax.random.normal(arg_keys[15], (D,), jnp.float32), 0.5, 1.5),
        "gain_first": gaussian(arg_keys[16], (D,), (0.111 * (0.25 * TOKENS) ** 0.5), 40.0, ((0, 32),), jnp.float32),
        "gain_second": jnp.clip(jnp.exp(math.log(861.7984) - 1.3862944 * jax.random.uniform(arg_keys[17], (D,), jnp.float32) ** steps_of(arg_keys[17], (D,), ((0, 32),), -0.2, 0.2)), 215.4496, 861.7984),
        "bc_conv": gaussian(arg_keys[18], (KW + 1, 2 * STATE), 0.5, 3.0, ((1, 32),), jnp.float32),
        "conv_first": gaussian(arg_keys[19], (KW + 1, 2 * STATE), (0.111 * (0.25 * TOKENS) ** 0.5), 40.0, ((1, 32),), jnp.float32),
        "conv_second": jnp.clip(jnp.exp(math.log(861.7984) - 1.3862944 * jax.random.uniform(arg_keys[20], (KW + 1, 2 * STATE), jnp.float32) ** steps_of(arg_keys[20], (KW + 1, 2 * STATE), ((1, 32),), -0.2, 0.2)), 215.4496, 861.7984),
        "x_channel": draw_x_channel(jax.random.fold_in(arg_keys[27], 71), 0),
        "channel_first": gaussian(arg_keys[22], (KW + 2, INNER), (0.111 * (0.25 * TOKENS) ** 0.5), 40.0, ((1, 4),), jnp.float32),
        "channel_second": jnp.clip(jnp.exp(math.log(861.7984) - 1.3862944 * jax.random.uniform(arg_keys[23], (KW + 2, INNER), jnp.float32) ** steps_of(arg_keys[23], (KW + 2, INNER), ((1, 4),), -0.2, 0.2)), 215.4496, 861.7984),
        "head_params": draw_head_params(jax.random.fold_in(arg_keys[27], 71), 0),
        "head_first": gaussian(arg_keys[25], (3, HEADS), (0.111 * (0.25 * TOKENS) ** 0.5), 40.0, ((1, 4),), jnp.float32),
        "head_second": jnp.clip(jnp.exp(math.log(861.7984) - 1.3862944 * jax.random.uniform(arg_keys[26], (3, HEADS), jnp.float32) ** steps_of(arg_keys[26], (3, HEADS), ((1, 4),), -0.2, 0.2)), 215.4496, 861.7984),
    }


@jax.custom_vjp
def low(v):
    return lax.optimization_barrier(v.astype(jnp.bfloat16)).astype(jnp.float32)

@jax.custom_vjp
def low_back(v):
    return v

def low_keep(v):
    return (low(v), None)

def low_pass(kept, grad):
    return (grad,)

def back_keep(v):
    return (v, None)

def back_low(kept, grad):
    return (low(grad),)
low.defvjp(low_keep, low_pass)
low_back.defvjp(back_keep, back_low)
epsilon = 1e-05
adam_epsilon = 1e-08
beta_first = 0.9
beta_second = 0.95
rate_matrix = 0.02
rate_small = 0.2
decay_matrix = 0.1
highest = lax.Precision.HIGHEST

def segments(lengths_row, total):
    ends = jnp.cumsum(lengths_row).astype(jnp.int32)
    places = jnp.arange(total, dtype=jnp.int32)
    labels = lax.optimization_barrier(jnp.sum((places[:, None] >= ends[None, :]).astype(jnp.int32), axis=1)).astype(jnp.int32)
    valid = (places < ends[-1]).astype(jnp.float32)
    return (labels, valid)

def causal_conv(values, kernel, bias, labels):
    width = kernel.shape[0]
    result = values * kernel[width - 1][None, :] + bias[None, :]
    for offset in range(1, width):
        moved = jnp.concatenate([jnp.zeros((offset, values.shape[1]), jnp.float32), values[:-offset]], axis=0)
        earlier = jnp.concatenate([jnp.full((offset,), -1, jnp.int32), labels[:-offset]], axis=0)
        same_seq = (earlier == labels).astype(jnp.float32)
        result = result + moved * same_seq[:, None] * kernel[width - 1 - offset][None, :]
    return result

def state_space(values, step_sizes, rates, in_mat, read_mat, labels):
    total, heads, width = values.shape
    count = total // SPAN
    lower = jnp.tril(jnp.ones((SPAN, SPAN), jnp.float32))

    def advance(carry, block):
        state, last_label = carry
        value_block, step_block, in_block, read_block, label_block = block
        log_decay = step_block * rates[None, :]
        cumulative = jnp.dot(lower, log_decay, precision=highest)
        same_seq = (label_block[:, None] == label_block[None, :]).astype(jnp.float32) * lower
        log_gaps = jnp.minimum(cumulative[:, None, :] - cumulative[None, :, :], 0.0)
        scores = jnp.dot(read_block, in_block.T, precision=highest)
        mixing = jnp.exp(log_gaps) * (same_seq * scores)[:, :, None] * step_block[None, :, :]
        intra = jnp.einsum('ijh,jhp->ihp', mixing, value_block, precision=highest)
        keep_first = (label_block == last_label).astype(jnp.float32)
        carried = jnp.einsum('in,hpn->ihp', read_block, state, precision=highest)
        carried = carried * (keep_first[:, None] * jnp.exp(cumulative))[:, :, None]
        tail_weight = (label_block == label_block[-1]).astype(jnp.float32)[:, None]
        tail_weight = tail_weight * jnp.exp(cumulative[-1][None, :] - cumulative) * step_block
        keep_last = (label_block[-1] == last_label).astype(jnp.float32)
        renewed = state * (keep_last * jnp.exp(cumulative[-1]))[:, None, None]
        renewed = renewed + jnp.einsum('jh,jhp,jn->hpn', tail_weight, value_block, in_block, precision=highest)
        return ((renewed, label_block[-1]), intra + carried)
    blocks = (values.reshape(count, SPAN, heads, width), step_sizes.reshape(count, SPAN, heads), in_mat.reshape(count, SPAN, in_mat.shape[1]), read_mat.reshape(count, SPAN, read_mat.shape[1]), labels.reshape(count, SPAN))
    start = (jnp.zeros((heads, width, in_mat.shape[1]), jnp.float32), jnp.array(-1, dtype=jnp.int32))
    _, result = lax.scan(jax.checkpoint(advance), start, blocks)
    return result.reshape(total, heads, width)

def mixer_part(proj, x_channel, head_params, bc_conv, labels):
    total = proj.shape[0]
    local = x_channel.shape[1]
    heads = head_params.shape[1]
    gate_cols = proj[:, :local]
    stream = proj[:, local:2 * local]
    step_raw = proj[:, 2 * local:2 * local + heads]
    shared = proj[:, 2 * local + heads:]
    conv_stream = jax.nn.silu(causal_conv(stream, x_channel[:KW], x_channel[KW], labels))
    conv_shared = jax.nn.silu(causal_conv(shared, bc_conv[:KW], bc_conv[KW], labels))
    step_sizes = jax.nn.softplus(step_raw + head_params[0][None, :])
    rates = -jnp.exp(head_params[1])
    values = conv_stream.reshape(total, heads, local // heads)
    result = state_space(values, step_sizes, rates, conv_shared[:, :STATE], conv_shared[:, STATE:], labels)
    result = result + head_params[2][None, :, None] * values
    return result.reshape(total, local) * jax.nn.silu(gate_cols)

def group_forward(rows, in_weight, dt_weight, bc_weight, out_weight, norm_gain, bc_conv, x_channel, head_params, labels, valid):
    rstd_in = lax.rsqrt(lax.optimization_barrier(jnp.mean(rows * rows, axis=1, keepdims=True)) + epsilon)
    normed = low(rows * rstd_in * norm_gain[None, :])
    weights = jnp.concatenate([low(in_weight).reshape(D, 2 * INNER), low(dt_weight), low(bc_weight)], axis=1)
    proj = low_back(jnp.dot(normed, weights, precision=highest))
    gated_raw = mixer_part(proj, x_channel, head_params, bc_conv, labels)
    rstd = lax.rsqrt(lax.optimization_barrier(jnp.mean(gated_raw * gated_raw, axis=1, keepdims=True)) + epsilon)
    gated = low(gated_raw * rstd * x_channel[KW + 1][None, :])
    mixed = jnp.dot(gated, low(out_weight), precision=highest)
    return rows + valid[:, None] * mixed

def adam_update(weight, grad, first, second, rate, decay):
    first_new = beta_first * first + (1.0 - beta_first) * grad
    second_new = beta_second * second + (1.0 - beta_second) * grad * grad
    first_hat = first_new / (1.0 - beta_first ** STEP)
    second_hat = second_new / (1.0 - beta_second ** STEP)
    weight_new = weight * (1.0 - rate * decay) - rate * first_hat / (jnp.sqrt(second_hat) + adam_epsilon)
    return (weight_new, first_new, second_new)

def reference(tokens, cotangent, lengths, in_weight, in_first, in_second, dt_weight, dt_first, dt_second, bc_weight, bc_first, bc_second, out_weight, out_first, out_second, norm_gain, gain_first, gain_second, bc_conv, conv_first, conv_second, x_channel, channel_first, channel_second, head_params, head_first, head_second):
    weights = (in_weight, dt_weight, bc_weight, out_weight, norm_gain, bc_conv, x_channel, head_params)

    def one_group(totals, block):
        rows, back_rows, lengths_row = block
        labels, valid = segments(lengths_row, CAP)

        def forward(rows_in, *params):
            return group_forward(rows_in, *params, labels, valid)
        result, pull = jax.vjp(forward, rows.astype(jnp.float32), *weights)
        grads = pull(back_rows.astype(jnp.float32))
        totals = tuple((a + b for a, b in zip(totals, grads[1:])))
        return (totals, (result.astype(jnp.bfloat16), grads[0].astype(jnp.bfloat16)))
    zeros = tuple((jnp.zeros_like(w) for w in weights))
    blocks = (tokens.reshape(N_DP, CAP, D), cotangent.reshape(N_DP, CAP, D), lengths)
    totals, (mixed, token_grad) = lax.scan(one_group, zeros, blocks)
    mixed = mixed.reshape(TOKENS, D)
    token_grad = token_grad.reshape(TOKENS, D)
    g_in, g_dt, g_bc, g_out, g_gain, g_conv, g_channel, g_head = totals
    in_new = adam_update(in_weight, g_in, in_first, in_second, rate_matrix, decay_matrix)
    dt_new = adam_update(dt_weight, g_dt, dt_first, dt_second, rate_matrix, decay_matrix)
    bc_new = adam_update(bc_weight, g_bc, bc_first, bc_second, rate_matrix, decay_matrix)
    out_new = adam_update(out_weight, g_out, out_first, out_second, rate_matrix, decay_matrix)
    gain_new = adam_update(norm_gain, g_gain, gain_first, gain_second, rate_small, 0.0)
    conv_new = adam_update(bc_conv, g_conv, conv_first, conv_second, rate_small, 0.0)
    channel_new = adam_update(x_channel, g_channel, channel_first, channel_second, rate_small, 0.0)
    head_new = adam_update(head_params, g_head, head_first, head_second, rate_small, 0.0)
    return (mixed, token_grad, in_new[0], in_new[1], in_new[2], dt_new[0], dt_new[1], dt_new[2], bc_new[0], bc_new[1], bc_new[2], out_new[0], out_new[1], out_new[2], gain_new[0], gain_new[1], gain_new[2], conv_new[0], conv_new[1], conv_new[2], channel_new[0], channel_new[1], channel_new[2], head_new[0], head_new[1], head_new[2])
```

```python
import functools

import jax
import jax.numpy as jnp
from jax import lax
from jax.experimental import pallas as pl
from jax.experimental.pallas import tpu as pltpu
from jax.sharding import PartitionSpec as P

STATE = 128
KW = 4
STEP = 5
HALO = 16
BLOCK = 256
PWIDTH = 64
LOG2E = 1.4426950408889634

epsilon = 1e-05
adam_epsilon = 1e-08
beta_first = 0.9
beta_second = 0.95
rate_matrix = 0.02
rate_small = 0.2
decay_matrix = 0.1
highest = lax.Precision.HIGHEST

f32 = jnp.float32
bf16 = jnp.bfloat16
NN = (((1,), (0,)), ((), ()))
NT = (((1,), (1,)), ((), ()))
TN = (((0,), (0,)), ((), ()))


def dot(a, b, dims=NN):
    return lax.dot_general(a, b, dims, preferred_element_type=f32)


def halves(a):
    high = a.astype(bf16)
    return high, (a - high.astype(f32)).astype(bf16)


def dot3(a, b, dims=NN):
    ah, al = halves(a)
    bh, bl = halves(b)
    return dot(ah, bh, dims) + (dot(ah, bl, dims) + dot(al, bh, dims))


def sigmoid(v):
    return 1.0 / (1.0 + jnp.exp(-v))


def low_lanes(rows):
    return lax.broadcasted_iota(jnp.int32, (rows, 2 * PWIDTH), 1) < PWIDTH


def spread(cols, field, heads):
    rows = cols.shape[0]
    low = low_lanes(rows)
    parts = []
    for pair in range(heads // 2):
        at = field * heads + 2 * pair
        parts.append(jnp.where(low, cols[:, at : at + 1], cols[:, at + 1 : at + 2]))
    return parts[0] if len(parts) == 1 else jnp.concatenate(parts, axis=1)


def shifted(stream_ref, rows, offset):
    return stream_ref[pl.ds(HALO - offset, rows), :]


def conv_of(stream_ref, chan, masks, rows):
    pre = chan[KW : KW + 1, :] + chan[KW - 1 : KW, :] * shifted(stream_ref, rows, 0)
    for offset in range(1, KW):
        tap = chan[KW - 1 - offset : KW - offset, :]
        pre = pre + tap * (masks[:, offset - 1 : offset] * shifted(stream_ref, rows, offset))
    return pre


def tiles_of(rows):
    size = min(BLOCK, rows)
    return size, rows // size


def decay_tile(cols, lines, heads, head, i, j, size):
    gap = cols[i * size : (i + 1) * size, heads + head : heads + head + 1]
    gap = gap - lines[head : head + 1, j * size : (j + 1) * size]
    if i == j:
        gap = jnp.minimum(gap, 0.0)
    return jnp.exp2(gap)


def stream_kernel(heads, nh, w, chan, masks, cols, in_mat, ps_out, xc_out, add_out):
    rows = in_mat.shape[0]
    ps_out[...] = dot(nh[...], w[...])
    pre = conv_of(ps_out, chan[...], masks[...], rows)
    xc = pre * sigmoid(pre)
    xc_out[...] = xc
    weight = spread(cols[...], 0, heads) * spread(cols[...], 3, heads)
    add_out[...] = dot3(xc * weight, in_mat[...], TN)


def scan_kernel(heads, nh, w, xc, cols, lines, scores, read_mat, state, chan, z_out, y_out, sq_out):
    rows = xc.shape[0]
    size, count = tiles_of(rows)
    step = pl.program_id(0)
    z = dot(nh[pl.ds(HALO, rows), :], w[...])
    z_out[...] = z
    col = cols[...]
    line = lines[...]
    x = xc[...]
    scaled = x * spread(col, 0, heads)
    carried = dot3(read_mat[...], state[...], NT) * spread(col, 2, heads)
    low = low_lanes(size)
    parts = []
    for pair in range(heads // 2):
        xh, xl = halves(scaled[:, pair * 128 : (pair + 1) * 128])
        both = jnp.concatenate([xh, xl], axis=1)
        tiles = []
        for i in range(count):
            outs = []
            for half in range(2):
                acc = jnp.zeros((size, 256), f32)
                for j in range(i + 1):
                    decay = decay_tile(col, line, heads, 2 * pair + half, i, j, size)
                    mix = decay * scores[i * size : (i + 1) * size, j * size : (j + 1) * size]
                    mh, ml = halves(mix)
                    part = both[j * size : (j + 1) * size]
                    acc = acc + dot(mh, part) + dot(ml, part)
                outs.append(acc[:, :128] + acc[:, 128:])
            tiles.append(jnp.where(low, outs[0], outs[1]))
        parts.append(jnp.concatenate(tiles, axis=0))
    y = jnp.concatenate(parts, axis=1) + carried if len(parts) > 1 else parts[0] + carried
    y_out[...] = y
    g = (y + chan[KW + 2 : KW + 3, :] * x) * (z * sigmoid(z))
    sq = g * g
    total = sq[:, :128]
    for at in range(128, sq.shape[1], 128):
        total = total + sq[:, at : at + 128]

    @pl.when(step == 0)
    def _():
        sq_out[...] = total

    @pl.when(step > 0)
    def _():
        sq_out[...] += total


def gate_parts(z, y, xc, chan):
    full = y[...] + chan[KW + 2 : KW + 3, :] * xc[...]
    zv = z[...]
    sig = sigmoid(zv)
    return full, zv, sig


def out_kernel(z, y, xc, chan, rstd, w, e, x, valid, mixed_out, dg_out, dw_out, gain_out, s_out, acc):
    step, steps = pl.program_id(0), pl.num_programs(0)
    full, zv, sig = gate_parts(z, y, xc, chan)
    g = full * (zv * sig)
    gain = chan[KW + 1 : KW + 2, :]
    scaled = g * rstd[...]
    gated = (scaled * gain).astype(bf16)
    wv = w[...]
    part = dot(gated, wv, NT)
    d_gated = dot(e[...], wv)
    dg_out[...] = d_gated
    dw_out[...] = dot(e[...], gated, TN).astype(dw_out.dtype)
    gain_out[...] = jnp.sum(scaled * d_gated, axis=0, keepdims=True)
    prod = g * gain * d_gated
    total = prod[:, :128]
    for at in range(128, prod.shape[1], 128):
        total = total + prod[:, at : at + 128]

    @pl.when(step == 0)
    def _():
        acc[...] = part
        s_out[...] = total

    @pl.when(step > 0)
    def _():
        acc[...] += part
        s_out[...] += total

    @pl.when(step == steps - 1)
    def _():
        mixed_out[...] = (x[...].astype(f32) + valid[...] * acc[...]).astype(bf16)


def gate_kernel(heads, inner, z, y, xc, chan, rstd, s, dgat, w, n, cols, read_mat, dy_out, dw_out, dh_out, add_out, skip_out):
    step = pl.program_id(0)
    full, zv, sig = gate_parts(z, y, xc, chan)
    gate = zv * sig
    r = rstd[...]
    d_g = r * chan[KW + 1 : KW + 2, :] * dgat[...] - full * gate * (r * r * r * (s[...] / inner))
    dy = d_g * gate
    dy_out[...] = dy
    dz = (d_g * full * (sig * (1.0 + zv * (1.0 - sig)))).astype(bf16)
    dw_out[...] = dot(n[...], dz, TN).astype(dw_out.dtype)
    part = dot(dz, w[...], NT)
    add_out[...] = dot3(dy * spread(cols[...], 2, heads), read_mat[...], TN)
    skip_out[...] = jnp.sum(dy * xc[...], axis=0, keepdims=True)

    @pl.when(step == 0)
    def _():
        dh_out[...] = part

    @pl.when(step > 0)
    def _():
        dh_out[...] += part


def head_sums(prod, heads):
    width = prod.shape[1]
    owner = lax.broadcasted_iota(jnp.int32, (width, 128), 0) // PWIDTH
    pick = (owner == lax.broadcasted_iota(jnp.int32, (width, 128), 1)).astype(bf16)
    high, low = halves(prod)
    return dot(high, pick) + dot(low, pick)


def back_kernel(heads, dy, xc, ps, y, cols, lines, scores, mask, in_mat, read_mat, back_state, state, chan, masks,
                pre_out, sums_out, rows_out, db_out, dc_out, dsc):
    rows = xc.shape[0]
    size, count = tiles_of(rows)
    step, steps = pl.program_id(0), pl.num_programs(0)

    @pl.when(step == 0)
    def _():
        dsc[...] = jnp.zeros_like(dsc)
        db_out[...] = jnp.zeros_like(db_out)
        dc_out[...] = jnp.zeros_like(dc_out)

    col = cols[...]
    line = lines[...]
    x = xc[...]
    d_y = dy[...]
    steps_wide = spread(col, 0, heads)
    scaled = x * steps_wide
    low = low_lanes(rows)
    low_tile = low_lanes(size)
    parts = []
    for pair in range(heads // 2):
        at = slice(pair * 128, (pair + 1) * 128)
        xv, dv = scaled[:, at], d_y[:, at]
        dh, dl = halves(dv)
        both = jnp.concatenate([dh, dl], axis=1)
        xh_f, dh_f = xv.astype(bf16).astype(f32), dv.astype(bf16).astype(f32)
        xl_f, dl_f = xv - xh_f, dv - dh_f
        xh_r, dl_r = pltpu.roll(xh_f, PWIDTH, 1), pltpu.roll(dl_f, PWIDTH, 1)
        tops = [[None, None] for _ in range(count)]
        for half in range(2):
            if half == 0:
                left = [jnp.where(low, dh_f, dl_r), jnp.where(low, dh_f, 0.0)]
                right = [jnp.where(low, xh_f, xh_r), jnp.where(low, xl_f, 0.0)]
            else:
                left = [jnp.where(low, dl_r, dh_f), jnp.where(low, 0.0, dh_f)]
                right = [jnp.where(low, xh_r, xh_f), jnp.where(low, 0.0, xl_f)]
            left = jnp.concatenate(left, axis=1).astype(bf16)
            right = jnp.concatenate(right, axis=1).astype(bf16)
            for j in range(count):
                acc = jnp.zeros((size, 256), f32)
                for i in range(j, count):
                    ti, tj = slice(i * size, (i + 1) * size), slice(j * size, (j + 1) * size)
                    decay = decay_tile(col, line, heads, 2 * pair + half, i, j, size)
                    mh, ml = halves(decay * scores[ti, tj])
                    dsc[ti, tj] += dot(left[ti], right[tj], NT) * decay
                    acc = acc + dot(mh, both[ti], TN) + dot(ml, both[ti], TN)
                tops[j][half] = acc[:, :128] + acc[:, 128:]
        parts.append(jnp.concatenate([jnp.where(low_tile, a, b) for a, b in tops], axis=0))
    inside = jnp.concatenate(parts, axis=1) if len(parts) > 1 else parts[0]
    tail = dot3(in_mat[...], back_state[...], NT) * spread(col, 3, heads)
    d_scaled = inside + tail
    q = head_sums(d_y * y[...] - scaled * inside, heads)
    u = head_sums(scaled * tail, heads)
    r = head_sums(x * d_scaled, heads)
    sums_out[...] = jnp.concatenate([q[:, :heads], u[:, :heads], r[:, :heads]], axis=1)
    db_out[...] += dot3(scaled * spread(col, 3, heads), back_state[...])
    dc_out[...] += dot3(d_y * spread(col, 2, heads), state[...])
    d_x = d_scaled * steps_wide + chan[KW + 2 : KW + 3, :] * d_y
    chan_v, masks_v = chan[...], masks[...]
    pre = conv_of(ps, chan_v, masks_v, rows)
    sig = sigmoid(pre)
    d_pre = d_x * (sig * (1.0 + pre * (1.0 - sig)))
    pre_out[...] = d_pre
    taps = []
    for k in range(KW):
        offset = KW - 1 - k
        moved = shifted(ps, rows, offset)
        if offset:
            moved = moved * masks_v[:, offset - 1 : offset]
        taps.append(jnp.sum(d_pre * moved, axis=0, keepdims=True))
    taps.append(jnp.sum(d_pre, axis=0, keepdims=True))
    taps.append(jnp.zeros((8 - KW - 1, d_pre.shape[1]), f32))
    rows_out[...] = jnp.concatenate(taps, axis=0)

    @pl.when(step == steps - 1)
    def _():
        d_scores = dsc[...] * mask[...].astype(f32)
        dc_out[...] += dot3(d_scores, in_mat[...])
        db_out[...] += dot3(d_scores, read_mat[...], TN)


def stream_back_kernel(pre, halo, chan, masks, w, n, dh_in, dw_out, dh_out, ext):
    rows = pre.shape[0]
    step = pl.program_id(0)
    ext[pl.ds(0, rows), :] = pre[...]
    ext[pl.ds(rows, 8), :] = halo[...]
    chan_v = chan[...]
    d_ps = chan_v[KW - 1 : KW, :] * pre[...]
    for offset in range(1, KW):
        tap = chan_v[KW - 1 - offset : KW - offset, :]
        moved = ext[pl.ds(offset, rows), :] * masks[pl.ds(offset, rows), offset - 1 : offset]
        d_ps = d_ps + tap * moved
    d_ps = d_ps.astype(bf16)
    dw_out[...] = dot(n[...], d_ps, TN).astype(dw_out.dtype)
    part = dot(d_ps, w[...], NT)

    @pl.when(step == 0)
    def _():
        dh_out[...] = dh_in[...] + part

    @pl.when(step > 0)
    def _():
        dh_out[...] += part


def kernel_call(kernel, grid, ins, outs, scratch=(), flops=0, bytes_=0):
    def spec(shape, block, index):
        if block is None:
            rank = len(shape)
            return pl.BlockSpec(shape, lambda i, rank=rank: (0,) * rank)
        return pl.BlockSpec(block, index)

    return pl.pallas_call(
        kernel,
        grid=(grid,),
        in_specs=[spec(a.shape, b, m) for a, b, m in ins],
        out_specs=[spec(s, b, m) for s, _, b, m in outs],
        out_shape=[jax.ShapeDtypeStruct(s, d) for s, d, _, _ in outs],
        scratch_shapes=list(scratch),
        compiler_params=pltpu.CompilerParams(
            dimension_semantics=("arbitrary",), vmem_limit_bytes=58 * 1024 * 1024
        ),
        cost_estimate=pl.CostEstimate(flops=flops, bytes_accessed=bytes_, transcendentals=0),
    )(*[a for a, _, _ in ins])


def adam_update(weight, grad, first, second, rate, decay):
    first_new = beta_first * first + (1.0 - beta_first) * grad
    second_new = beta_second * second + (1.0 - beta_second) * grad * grad
    first_hat = first_new / (1.0 - beta_first**STEP)
    second_hat = second_new / (1.0 - beta_second**STEP)
    weight_new = weight * (1.0 - rate * decay) - rate * first_hat / (
        jnp.sqrt(second_hat) + adam_epsilon
    )
    return (weight_new, first_new, second_new)


def gather_slabs(shard):
    return lax.all_gather(lax.all_gather(shard, "tensor", axis=0), "dp", axis=1, tiled=True)


def scatter_slabs(part):
    own = lax.psum_scatter(part, "dp", scatter_dimension=1, tiled=True)
    return lax.psum_scatter(own, "tensor", scatter_dimension=0, tiled=True)[0]


def conv_rows(stream, kernel, masks, rows):
    pre = kernel[KW][None, :] + kernel[KW - 1][None, :] * stream[HALO:]
    for offset in range(1, KW):
        moved = stream[HALO - offset : HALO - offset + rows]
        pre = pre + kernel[KW - 1 - offset][None, :] * (masks[:rows, offset - 1 : offset] * moved)
    return pre


def body(
    tokens,
    cotangent,
    lengths,
    in_weight,
    in_first,
    in_second,
    dt_weight,
    dt_first,
    dt_second,
    bc_weight,
    bc_first,
    bc_second,
    out_weight,
    out_first,
    out_second,
    norm_gain,
    gain_first,
    gain_second,
    bc_conv,
    conv_first,
    conv_second,
    x_channel,
    channel_first,
    channel_second,
    head_params,
    head_first,
    head_second,
):
    n_dp, n_t = lax.axis_size("dp"), lax.axis_size("tensor")
    me = lax.axis_index("tensor")
    rows, width = tokens.shape
    local = x_channel.shape[1]
    inner = local * n_t
    local_heads = head_params.shape[1]
    all_heads = local_heads * n_t
    cb = BLOCK if local % BLOCK == 0 else 128
    per = local // cb
    blocks = inner // cb
    hb = cb // PWIDTH
    own = me * rows
    up = [(i, i + 1) for i in range(n_t - 1)]
    down = [(i + 1, i) for i in range(n_t - 1)]

    w_s = gather_slabs(in_weight[:, 1].astype(bf16))
    w_z = gather_slabs(in_weight[:, 0].astype(bf16))
    w_o = gather_slabs(out_weight.T.astype(bf16))
    small = [
        bc_weight,
        dt_weight,
        norm_gain,
        bc_conv,
        x_channel,
        head_params,
    ]
    sizes = [a.size for a in small]
    flat = jnp.concatenate([a.reshape(-1) for a in small])
    flat = lax.all_gather(flat, ("dp", "tensor"), axis=0)
    ends = [sum(sizes[: i + 1]) for i in range(len(sizes))]
    bc_all, dt_all, gain_all, conv_all, chan_all, head_all = (
        flat[:, e - s : e] for s, e in zip(sizes, ends)
    )
    bc_low = bc_all.reshape(width, -1).astype(bf16)
    dt_low = dt_all.reshape(n_dp, n_t, -1, local_heads).swapaxes(1, 2).reshape(width, all_heads).astype(bf16)
    gain = gain_all.reshape(width)
    conv_full = conv_all.reshape(n_dp * n_t, KW + 1, -1).swapaxes(0, 1).reshape(KW + 1, -1)
    channel = chan_all[:n_t].reshape(n_t, KW + 2, local)
    heads = head_all[:n_t].reshape(n_t, 3, local_heads).swapaxes(0, 1).reshape(3, all_heads)
    skip = jnp.repeat(heads[2], PWIDTH).reshape(n_t, 1, local)
    chan = jnp.concatenate([channel, skip, jnp.zeros((n_t, 1, local), f32)], axis=1)

    ends_of = jnp.cumsum(lengths[0])

    def labels_at(places):
        found = jnp.sum((places[:, None] >= ends_of[None, :]).astype(jnp.int32), axis=1)
        return jnp.where(places < 0, -1, found)

    span = labels_at(own + jnp.arange(-HALO, rows + 8, dtype=jnp.int32))
    labels = span[HALO : HALO + rows]
    valid = (own + jnp.arange(rows, dtype=jnp.int32) < ends_of[-1]).astype(f32)[:, None]
    masks = jnp.stack(
        [(span[HALO - o : HALO - o + rows + 8] == span[HALO:]).astype(f32) for o in (1, 2, 3)], axis=1
    )
    before, last = span[HALO - 1], labels[rows - 1]
    keep = (labels == before).astype(f32)[:, None]
    tail = (labels == last).astype(f32)[:, None]
    through = (last == before).astype(f32)
    tril = jnp.tril(jnp.ones((rows, rows), f32))
    same = (labels[:, None] == labels[None, :]).astype(f32) * tril

    prior = lax.ppermute(tokens[-HALO:], "tensor", up)
    x_ext = jnp.concatenate([prior, tokens], axis=0).astype(f32)
    rstd_ext = lax.rsqrt(jnp.mean(x_ext * x_ext, axis=1, keepdims=True) + epsilon)
    normed_ext = (x_ext * rstd_ext * gain[None, :]).astype(bf16)
    x, rstd_in, normed = x_ext[HALO:], rstd_ext[HALO:], normed_ext[HALO:]

    bcp = dot(normed_ext, bc_low)
    bc_pre = conv_rows(bcp, conv_full, masks, rows)
    bc_sig = sigmoid(bc_pre)
    bcc = bc_pre * bc_sig
    in_mat, read_mat = bcc[:, :STATE], bcc[:, STATE:]
    step_raw = dot(normed, dt_low) + heads[0][None, :]
    step = jax.nn.softplus(step_raw)
    rates = -jnp.exp(heads[1])
    cum = jnp.dot(tril, step * rates[None, :], precision=highest)
    decay_in = keep * jnp.exp(cum)
    decay_out = tail * jnp.exp(cum[-1:] - cum)
    decay_all = through * jnp.exp(cum[-1])
    scores = same * lax.dot_general(read_mat, in_mat, NT, precision=highest)
    cum2 = cum * LOG2E
    cols = jnp.stack([step, cum2, decay_in, decay_out], axis=1)
    cols = cols.reshape(rows, 4, blocks, hb).transpose(2, 0, 1, 3).reshape(blocks, rows, 4 * hb)
    lines = cum2.T.reshape(blocks, hb, rows)

    def slab(i):
        return (i // per, 0, i % per)

    wspec = (None, width, cb), slab
    cspec = (None, 8, cb), slab
    colspec = (None, rows, 4 * hb), lambda i: (i, 0, 0)
    linespec = (None, hb, rows), lambda i: (i, 0, 0)
    chspec = (rows, cb), lambda i: (0, i)
    stspec = (cb, STATE), lambda i: (i, 0)
    full = (None, None)
    big = 2 * rows * width * inner

    ps, xc, added = kernel_call(
        functools.partial(stream_kernel, hb),
        blocks,
        [(normed_ext, *full), (w_s, *wspec), (chan, *cspec), (masks[:rows], *full), (cols, *colspec), (in_mat, *full)],
        [
            ((rows + HALO, inner), f32, (rows + HALO, cb), lambda i: (0, i)),
            ((rows, inner), f32, *chspec),
            ((inner, STATE), f32, *stspec),
        ],
        flops=big,
        bytes_=4 * width * inner,
    )

    decays = lax.all_gather(decay_all, "tensor", axis=0)

    def wide(v):
        return jnp.repeat(v, PWIDTH)[:, None]

    parts = lax.all_gather(added.astype(bf16), "tensor", axis=0)
    run = jnp.ones((all_heads,), f32)
    state = jnp.zeros((inner, STATE), f32)
    for other in reversed(range(n_t)):
        ahead = other < me
        state = state + wide(jnp.where(ahead, run, 0.0)) * parts[other].astype(f32)
        run = jnp.where(ahead, run * decays[other], run)

    z, y, squares = kernel_call(
        functools.partial(scan_kernel, hb),
        blocks,
        [
            (normed_ext, *full),
            (w_z, *wspec),
            (xc, *chspec),
            (cols, *colspec),
            (lines, *linespec),
            (scores, *full),
            (read_mat, *full),
            (state, *stspec),
            (chan, *cspec),
        ],
        [
            ((rows, inner), f32, *chspec),
            ((rows, inner), f32, *chspec),
            ((rows, 128), f32, *full),
        ],
        flops=2 * big,
        bytes_=8 * width * inner,
    )
    rstd = lax.rsqrt(jnp.sum(squares, axis=1, keepdims=True) / inner + epsilon)
    back = cotangent.astype(f32)
    masked = (back * valid).astype(bf16)

    mixed, d_gated, dw_o, d_gain_gate, totals = kernel_call(
        out_kernel,
        blocks,
        [
            (z, *chspec),
            (y, *chspec),
            (xc, *chspec),
            (chan, *cspec),
            (rstd, *full),
            (w_o, *wspec),
            (masked, *full),
            (tokens, *full),
            (valid, *full),
        ],
        [
            ((rows, width), bf16, *full),
            ((rows, inner), f32, *chspec),
            ((n_t, width, local), f32, *wspec),
            ((1, inner), f32, (1, cb), lambda i: (0, i)),
            ((rows, 128), f32, *full),
        ],
        scratch=[pltpu.VMEM((rows, width), f32)],
        flops=3 * big,
        bytes_=8 * width * inner,
    )
    total = jnp.sum(totals, axis=1, keepdims=True)

    dy, dw_z, dh, back_added, skip_rows = kernel_call(
        functools.partial(gate_kernel, hb, inner),
        blocks,
        [
            (z, *chspec),
            (y, *chspec),
            (xc, *chspec),
            (chan, *cspec),
            (rstd, *full),
            (total, *full),
            (d_gated, *chspec),
            (w_z, *wspec),
            (normed, *full),
            (cols, *colspec),
            (read_mat, *full),
        ],
        [
            ((rows, inner), f32, *chspec),
            ((n_t, width, local), f32, *wspec),
            ((rows, width), f32, *full),
            ((inner, STATE), f32, *stspec),
            ((1, inner), f32, (1, cb), lambda i: (0, i)),
        ],
        flops=2 * big,
        bytes_=8 * width * inner,
    )
    parts = lax.all_gather(back_added.astype(bf16), "tensor", axis=0)
    run = jnp.ones((all_heads,), f32)
    back_state = jnp.zeros((inner, STATE), f32)
    for other in range(n_t):
        behind = other > me
        back_state = back_state + wide(jnp.where(behind, run, 0.0)) * parts[other].astype(f32)
        run = jnp.where(behind, run * decays[other], run)

    d_pre, sums, tap_rows, d_in_mat, d_read_mat = kernel_call(
        functools.partial(back_kernel, hb),
        blocks,
        [
            (dy, *chspec),
            (xc, *chspec),
            (ps, (rows + HALO, cb), lambda i: (0, i)),
            (y, *chspec),
            (cols, *colspec),
            (lines, *linespec),
            (scores, *full),
            (same.astype(bf16), *full),
            (in_mat, *full),
            (read_mat, *full),
            (back_state, *stspec),
            (state, *stspec),
            (chan, *cspec),
            (masks[:rows], *full),
        ],
        [
            ((rows, inner), f32, *chspec),
            ((blocks, rows, 3 * hb), f32, (None, rows, 3 * hb), lambda i: (i, 0, 0)),
            ((8, inner), f32, (8, cb), lambda i: (0, i)),
            ((rows, STATE), f32, *full),
            ((rows, STATE), f32, *full),
        ],
        scratch=[pltpu.VMEM((rows, rows), f32)],
        flops=2 * big,
        bytes_=8 * width * inner,
    )
    halo = lax.ppermute(d_pre[:8], "tensor", down)

    sums = sums.reshape(blocks, rows, 3, hb).transpose(2, 1, 0, 3).reshape(3, rows, all_heads)
    crossing = decay_all * jnp.sum((back_state * state).reshape(all_heads, -1), axis=1)
    d_log = (
        jnp.dot(tril.T, sums[0], precision=highest)
        + jnp.dot(tril - jnp.eye(rows, dtype=f32), sums[1], precision=highest)
        + crossing[None, :]
    )
    d_step = rates[None, :] * d_log + sums[2]
    d_rates = jnp.sum(d_log * step, axis=0)
    d_step_raw = d_step * jax.nn.sigmoid(step_raw)
    d_heads = jnp.stack(
        [
            jnp.sum(d_step_raw, axis=0),
            d_rates * rates,
            jnp.sum(skip_rows.reshape(all_heads, PWIDTH), axis=1),
        ]
    )
    d_dt = d_step_raw.astype(bf16)
    d_bc_pre = jnp.concatenate([d_in_mat, d_read_mat], axis=1) * (bc_sig * (1.0 + bc_pre * (1.0 - bc_sig)))
    d_conv = [
        jnp.sum(
            d_bc_pre
            * bcp[HALO - (KW - 1 - k) : HALO - (KW - 1 - k) + rows]
            * (masks[:rows, KW - 2 - k : KW - 1 - k] if k < KW - 1 else 1.0),
            axis=0,
        )
        for k in range(KW)
    ] + [jnp.sum(d_bc_pre, axis=0)]
    d_conv = jnp.stack(d_conv)
    bc_halo = lax.ppermute(d_bc_pre[:8], "tensor", down)
    bc_ext = jnp.concatenate([d_bc_pre, bc_halo], axis=0)
    d_bc = conv_full[KW - 1][None, :] * d_bc_pre
    for o in range(1, KW):
        d_bc = d_bc + conv_full[KW - 1 - o][None, :] * (
            masks[o : o + rows, o - 1 : o] * bc_ext[o : o + rows]
        )
    d_bc = d_bc.astype(bf16)

    dw_s, dh = kernel_call(
        stream_back_kernel,
        blocks,
        [
            (d_pre, *chspec),
            (halo, (8, cb), lambda i: (0, i)),
            (chan, *cspec),
            (masks, *full),
            (w_s, *wspec),
            (normed, *full),
            (dh, *full),
        ],
        [
            ((n_t, width, local), f32, *wspec),
            ((rows, width), f32, *full),
        ],
        scratch=[pltpu.VMEM((rows + 8, cb), f32)],
        flops=2 * big,
        bytes_=8 * width * inner,
    )
    d_normed = dh + dot(d_bc, bc_low, NT) + dot(d_dt, dt_low, NT)
    dw_bc = dot(normed, d_bc, TN)
    dw_dt = dot(normed, d_dt, TN)
    scaled = gain[None, :] * d_normed
    token_grad = (
        back + rstd_in * scaled - x * rstd_in**3 * jnp.sum(x * scaled, axis=1, keepdims=True) / width
    ).astype(bf16)
    d_gain = jnp.sum(x * rstd_in * d_normed, axis=0)

    g_s, g_z, g_o = scatter_slabs(dw_s), scatter_slabs(dw_z), scatter_slabs(dw_o)
    d_channel = jnp.concatenate([tap_rows[: KW + 1], d_gain_gate], axis=0)
    by_t = [
        d_channel.reshape(KW + 2, n_t, local).swapaxes(0, 1).reshape(n_t, -1),
        d_heads.reshape(3, n_t, local_heads).swapaxes(0, 1).reshape(n_t, -1),
    ]
    by_t = jnp.concatenate(by_t, axis=1)
    pieces = [
        dw_bc.reshape(n_dp, n_t, -1),
        dw_dt.reshape(n_dp, -1, n_t, local_heads).swapaxes(1, 2).reshape(n_dp, n_t, -1),
        d_gain.reshape(n_dp, n_t, -1),
        d_conv.reshape(KW + 1, n_dp, n_t, -1).transpose(1, 2, 0, 3).reshape(n_dp, n_t, -1),
        jnp.broadcast_to(by_t[None], (n_dp, *by_t.shape)),
    ]
    packed = jnp.concatenate(pieces, axis=2).reshape(n_dp * n_t, -1)
    mine = lax.psum_scatter(packed, ("dp", "tensor"), scatter_dimension=0, tiled=True)[0]
    g_bc, g_dt, g_gain, g_conv, g_channel, g_head = (
        mine[e - s : e].reshape(a.shape) for a, s, e in zip(small, sizes, ends)
    )
    g_in = jnp.stack([g_z, g_s], axis=1)
    in_new = adam_update(in_weight, g_in, in_first, in_second, rate_matrix, decay_matrix)
    dt_new = adam_update(dt_weight, g_dt, dt_first, dt_second, rate_matrix, decay_matrix)
    bc_new = adam_update(bc_weight, g_bc, bc_first, bc_second, rate_matrix, decay_matrix)
    out_new = adam_update(out_weight, g_o.T, out_first, out_second, rate_matrix, decay_matrix)
    gain_new = adam_update(norm_gain, g_gain, gain_first, gain_second, rate_small, 0.0)
    conv_new = adam_update(bc_conv, g_conv, conv_first, conv_second, rate_small, 0.0)
    channel_new = adam_update(x_channel, g_channel, channel_first, channel_second, rate_small, 0.0)
    head_new = adam_update(head_params, g_head, head_first, head_second, rate_small, 0.0)
    return (
        mixed,
        token_grad,
        *in_new,
        *dt_new,
        *bc_new,
        *out_new,
        *gain_new,
        *conv_new,
        *channel_new,
        *head_new,
    )


def solution(mesh):
    return jax.shard_map(
        body,
        mesh=mesh,
        in_specs=(
            P(("dp", "tensor"), None),
            P(("dp", "tensor"), None),
            P("dp", None),
            P("dp", None, "tensor"),
            P("dp", None, "tensor"),
            P("dp", None, "tensor"),
            P("dp", "tensor"),
            P("dp", "tensor"),
            P("dp", "tensor"),
            P(("dp", "tensor"), None),
            P(("dp", "tensor"), None),
            P(("dp", "tensor"), None),
            P("tensor", "dp"),
            P("tensor", "dp"),
            P("tensor", "dp"),
            P(("dp", "tensor")),
            P(("dp", "tensor")),
            P(("dp", "tensor")),
            P(None, ("dp", "tensor")),
            P(None, ("dp", "tensor")),
            P(None, ("dp", "tensor")),
            P(None, "tensor"),
            P(None, "tensor"),
            P(None, "tensor"),
            P(None, "tensor"),
            P(None, "tensor"),
            P(None, "tensor"),
        ),
        out_specs=(
            P(("dp", "tensor"), None),
            P(("dp", "tensor"), None),
            P("dp", None, "tensor"),
            P("dp", None, "tensor"),
            P("dp", None, "tensor"),
            P("dp", "tensor"),
            P("dp", "tensor"),
            P("dp", "tensor"),
            P(("dp", "tensor"), None),
            P(("dp", "tensor"), None),
            P(("dp", "tensor"), None),
            P("tensor", "dp"),
            P("tensor", "dp"),
            P("tensor", "dp"),
            P(("dp", "tensor")),
            P(("dp", "tensor")),
            P(("dp", "tensor")),
            P(None, ("dp", "tensor")),
            P(None, ("dp", "tensor")),
            P(None, ("dp", "tensor")),
            P(None, "tensor"),
            P(None, "tensor"),
            P(None, "tensor"),
            P(None, "tensor"),
            P(None, "tensor"),
            P(None, "tensor"),
        ),
        check_vma=False,
    )
```

```python
import functools

import jax
import jax.numpy as jnp
from jax import lax
from jax.experimental import pallas as pl
from jax.experimental.pallas import tpu as pltpu
from jax.sharding import PartitionSpec as P

STATE = 128
KW = 4
STEP = 5
HALO = 16
BLOCK = 256
PWIDTH = 64
LOG2E = 1.4426950408889634

epsilon = 1e-05
adam_epsilon = 1e-08
beta_first = 0.9
beta_second = 0.95
rate_matrix = 0.02
rate_small = 0.2
decay_matrix = 0.1
highest = lax.Precision.HIGHEST

f32 = jnp.float32
bf16 = jnp.bfloat16
NN = (((1,), (0,)), ((), ()))
NT = (((1,), (1,)), ((), ()))
TN = (((0,), (0,)), ((), ()))


def dot(a, b, dims=NN):
    return lax.dot_general(a, b, dims, preferred_element_type=f32)


def halves(a):
    high = a.astype(bf16)
    return high, (a - high.astype(f32)).astype(bf16)


def dot3(a, b, dims=NN):
    ah, al = halves(a)
    bh, bl = halves(b)
    return dot(ah, bh, dims) + (dot(ah, bl, dims) + dot(al, bh, dims))


def sigmoid(v):
    return 1.0 / (1.0 + jnp.exp(-v))


def low_lanes(rows):
    return lax.broadcasted_iota(jnp.int32, (rows, 2 * PWIDTH), 1) < PWIDTH


def dot_exact(ones, a):
    high = a.astype(bf16)
    rest = a - high.astype(f32)
    middle = rest.astype(bf16)
    low = (rest - middle.astype(f32)).astype(bf16)
    return dot(ones, high) + (dot(ones, middle) + dot(ones, low))


EXTRA = 16
FULL = 32000.0


def column_exponent(value):
    most = jnp.max(jnp.abs(value), axis=0, keepdims=True)
    return jnp.floor(jnp.log2(jnp.maximum(most, 1e-30))) + 1.0


def put_codes(ref, start, value, exponent):
    codes = jnp.round(value * (FULL * jnp.exp2(-exponent)))
    ref[start : start + value.shape[0], :] = codes.astype(jnp.int32).astype(jnp.int16)


def put_exponent(ref, exponent):
    rows = ref.shape[0]
    wide = jnp.broadcast_to(exponent, (EXTRA, exponent.shape[1]))
    ref[rows - EXTRA : rows, :] = wide.astype(jnp.int32).astype(jnp.int16)


def exponent_in(ref):
    rows = ref.shape[0]
    return ref[rows - EXTRA : rows, :].astype(jnp.int32).astype(f32)[:1]


def codes_in(ref, start, rows, exponent):
    codes = ref[start : start + rows, :].astype(jnp.int32).astype(f32)
    return codes * (jnp.exp2(exponent) / FULL)


def store_product(value, refs):
    if len(refs) == 1:
        refs[0][...] = value
        return
    exponent = column_exponent(value)
    size = value.shape[0] // len(refs)
    for at, ref in enumerate(refs):
        put_codes(ref, 0, value[at * size : (at + 1) * size], exponent)
        put_exponent(ref, exponent)


def core_sum_kernel(keep, got, x_out, y_out, keep_out):
    rows = (keep.shape[0] - EXTRA) // 4
    half = rows // 2
    mine, there = exponent_in(keep), exponent_in(got)
    exponent = jnp.maximum(mine, there) + 1.0

    def total(part, second):
        start = part * rows + second * half
        return codes_in(keep, start, half, mine) + codes_in(got, start, half, there)

    for ref, parts in (
        (x_out, ((1, 0), (3, 0))),
        (y_out, ((2, 1), (3, 1))),
        (keep_out, ((0, 0), (2, 0), (0, 1), (1, 1))),
    ):
        for at, (part, second) in enumerate(parts):
            put_codes(ref, at * half, total(part, second), exponent)
        put_exponent(ref, exponent)


def cross_sum_kernel(keep, x_got, y_got, y_out, x_out, keep_out, exponent_out):
    half = (y_out.shape[0] - EXTRA)
    mine, x_there, y_there = exponent_in(keep), exponent_in(x_got), exponent_in(y_got)
    own_a = codes_in(keep, 0, half, mine) + codes_in(x_got, 0, half, x_there)
    far_a = codes_in(keep, half, half, mine) + codes_in(x_got, half, half, x_there)
    own_b = codes_in(keep, 2 * half, half, mine) + codes_in(y_got, 0, half, y_there)
    far_b = codes_in(keep, 3 * half, half, mine) + codes_in(y_got, half, half, y_there)
    exp_a, exp_b = jnp.maximum(mine, x_there) + 1.0, jnp.maximum(mine, y_there) + 1.0
    put_codes(y_out, 0, far_a, exp_a)
    put_exponent(y_out, exp_a)
    put_codes(x_out, 0, far_b, exp_b)
    put_exponent(x_out, exp_b)
    keep_out[0:half, :] = own_a
    keep_out[half : 2 * half, :] = own_b
    exponent_out[...] = jnp.broadcast_to(jnp.maximum(exp_a, exp_b), exponent_out.shape)


def plane_sum_kernel(keep, exponent_ref, y_got, x_got, own_out, z_out):
    half = keep.shape[0] // 2
    y_there, x_there = exponent_in(y_got), exponent_in(x_got)
    own_a = keep[0:half, :] + codes_in(y_got, 0, half, y_there)
    own_b = keep[half : 2 * half, :] + codes_in(x_got, 0, half, x_there)
    exponent = jnp.maximum(jnp.maximum(y_there, x_there), exponent_ref[0:1, :]) + 1.0
    put_codes(z_out, 0, own_a, exponent)
    put_codes(z_out, half, own_b, exponent)
    put_exponent(z_out, exponent)

    @pl.when(pl.program_id(0) == 0)
    def _():
        own_out[0:half, :] = own_a
        own_out[half : 2 * half, :] = own_b


def spread(cols, field, heads):
    rows = cols.shape[0]
    low = low_lanes(rows)
    parts = []
    for pair in range(heads // 2):
        at = field * heads + 2 * pair
        parts.append(jnp.where(low, cols[:, at : at + 1], cols[:, at + 1 : at + 2]))
    return parts[0] if len(parts) == 1 else jnp.concatenate(parts, axis=1)


def shifted(stream_ref, rows, offset):
    return stream_ref[pl.ds(HALO - offset, rows), :]


def conv_of(stream_ref, chan, masks, rows):
    pre = chan[KW : KW + 1, :] + chan[KW - 1 : KW, :] * shifted(stream_ref, rows, 0)
    for offset in range(1, KW):
        tap = chan[KW - 1 - offset : KW - offset, :]
        pre = pre + tap * (masks[:, offset - 1 : offset] * shifted(stream_ref, rows, offset))
    return pre


def tiles_of(rows):
    size = min(BLOCK, rows)
    return size, rows // size


def decay_tile(cols, lines, heads, head, i, j, size):
    gap = cols[i * size : (i + 1) * size, heads + head : heads + head + 1]
    gap = gap - lines[head : head + 1, j * size : (j + 1) * size]
    if i == j:
        gap = jnp.minimum(gap, 0.0)
    return jnp.exp2(gap)


def field_columns(fields, groups):
    size = fields[0].shape[1] // groups
    return [jnp.concatenate([f[:, g * size : (g + 1) * size] for f in fields], axis=1) for g in range(groups)]


def small_kernel(nh, wbc, wdt, conv, marks, line_label, heads, bcp_out, pre_out, raw_out, step_out, in_out, read_out,
                 in_t_out, read_t_out, wide_out, narrow_out, lines_out, scores_out, through_out):
    rows = step_out.shape[0]
    bcp_out[...] = dot(nh[...], wbc[...])
    masks = marks[...]
    pre = conv_of(bcp_out, conv[...], masks, rows)
    pre_out[...] = pre
    bcc = pre * sigmoid(pre)
    in_mat, read_mat = bcc[:, :STATE], bcc[:, STATE:]
    in_out[...] = in_mat
    read_out[...] = read_mat
    in_t_out[...] = in_mat.T
    read_t_out[...] = read_mat.T
    raw = dot(nh[pl.ds(HALO, rows), :], wdt[...]) + heads[0:1, :]
    raw_out[...] = raw
    step = jnp.maximum(raw, 0.0) + jnp.log1p(jnp.exp(-jnp.abs(raw)))
    step_out[...] = step
    log_decay = step * (-jnp.exp(heads[1:2, :]))
    label, keep, tail, through = masks[:, 3:4], masks[:, 4:5], masks[:, 5:6], masks[0:1, 6:7]
    row_at = lax.broadcasted_iota(jnp.int32, (rows, rows), 0)
    col_at = lax.broadcasted_iota(jnp.int32, (rows, rows), 1)
    lower = row_at >= col_at
    cum = dot_exact(jnp.where(lower, 1.0, 0.0).astype(bf16), log_decay)
    end = cum[rows - 1 : rows, :]
    through_out[...] = jnp.broadcast_to(through * jnp.exp(end), through_out.shape)
    cum2 = cum * LOG2E
    fields = [step, cum2, keep * jnp.exp(cum), tail * jnp.exp(end - cum)]
    for at, group in enumerate(field_columns(fields, wide_out.shape[0])):
        wide_out[at] = group
    for at, group in enumerate(field_columns(fields, narrow_out.shape[0])):
        narrow_out[at] = group
    padded = jnp.concatenate([cum2, jnp.zeros((rows, 128 - cum2.shape[1]), f32)], axis=1)
    lines_out[...] = padded.T[: lines_out.shape[0]]
    same = jnp.logical_and(lower, label == line_label[0:1, :])
    scores_out[...] = jnp.where(same, dot3(read_mat, in_mat, NT), 0.0)


def stream_kernel(heads, nh, w, chan, masks, cols, in_t, ps_out, xc_out, add_out):
    rows = in_t.shape[1]
    ps_out[...] = dot(nh[...], w[...])
    pre = conv_of(ps_out, chan[...], masks[...], rows)
    xc = pre * sigmoid(pre)
    xc_out[...] = xc
    weight = spread(cols[...], 0, heads) * spread(cols[...], 3, heads)
    add_out[...] = dot3(in_t[...], xc * weight)


CARRY_LAG = 2


class Carry:
    def __init__(self, n_t, upward, added, decay, enters, out_codes, in_codes, send_sem, recv_sem):
        self.n_t, self.added, self.decay, self.enters = n_t, added, decay, enters
        self.out_codes, self.in_codes, self.send_sem, self.recv_sem = out_codes, in_codes, send_sem, recv_sem
        me = lax.axis_index("tensor")
        self.dp, self.me = lax.axis_index("dp"), me
        self.at = me if upward else n_t - 1 - me
        self.following = lax.rem(me + (1 if upward else n_t - 1), n_t)
        self.chunks, _, self.size = out_codes.shape
        self.ticks = self.chunks + CARRY_LAG * (n_t - 1)

    def meet(self):
        barrier = pltpu.get_barrier_semaphore()
        for there in (1, self.n_t - 1):
            pl.semaphore_signal(
                barrier, inc=1, device_id=(self.dp, lax.rem(self.me + there, self.n_t)), device_id_type=pl.DeviceIdType.MESH
            )
        pl.semaphore_wait(barrier, 2)

    def copy(self, chunk):
        return pltpu.make_async_remote_copy(
            src_ref=self.out_codes.at[chunk], dst_ref=self.in_codes.at[chunk],
            send_sem=self.send_sem.at[chunk], recv_sem=self.recv_sem.at[chunk],
            device_id=(self.dp, self.following), device_id_type=pl.DeviceIdType.MESH,
        )

    def tick(self, number):
        chunk = number - CARRY_LAG * self.at

        @pl.when(jnp.logical_and(chunk >= 0, chunk < self.chunks))
        def _():
            lanes = pl.ds(pl.multiple_of(chunk * self.size, 128), self.size)

            @pl.when(self.at == 0)
            def _():
                self.enters[:, lanes] = jnp.zeros((STATE, self.size), f32)

            @pl.when(self.at > 0)
            def _():
                self.copy(chunk).wait_recv()
                came = self.in_codes.at[chunk]
                self.enters[:, lanes] = codes_in(came, 0, STATE, exponent_in(came))

            @pl.when(self.at < self.n_t - 1)
            def _():
                value = self.added[:, lanes] + self.decay[0:1, lanes] * self.enters[:, lanes]
                exponent = column_exponent(value)
                put_codes(self.out_codes.at[chunk], 0, value, exponent)
                put_exponent(self.out_codes.at[chunk], exponent)
                self.copy(chunk).start()

    def finish(self):
        @pl.when(self.at < self.n_t - 1)
        def _():
            for chunk in range(self.chunks):
                self.copy(chunk).wait_send()


def carry_scratch(chunks, size):
    return [
        pltpu.VMEM((chunks, STATE + EXTRA, size), jnp.int16),
        pltpu.VMEM((chunks, STATE + EXTRA, size), jnp.int16),
        pltpu.SemaphoreType.DMA((chunks,)),
        pltpu.SemaphoreType.DMA((chunks,)),
    ]


def inside_kernel(heads, n_t, xc, cols, lines, scores, added, decay, y_out, enters, *scratch):
    rows = xc.shape[0]
    step, steps = pl.program_id(0), pl.num_programs(0)
    carry = Carry(n_t, True, added, decay, enters, *scratch)

    @pl.when(step == 0)
    def _():
        carry.meet()

    carry.tick(step)
    size, count = tiles_of(rows)
    col = cols[...]
    line = lines[...]
    scaled = xc[...] * spread(col, 0, heads)
    low = low_lanes(size)
    for pair in range(heads // 2):
        xh, xl = halves(scaled[:, pair * 128 : (pair + 1) * 128])
        both = jnp.concatenate([xh, xl], axis=1)
        for i in range(count):
            outs = []
            for half in range(2):
                acc = jnp.zeros((size, 256), f32)
                for j in range(i + 1):
                    decay_here = decay_tile(col, line, heads, 2 * pair + half, i, j, size)
                    mix = decay_here * scores[i * size : (i + 1) * size, j * size : (j + 1) * size]
                    mh, ml = halves(mix)
                    part = both[j * size : (j + 1) * size]
                    acc = acc + dot(mh, part) + dot(ml, part)
                outs.append(acc[:, :128] + acc[:, 128:])
            y_out[i * size : (i + 1) * size, pair * 128 : (pair + 1) * 128] = jnp.where(low, outs[0], outs[1])

    @pl.when(step == steps - 1)
    def _():
        @pl.loop(carry.chunks, carry.ticks)
        def _(number):
            carry.tick(number)

        carry.finish()


def carry_kernel(heads, nh, w, inside, xc, cols, read_mat, state, chan, z_out, y_out, sq_out):
    rows = xc.shape[0]
    step = pl.program_id(0)
    z = dot(nh[pl.ds(HALO, rows), :], w[...])
    z_out[...] = z
    y = inside[...] + dot3(read_mat[...], state[...]) * spread(cols[...], 2, heads)
    y_out[...] = y
    g = (y + chan[KW + 2 : KW + 3, :] * xc[...]) * (z * sigmoid(z))
    sq = g * g
    total = sq[:, :128]
    for at in range(128, sq.shape[1], 128):
        total = total + sq[:, at : at + 128]

    @pl.when(step == 0)
    def _():
        sq_out[...] = total

    @pl.when(step > 0)
    def _():
        sq_out[...] += total


def gate_parts(z, y, xc, chan):
    full = y[...] + chan[KW + 2 : KW + 3, :] * xc[...]
    zv = z[...]
    sig = sigmoid(zv)
    return full, zv, sig


def out_kernel(me, z, y, xc, chan, rstd, w, e, et, x, valid, mixed_out, dg_out, gain_out, s_out, *rest):
    dw_out, acc = rest[:-1], rest[-1]
    step, steps = pl.program_id(0), pl.num_programs(0)
    full, zv, sig = gate_parts(z, y, xc, chan)
    g = full * (zv * sig)
    gain = chan[KW + 1 : KW + 2, :]
    scaled = g * rstd[...]
    gated = (scaled * gain).astype(bf16)
    wv = w[...]
    part = dot(gated, wv, NT)
    d_gated = dot(e[...], wv)
    dg_out[...] = d_gated
    store_product(dot(et[...], gated), dw_out)
    gain_out[...] = jnp.sum(scaled * d_gated, axis=0, keepdims=True)
    prod = g * gain * d_gated
    total = prod[:, :128]
    for at in range(128, prod.shape[1], 128):
        total = total + prod[:, at : at + 128]

    @pl.when(step == 0)
    def _():
        acc[...] = part
        s_out[...] = total

    @pl.when(step > 0)
    def _():
        acc[...] += part
        s_out[...] += total

    @pl.when(step == steps - 1)
    def _():
        mixed_out[...] = (x[...].astype(f32) + valid[...] * acc[...]).astype(bf16)


def gate_kernel(heads, inner, me, z, y, xc, chan, rstd, s, dgat, w, nt, cols, read_t, dy_out, dh_out, add_out, skip_out, *dw_out):
    step = pl.program_id(0)
    full, zv, sig = gate_parts(z, y, xc, chan)
    gate = zv * sig
    r = rstd[...]
    d_g = r * chan[KW + 1 : KW + 2, :] * dgat[...] - full * gate * (r * r * r * (s[...] / inner))
    dy = d_g * gate
    dy_out[...] = dy
    dz = (d_g * full * (sig * (1.0 + zv * (1.0 - sig)))).astype(bf16)
    store_product(dot(nt[...], dz), dw_out)
    part = dot(dz, w[...], NT)
    add_out[...] = dot3(read_t[...], dy * spread(cols[...], 2, heads))
    skip_out[...] = jnp.sum(dy * xc[...], axis=0, keepdims=True)

    @pl.when(step == 0)
    def _():
        dh_out[...] = part

    @pl.when(step > 0)
    def _():
        dh_out[...] += part


def head_sums(prod, heads):
    width = prod.shape[1]
    owner = lax.broadcasted_iota(jnp.int32, (width, 128), 0) // PWIDTH
    pick = (owner == lax.broadcasted_iota(jnp.int32, (width, 128), 1)).astype(bf16)
    high, low = halves(prod)
    return dot(high, pick) + dot(low, pick)


def inside_back_kernel(heads, n_t, dy, xc, y, cols, lines, scores, marks, line_label, in_mat, read_mat, added, decay_row,
                       dx_out, sums_out, db_out, dc_out, enters, dsc, *scratch):
    rows = xc.shape[0]
    size, count = tiles_of(rows)
    step, steps = pl.program_id(0), pl.num_programs(0)
    carry = Carry(n_t, False, added, decay_row, enters, *scratch)

    @pl.when(step == 0)
    def _():
        dsc[...] = jnp.zeros_like(dsc)
        carry.meet()

    carry.tick(step)

    col = cols[...]
    line = lines[...]
    d_y = dy[...]
    d_yt = d_y.T
    scaled = xc[...] * spread(col, 0, heads)
    low = low_lanes(rows)
    pieces = []
    for pair in range(heads // 2):
        at = slice(pair * 128, (pair + 1) * 128)
        xv, dv = scaled[:, at], d_y[:, at]
        th, tl = halves(d_yt[at])
        xh_f, dh_f = xv.astype(bf16).astype(f32), dv.astype(bf16).astype(f32)
        xl_f, dl_f = xv - xh_f, dv - dh_f
        xh_r, dl_r = pltpu.roll(xh_f, PWIDTH, 1), pltpu.roll(dl_f, PWIDTH, 1)
        for half in range(2):
            if half == 0:
                left = [jnp.where(low, dh_f, dl_r), jnp.where(low, dh_f, 0.0)]
                right = [jnp.where(low, xh_f, xh_r), jnp.where(low, xl_f, 0.0)]
            else:
                left = [jnp.where(low, dl_r, dh_f), jnp.where(low, 0.0, dh_f)]
                right = [jnp.where(low, xh_r, xh_f), jnp.where(low, 0.0, xl_f)]
            left = jnp.concatenate(left, axis=1).astype(bf16)
            right = jnp.concatenate(right, axis=1).astype(bf16)
            own = slice(half * PWIDTH, (half + 1) * PWIDTH)
            turned = jnp.concatenate([th[own], tl[own]], axis=0)
            tiles = []
            for j in range(count):
                acc = jnp.zeros((2 * PWIDTH, size), f32)
                for i in range(j, count):
                    ti, tj = slice(i * size, (i + 1) * size), slice(j * size, (j + 1) * size)
                    decay = decay_tile(col, line, heads, 2 * pair + half, i, j, size)
                    mh, ml = halves(decay * scores[ti, tj])
                    dsc[ti, tj] += dot(left[ti], right[tj], NT) * decay
                    acc = acc + dot(turned[:, ti], mh) + dot(turned[:, ti], ml)
                tiles.append(acc[:PWIDTH] + acc[PWIDTH:])
            pieces.append(jnp.concatenate(tiles, axis=1) if count > 1 else tiles[0])
    inside = jnp.concatenate(pieces, axis=0).T
    dx_out[...] = inside
    sums_out[...] = head_sums(d_y * y[...] - scaled * inside, heads)[:, :heads]

    @pl.when(step == steps - 1)
    def _():
        row_at = lax.broadcasted_iota(jnp.int32, (rows, rows), 0)
        col_at = lax.broadcasted_iota(jnp.int32, (rows, rows), 1)
        same = jnp.logical_and(row_at >= col_at, marks[:, 3:4] == line_label[0:1, :])
        d_scores = jnp.where(same, dsc[...], 0.0)
        dc_out[...] = dot3(d_scores, in_mat[...])
        db_out[...] = dot3(d_scores.T, read_mat[...])

        @pl.loop(carry.chunks, carry.ticks)
        def _(number):
            carry.tick(number)

        carry.finish()


def carry_back_kernel(heads, dy, xc, ps, inside, cols, in_mat, back_state, state, chan, masks, db_in, dc_in,
                      pre_out, sums_out, rows_out, db_out, dc_out):
    rows = xc.shape[0]
    step = pl.program_id(0)

    @pl.when(step == 0)
    def _():
        db_out[...] = db_in[...]
        dc_out[...] = dc_in[...]

    col = cols[...]
    x = xc[...]
    d_y = dy[...]
    steps_wide, out_wide = spread(col, 0, heads), spread(col, 3, heads)
    scaled = x * steps_wide
    tail = dot3(in_mat[...], back_state[...]) * out_wide
    d_scaled = inside[...] + tail
    u = head_sums(scaled * tail, heads)
    r = head_sums(x * d_scaled, heads)
    sums_out[...] = jnp.concatenate([u[:, :heads], r[:, :heads]], axis=1)
    db_out[...] += dot3(scaled * out_wide, back_state[...], NT)
    dc_out[...] += dot3(d_y * spread(col, 2, heads), state[...], NT)
    d_x = d_scaled * steps_wide + chan[KW + 2 : KW + 3, :] * d_y
    chan_v, masks_v = chan[...], masks[...]
    pre = conv_of(ps, chan_v, masks_v, rows)
    sig = sigmoid(pre)
    d_pre = d_x * (sig * (1.0 + pre * (1.0 - sig)))
    pre_out[...] = d_pre
    taps = []
    for k in range(KW):
        offset = KW - 1 - k
        moved = shifted(ps, rows, offset)
        if offset:
            moved = moved * masks_v[:, offset - 1 : offset]
        taps.append(jnp.sum(d_pre * moved, axis=0, keepdims=True))
    taps.append(jnp.sum(d_pre, axis=0, keepdims=True))
    taps.append(jnp.sum(back_state[...] * state[...], axis=0, keepdims=True))
    taps.append(jnp.zeros((8 - KW - 2, d_pre.shape[1]), f32))
    rows_out[...] = jnp.concatenate(taps, axis=0)


def stream_back_kernel(me, pre, halo, chan, masks, w, nt, dh_in, dh_out, *rest):
    dw_out, ext = rest[:-1], rest[-1]
    rows = pre.shape[0]
    step = pl.program_id(0)
    ext[pl.ds(0, rows), :] = pre[...]
    ext[pl.ds(rows, 8), :] = halo[...]
    chan_v = chan[...]
    d_ps = chan_v[KW - 1 : KW, :] * pre[...]
    for offset in range(1, KW):
        tap = chan_v[KW - 1 - offset : KW - offset, :]
        moved = ext[pl.ds(offset, rows), :] * masks[pl.ds(offset, rows), offset - 1 : offset]
        d_ps = d_ps + tap * moved
    d_ps = d_ps.astype(bf16)
    store_product(dot(nt[...], d_ps), dw_out)
    part = dot(d_ps, w[...], NT)

    @pl.when(step == 0)
    def _():
        dh_out[...] = dh_in[...] + part

    @pl.when(step > 0)
    def _():
        dh_out[...] += part


def gather_columns(ref, field, fields):
    size = ref.shape[2] // fields
    return jnp.concatenate([ref[g][:, field * size : (field + 1) * size] for g in range(ref.shape[0])], axis=1)


def post_kernel(sums, more, raw, step, heads, through, taps, db, dc, pre, bcp, masks, pre_out, dt_out, head_out, conv_out):
    rows, count = raw.shape
    row_at = lax.broadcasted_iota(jnp.int32, (rows, rows), 0)
    col_at = lax.broadcasted_iota(jnp.int32, (rows, rows), 1)
    upper = jnp.where(col_at >= row_at, 1.0, 0.0).astype(bf16)
    below = jnp.where(col_at < row_at, 1.0, 0.0).astype(bf16)
    q, u, r = gather_columns(sums, 0, 1), gather_columns(more, 0, 2), gather_columns(more, 1, 2)
    crossing = head_sums(taps[...], count)[KW + 1 : KW + 2, :count] * through[0:1, :]
    d_log = dot_exact(upper, q) + dot_exact(below, u) + crossing
    rates = -jnp.exp(heads[1:2, :])
    d_raw = (rates * d_log + r) * sigmoid(raw[...])
    dt_out[...] = d_raw.astype(bf16)
    head_out[...] = jnp.concatenate(
        [
            jnp.sum(d_raw, axis=0, keepdims=True),
            jnp.sum(d_log * step[...], axis=0, keepdims=True) * rates,
            jnp.zeros((6, count), f32),
        ],
        axis=0,
    )
    prev = pre[...]
    sig = sigmoid(prev)
    d_pre = jnp.concatenate([db[...], dc[...]], axis=1) * (sig * (1.0 + prev * (1.0 - sig)))
    pre_out[...] = d_pre
    out = []
    for tap in range(KW):
        offset = KW - 1 - tap
        moved = shifted(bcp, rows, offset)
        if offset:
            moved = moved * masks[:, offset - 1 : offset]
        out.append(jnp.sum(d_pre * moved, axis=0, keepdims=True))
    out.append(jnp.sum(d_pre, axis=0, keepdims=True))
    out.append(jnp.zeros((8 - KW - 1, d_pre.shape[1]), f32))
    conv_out[...] = jnp.concatenate(out, axis=0)


def conv_back(ext, chan, masks, rows):
    total = chan[KW - 1 : KW, :] * ext[pl.ds(0, rows), :]
    for offset in range(1, KW):
        tap = chan[KW - 1 - offset : KW - offset, :]
        total = total + tap * (ext[pl.ds(offset, rows), :] * masks[pl.ds(offset, rows), offset - 1 : offset])
    return total


def tail_kernel(n_t, pre, w, dh_in, halo, chan, masks, nt, small_pre, small_halo, conv, d_dt, w_small, by_t, conv_rows_in,
                x, back, rstd, gain,
                g_out, token_out, small_out, by_t_out, tiny_out,
                pre_ring, w_ring, acc, ext, small_ext, load_sem, acc_sem,
                p_send, p_keep, p_got, x_pay, y_pay, x_got, y_got, keep1, y_pay2, x_pay2, y_got2, x_got2, keep2, exp2_ref,
                z_pay, z_got,
                s_send, s_keep, s_core, s_x, s_xgot, s_y, s_ygot, s_z, s_zgot,
                t_acc, t_got, b_acc, b_zgot, b_got,
                send_sem, recv_sem):
    rows, columns = pre_ring.shape[1:]
    dp, me = lax.axis_index("dp"), lax.axis_index("tensor")
    core, xn, yn = flip(dp, 1), flip(dp, 2), flip(dp, 4)
    others = [flip_all(me, r) for r in range(1, n_t)]
    order = list(range(n_t - 1, -1, -1))
    slabs = [flip_all(me, r) for r in order]
    barrier = pltpu.get_barrier_semaphore()
    for there in (core, xn, yn):
        pl.semaphore_signal(barrier, inc=1, device_id=(there, me), device_id_type=MESH)
    for there in others:
        pl.semaphore_signal(barrier, inc=1, device_id=(dp, there), device_id_type=MESH)
    pl.semaphore_wait(barrier, 3 + len(others))
    used, started = [0], []

    def send(src, dst, device):
        at = used[0]
        used[0] += 1
        copy = pltpu.make_async_remote_copy(
            src_ref=src, dst_ref=dst, send_sem=send_sem.at[at], recv_sem=recv_sem.at[at],
            device_id=device, device_id_type=MESH,
        )
        copy.start()
        started.append(copy)
        return copy

    def loads(i):
        lanes = pl.ds(pl.multiple_of(slabs[i] * columns, 128), columns)
        copies = [
            pltpu.make_async_copy(pre.at[:, lanes], pre_ring.at[i % 2], load_sem.at[0, i]),
            pltpu.make_async_copy(w.at[slabs[i]], w_ring.at[i % 2], load_sem.at[1, i]),
        ]
        for copy in copies:
            copy.start()
        return copies

    dh_copy = pltpu.make_async_copy(dh_in, acc, acc_sem)
    dh_copy.start()
    waiting = {0: loads(0)}

    small_ext[pl.ds(0, rows), :] = small_pre[...]
    small_ext[pl.ds(rows, 8), :] = small_halo[...]
    d_bc = conv_back(small_ext, conv, masks, rows).astype(bf16)
    wide = w_small.shape[1]
    d_small = jnp.concatenate([d_bc.astype(f32), d_dt[...].astype(f32)], axis=1)
    d_small = jnp.concatenate([d_small, jnp.zeros((rows, wide - d_small.shape[1]), f32)], axis=1).astype(bf16)
    half = nt.shape[0] // 2
    part = half // 4
    s_send[...] = dot(nt[pl.ds(half, half), :], d_small)
    s_keep[...] = dot(nt[pl.ds(0, half), :], d_small)
    c_core = send(s_send, s_core, (core, me))
    b_first = [send(by_t.at[there], b_zgot.at[r], (dp, there)) for r, there in enumerate(others)]
    state = {}

    def small_x():
        c_core.wait_recv()
        s_keep[...] += s_core[...]
        s_x[pl.ds(0, part), :] = s_keep[pl.ds(part, part), :]
        s_x[pl.ds(part, part), :] = s_keep[pl.ds(3 * part, part), :]
        state["sx"] = send(s_x, s_xgot, (xn, me))

    def small_y():
        state["sx"].wait_recv()
        s_y[...] = s_keep[pl.ds(2 * part, part), :] + s_xgot[pl.ds(part, part), :]
        state["sy"] = send(s_y, s_ygot, (yn, me))

    def small_z():
        state["sy"].wait_recv()
        s_z[...] = s_keep[pl.ds(0, part), :] + s_xgot[pl.ds(0, part), :] + s_ygot[...]
        state["sz"] = [send(s_z, s_zgot.at[r], (dp, there)) for r, there in enumerate(others)]

    def small_end():
        total = s_z[...]
        for r, copy in enumerate(state["sz"]):
            copy.wait_recv()
            total = total + s_zgot[r]
        small_out[...] = total

    def by_t_first():
        total = by_t[me]
        for r, copy in enumerate(b_first):
            copy.wait_recv()
            total = total + b_zgot[r]
        b_acc[0] = total
        state["b"] = send(b_acc.at[0], b_got.at[0], (core, me))

    def by_t_hop(at):
        state["b"].wait_recv()
        total = b_acc[at] + b_got[at]
        if at == 2:
            by_t_out[...] = total
            return
        b_acc[at + 1] = total
        state["b"] = send(b_acc.at[at + 1], b_got.at[at + 1], ((xn, yn)[at], me))

    tiny_peers = [(core, me), (xn, me), (yn, me)]
    bit = 1
    while bit < n_t:
        tiny_peers.append((dp, flip(me, bit)))
        bit *= 2

    def tiny_hop(at):
        if at:
            state["t"].wait_recv()
            total = t_acc[at - 1] + t_got[at - 1]
            if at == len(tiny_peers):
                tiny_out[...] = total
                return
            t_acc[at] = total
        state["t"] = send(t_acc.at[at], t_got.at[at], tiny_peers[at])

    def product(i):
        slot = i % 2
        for copy in waiting[i]:
            copy.wait()
        if i + 1 < n_t:
            waiting[i + 1] = loads(i + 1)
        ext[pl.ds(0, rows), :] = pre_ring[slot]
        ext[pl.ds(rows, 8), :] = halo[:, pl.ds(pl.multiple_of(slabs[i] * columns, 128), columns)]
        d_ps = conv_back(ext, chan[slabs[i]], masks, rows).astype(bf16)
        if i >= 2:
            state["p", i - 2].wait_send()
        value = dot(nt[pl.ds(half, half), :], d_ps)
        exponent = column_exponent(value)
        put_codes(p_send.at[slot], 0, value, exponent)
        put_exponent(p_send.at[slot], exponent)
        state["p", i] = send(p_send.at[slot], p_got.at[i], (core, me))
        value = dot(nt[pl.ds(0, half), :], d_ps)
        exponent = column_exponent(value)
        put_codes(p_keep.at[slot], 0, value, exponent)
        put_exponent(p_keep.at[slot], exponent)
        if i == 0:
            dh_copy.wait()
        acc[...] += dot(d_ps, w_ring[slot], NT)

    def first(i):
        state["p", i].wait_recv()
        core_sum_kernel(p_keep.at[i % 2], p_got.at[i], x_pay.at[i], y_pay.at[i], keep1.at[i])
        state["x", i] = send(x_pay.at[i], x_got.at[i], (xn, me))
        state["y", i] = send(y_pay.at[i], y_got.at[i], (yn, me))

    def second(i):
        state["x", i].wait_recv()
        state["y", i].wait_recv()
        cross_sum_kernel(
            keep1.at[i], x_got.at[i], y_got.at[i], y_pay2.at[i], x_pay2.at[i], keep2.at[i], exp2_ref.at[i]
        )
        state["y2", i] = send(y_pay2.at[i], y_got2.at[i], (yn, me))
        state["x2", i] = send(x_pay2.at[i], x_got2.at[i], (xn, me))

    def third(i):
        state["y2", i].wait_recv()
        state["x2", i].wait_recv()
        own_half = keep2.shape[1] // 2
        y_there, x_there = exponent_in(y_got2.at[i]), exponent_in(x_got2.at[i])
        own_a = keep2[i, 0:own_half, :] + codes_in(y_got2.at[i], 0, own_half, y_there)
        own_b = keep2[i, own_half : 2 * own_half, :] + codes_in(x_got2.at[i], 0, own_half, x_there)
        if order[i] == 0:
            g_out[0:own_half, :] = own_a
            g_out[own_half : 2 * own_half, :] = own_b
            return
        exponent = jnp.maximum(jnp.maximum(y_there, x_there), exp2_ref[i, 0:1, :]) + 1.0
        ref = z_pay.at[i]
        put_codes(ref, 0, own_a, exponent)
        put_codes(ref, own_half, own_b, exponent)
        put_exponent(ref, exponent)
        state["z", i] = send(ref, z_got.at[i], (dp, slabs[i]))

    product(0)
    small_x()
    by_t_first()
    product(1)
    first(0)
    small_y()
    by_t_hop(0)
    product(2)
    first(1)
    second(0)
    small_z()
    by_t_hop(1)
    for i in range(3, n_t):
        product(i)
        first(i - 1)
        second(i - 2)
        third(i - 3)
    d_normed = acc[...] + dot(d_small, w_small[...], NT)
    x_v = x[...].astype(f32)
    scaled = gain[0:1, :] * d_normed
    r = rstd[...]
    inner = jnp.sum(x_v * scaled, axis=1, keepdims=True) * (1.0 / x_v.shape[1])
    token_out[...] = (back[...].astype(f32) + r * scaled - x_v * (r * r * r) * inner).astype(bf16)
    d_gain = jnp.sum(x_v * r * d_normed, axis=0, keepdims=True)
    t_acc[0, 0:8, :] = jnp.concatenate([d_gain, jnp.zeros((7, d_gain.shape[1]), f32)], axis=0)
    t_acc[0, 8:16, :] = jnp.concatenate(
        [conv_rows_in[...], jnp.zeros((8, d_gain.shape[1] - conv_rows_in.shape[1]), f32)], axis=1
    )
    last = n_t - 1
    first(last)
    tiny_hop(0)
    second(last - 1)
    third(last - 2)
    tiny_hop(1)
    by_t_hop(2)
    second(last)
    tiny_hop(2)
    third(last - 1)
    tiny_hop(3)
    small_end()
    third(last)
    for at in range(4, len(tiny_peers) + 1):
        tiny_hop(at)
    for i in range(n_t - 1):
        state["z", i].wait_recv()
        ref = z_got.at[i]
        g_out[...] += codes_in(ref, 0, g_out.shape[0], exponent_in(ref))
    waited = [state["p", i] for i in range(n_t - 2)]
    for copy in started:
        if not any(copy is other for other in waited):
            copy.wait_send()


def tail_scratch(n_t, rows, width, columns, wide):
    i16 = jnp.int16
    half = width // 2
    part = half // 4
    hops = 3 + (n_t.bit_length() - 1)
    return [
        pltpu.VMEM((2, rows, columns), f32),
        pltpu.VMEM((2, width, columns), bf16),
        pltpu.VMEM((rows, width), f32),
        pltpu.VMEM((rows + 8, columns), f32),
        pltpu.VMEM((rows + 8, 2 * STATE), f32),
        pltpu.SemaphoreType.DMA((2, n_t)),
        pltpu.SemaphoreType.DMA,
        pltpu.VMEM((2, half + EXTRA, columns), i16),
        pltpu.VMEM((2, half + EXTRA, columns), i16),
        pltpu.VMEM((n_t, half + EXTRA, columns), i16),
        *[pltpu.VMEM((n_t, part + EXTRA, columns), i16) for _ in range(4)],
        pltpu.VMEM((n_t, 2 * part + EXTRA, columns), i16),
        *[pltpu.VMEM((n_t, part // 2 + EXTRA, columns), i16) for _ in range(4)],
        pltpu.VMEM((n_t, part, columns), f32),
        pltpu.VMEM((n_t, 8, columns), f32),
        pltpu.VMEM((n_t - 1, part + EXTRA, columns), i16),
        pltpu.VMEM((n_t - 1, part + EXTRA, columns), i16),
        pltpu.VMEM((half, wide), f32),
        pltpu.VMEM((half, wide), f32),
        pltpu.VMEM((half, wide), f32),
        pltpu.VMEM((2 * part, wide), f32),
        pltpu.VMEM((2 * part, wide), f32),
        pltpu.VMEM((part, wide), f32),
        pltpu.VMEM((part, wide), f32),
        pltpu.VMEM((part, wide), f32),
        pltpu.VMEM((n_t - 1, part, wide), f32),
        pltpu.VMEM((hops, 16, width), f32),
        pltpu.VMEM((hops, 16, width), f32),
        pltpu.VMEM((3, 8, columns), f32),
        pltpu.VMEM((n_t - 1, 8, columns), f32),
        pltpu.VMEM((3, 8, columns), f32),
        pltpu.SemaphoreType.DMA((6 * n_t + 8 * n_t,)),
        pltpu.SemaphoreType.DMA((6 * n_t + 8 * n_t,)),
    ]


def kernel_call(kernel, grid, ins, outs, scratch=(), scalar=None, flops=0, bytes_=0, ident=None):
    def spec(shape, block, index):
        if block is pl.ANY:
            return pl.BlockSpec(memory_space=pl.ANY)
        if block is None:
            rank = len(shape)
            return pl.BlockSpec(shape, lambda i, *_, rank=rank: (0,) * rank)
        return pl.BlockSpec(block, index)

    return pl.pallas_call(
        kernel,
        grid_spec=pltpu.PrefetchScalarGridSpec(
            num_scalar_prefetch=0 if scalar is None else 1,
            grid=(grid,),
            in_specs=[spec(a.shape, b, m) for a, b, m in ins],
            out_specs=[spec(s, b, m) for s, _, b, m in outs],
            scratch_shapes=list(scratch),
        ),
        out_shape=[jax.ShapeDtypeStruct(s, d) for s, d, _, _ in outs],
        compiler_params=pltpu.CompilerParams(
            dimension_semantics=("arbitrary",),
            vmem_limit_bytes=60 * 1024 * 1024,
            **({} if ident is None else {"collective_id": ident, "has_side_effects": True}),
        ),
        cost_estimate=pl.CostEstimate(flops=flops, bytes_accessed=bytes_, transcendentals=0),
    )(*([] if scalar is None else [scalar]), *[a for a, _, _ in ins])


MESH = pl.DeviceIdType.MESH


def flip(index, bit):
    return index + bit - 2 * bit * ((index // bit) % 2)


def flip_all(index, mask):
    bit = 1
    while bit <= mask:
        if mask & bit:
            index = flip(index, bit)
        bit *= 2
    return index


def gather_kernel(n_t, kinds, *refs):
    count = len(kinds)
    shards, outs = refs[:count], refs[count : 2 * count]
    local_sem, send_sem, recv_sem = refs[2 * count :]
    dp, me = lax.axis_index("dp"), lax.axis_index("tensor")
    core, xn, yn = flip(dp, 1), flip(dp, 2), flip(dp, 4)
    diagonal = flip(xn, 4)
    others = [flip_all(me, r) for r in range(1, n_t)]
    barrier = pltpu.get_barrier_semaphore()
    for there in (core, xn, yn):
        pl.semaphore_signal(barrier, inc=1, device_id=(there, me), device_id_type=MESH)
    for there in others:
        pl.semaphore_signal(barrier, inc=1, device_id=(dp, there), device_id_type=MESH)
    pl.semaphore_wait(barrier, 3 + len(others))
    used = [0]
    started = []

    def send(src, dst, device):
        at = used[0]
        used[0] += 1
        copy = pltpu.make_async_remote_copy(
            src_ref=src, dst_ref=dst, send_sem=send_sem.at[at], recv_sem=recv_sem.at[at],
            device_id=device, device_id_type=MESH,
        )
        copy.start()
        started.append(copy)
        return copy

    def place(k, there, slab, part=None):
        rows = shards[k].shape[0]
        if kinds[k] == "line":
            return outs[k].at[slab]
        if kinds[k] == "flat":
            if slab is not None:
                return outs[k].at[there, pl.ds(pl.multiple_of(slab * rows, 8), rows)]
            if part is None:
                return outs[k].at[there]
            return outs[k].at[there, pl.ds(part * (n_t * rows // 2), n_t * rows // 2)]
        start, size = there * rows, rows
        if part is not None:
            start, size = start + part * (rows // 2), rows // 2
        return outs[k].at[slab, pl.ds(pl.multiple_of(start, 16), size)]

    own, far = [], []
    for k in range(count):
        keep = pltpu.make_async_copy(shards[k], place(k, dp, me), local_sem.at[k])
        keep.start()
        own.append(keep)
    units = []
    for k in range(count):
        far.append([None] + [send(shards[k], place(k, dp, me), (dp, there)) for there in others])
        if kinds[k] == "flat":
            units.append((k, None))
        elif kinds[k] == "slab":
            units += [(k, r) for r in range(n_t)]

    state = {}

    def slab_of(unit):
        return None if unit[1] is None else flip_all(me, unit[1])

    def first(unit):
        k, r = unit
        slab = slab_of(unit)
        if r is None:
            own[k].wait()
            for copy in far[k][1:]:
                copy.wait_recv()
        elif r:
            far[k][r].wait_recv()
        src = shards[k] if r == 0 else place(k, dp, slab)
        state[unit] = [send(src, place(k, dp, slab), (there, me)) for there in (xn, yn, core)]

    def second(unit):
        k, r = unit
        slab = slab_of(unit)
        x, y, _ = state[unit]
        x.wait_recv()
        state[unit].append(send(place(k, xn, slab, 0), place(k, xn, slab, 0), (yn, me)))
        state[unit].append(send(place(k, xn, slab), place(k, xn, slab), (core, me)))
        y.wait_recv()
        state[unit].append(send(place(k, yn, slab, 1), place(k, yn, slab, 1), (xn, me)))
        state[unit].append(send(place(k, yn, slab), place(k, yn, slab), (core, me)))

    def third(unit):
        k, r = unit
        slab = slab_of(unit)
        state[unit][3].wait_recv()
        state[unit][5].wait_recv()
        state[unit].append(send(place(k, diagonal, slab), place(k, diagonal, slab), (core, me)))

    def fourth(unit):
        for at in (2, 4, 6, 7):
            state[unit][at].wait_recv()

    last = len(units)
    for step in range(last + 3):
        if step < last:
            first(units[step])
        if 0 <= step - 1 < last:
            second(units[step - 1])
        if 0 <= step - 2 < last:
            third(units[step - 2])
        if 0 <= step - 3 < last:
            fourth(units[step - 3])
    for k in range(count):
        if kinds[k] == "line":
            for copy in far[k][1:]:
                copy.wait_recv()
        if kinds[k] != "flat":
            own[k].wait()
    for copy in started:
        copy.wait_send()


def gather_all(shards, kinds, n_dp, n_t, ident):
    count = len(shards)
    copies = count * (n_t - 1) + 8 * sum({"line": 0, "flat": 1, "slab": n_t}[kind] for kind in kinds)

    def shape(a, kind):
        rows, columns = a.shape
        lead = {"line": (n_t, rows), "flat": (n_dp, n_t * rows), "slab": (n_t, n_dp * rows)}[kind]
        return jax.ShapeDtypeStruct((*lead, columns), a.dtype)

    return pl.pallas_call(
        functools.partial(gather_kernel, n_t, kinds),
        out_shape=[shape(a, kind) for a, kind in zip(shards, kinds)],
        in_specs=[pl.BlockSpec(memory_space=pl.ANY)] * count,
        out_specs=[pl.BlockSpec(memory_space=pl.ANY)] * count,
        scratch_shapes=[
            pltpu.SemaphoreType.DMA((count,)),
            pltpu.SemaphoreType.DMA((copies,)),
            pltpu.SemaphoreType.DMA((copies,)),
        ],
        compiler_params=pltpu.CompilerParams(collective_id=ident, has_side_effects=True),
    )(*shards)


def adam_update(weight, grad, first, second, rate, decay):
    first_new = beta_first * first + (1.0 - beta_first) * grad
    second_new = beta_second * second + (1.0 - beta_second) * grad * grad
    first_hat = first_new / (1.0 - beta_first**STEP)
    second_hat = second_new / (1.0 - beta_second**STEP)
    weight_new = weight * (1.0 - rate * decay) - rate * first_hat / (
        jnp.sqrt(second_hat) + adam_epsilon
    )
    return (weight_new, first_new, second_new)


def xor_pairs(size, mask):
    return [(i, i ^ mask) for i in range(size)]


def tied(value, *others):
    return lax.optimization_barrier((value, *others))[0]


class PairSum:
    def __init__(self, keep, send):
        self.count, rows, self.columns = keep.shape
        self.rows = (rows - EXTRA) // 4
        self.keep = keep
        self.got = lax.ppermute(send, "dp", xor_pairs(8, 1))

    def call(self, kernel, ins, outs):
        def each(rows):
            return (None, rows, self.columns), lambda i: (i, 0, 0)

        return kernel_call(
            kernel,
            self.count,
            [(a, *each(a.shape[1])) for a in ins],
            [
                ((self.count, rows, self.columns), dtype, *each(rows))
                if lead is None
                else ((rows, self.columns), dtype, None, None)
                for rows, dtype, lead in outs
            ],
        )

    def over_xy(self):
        i16, rows = jnp.int16, self.rows
        outs = [(rows + EXTRA, i16, None), (rows + EXTRA, i16, None), (2 * rows + EXTRA, i16, None)]
        x, y, self.keep = self.call(core_sum_kernel, [self.keep, self.got], outs)
        self.x = lax.ppermute(x, "dp", xor_pairs(8, 2))
        self.y = lax.ppermute(y, "dp", xor_pairs(8, 4))
        return x, y

    def over_yx(self):
        i16, rows = jnp.int16, self.rows
        outs = [(rows // 2 + EXTRA, i16, None), (rows // 2 + EXTRA, i16, None), (rows, f32, None), (8, f32, None)]
        y, x, self.keep, self.exponent = self.call(cross_sum_kernel, [self.keep, self.x, self.y], outs)
        self.y = lax.ppermute(y, "dp", xor_pairs(8, 4))
        self.x = lax.ppermute(x, "dp", xor_pairs(8, 2))
        return x, y

    def over_z(self):
        rows = self.rows
        self.own, z = self.call(
            plane_sum_kernel,
            [self.keep, self.exponent, self.y, self.x],
            [(rows, f32, 0), (rows + EXTRA, jnp.int16, None)],
        )
        self.far = [lax.ppermute(z[r], "tensor", xor_pairs(self.count, r)) for r in range(1, self.count)]
        return self.own, z

    def result(self):
        own = self.own
        for got in self.far:
            scale = jnp.exp2(got[self.rows : self.rows + 1].astype(f32)) / FULL
            own = own + got[: self.rows].astype(f32) * scale
        return own


def gather_plain(shard, kind):
    if kind == "flat":
        return lax.all_gather(lax.all_gather(shard, "tensor", axis=0, tiled=True), "dp", axis=0)
    lines = lax.all_gather(shard, "tensor", axis=0)
    return lines if kind == "line" else lax.all_gather(lines, "dp", axis=1, tiled=True)


def scatter_plain(part):
    own = lax.psum_scatter(part, "dp", scatter_dimension=1, tiled=True)
    return lax.psum_scatter(own, "tensor", scatter_dimension=0, tiled=True)[0]


def body(
    tokens,
    cotangent,
    lengths,
    in_weight,
    in_first,
    in_second,
    dt_weight,
    dt_first,
    dt_second,
    bc_weight,
    bc_first,
    bc_second,
    out_weight,
    out_first,
    out_second,
    norm_gain,
    gain_first,
    gain_second,
    bc_conv,
    conv_first,
    conv_second,
    x_channel,
    channel_first,
    channel_second,
    head_params,
    head_first,
    head_second,
):
    n_dp, n_t = lax.axis_size("dp"), lax.axis_size("tensor")
    me = lax.axis_index("tensor")
    rows, width = tokens.shape
    local = x_channel.shape[1]
    inner = local * n_t
    local_heads = head_params.shape[1]
    all_heads = local_heads * n_t
    cb = local
    per, blocks, hb = 1, n_t, local_heads
    narrow = 512
    steps_in, hn = inner // narrow, narrow // PWIDTH
    own = me * rows
    up = [(i, i + 1) for i in range(n_t - 1)]
    down = [(i + 1, i) for i in range(n_t - 1)]

    paired = n_dp == 8 and n_t & (n_t - 1) == 0
    dp_me = lax.axis_index("dp")
    per_bc, per_conv = bc_weight.shape[0], bc_conv.shape[1]
    line = jnp.concatenate(
        [
            x_channel,
            jnp.repeat(head_params[2], PWIDTH)[None],
            jnp.pad(head_params[:2].reshape(1, -1), ((0, 0), (0, local - 2 * local_heads))),
        ],
        axis=0,
    )
    tiny = jnp.concatenate([norm_gain, bc_conv.reshape(-1)])
    tiny = jnp.pad(tiny[None], ((0, 7), (0, 128 - tiny.size)))
    shards = [
        (line, "line"),
        (tiny, "flat"),
        (bc_weight.astype(bf16), "flat"),
        (dt_weight.astype(bf16), "slab"),
        (in_weight[:, 1].astype(bf16), "slab"),
        (in_weight[:, 0].astype(bf16), "slab"),
        (out_weight.T.astype(bf16), "slab"),
    ]
    if paired:
        got = gather_all([a for a, _ in shards], [kind for _, kind in shards], n_dp, n_t, 0)
    else:
        got = [gather_plain(a, kind) for a, kind in shards]
    chan, tiny, bc_low, dt_low, w_s, w_z, w_o = got
    bc_low = bc_low.reshape(width, -1)
    dt_low = dt_low.swapaxes(0, 1).reshape(width, all_heads)
    tiny = tiny.reshape(n_dp * n_t, 8, 128)[:, 0]
    gain = tiny[:, :per_bc].reshape(width)
    conv_full = tiny[:, per_bc : per_bc + (KW + 1) * per_conv].reshape(-1, KW + 1, per_conv)
    conv_full = conv_full.swapaxes(0, 1).reshape(KW + 1, -1)
    heads = chan[:, 7, : 2 * local_heads].reshape(n_t, 2, local_heads).swapaxes(0, 1).reshape(2, all_heads)

    ends_of = jnp.cumsum(lengths[0])

    def labels_at(places):
        found = jnp.sum((places[:, None] >= ends_of[None, :]).astype(jnp.int32), axis=1)
        return jnp.where(places < 0, -1, found)

    span = labels_at(own + jnp.arange(-HALO, rows + 8, dtype=jnp.int32))
    labels = span[HALO : HALO + rows]
    valid = (own + jnp.arange(rows, dtype=jnp.int32) < ends_of[-1]).astype(f32)[:, None]
    masks = jnp.stack(
        [(span[HALO - o : HALO - o + rows + 8] == span[HALO:]).astype(f32) for o in (1, 2, 3)], axis=1
    )
    before, last = span[HALO - 1], labels[rows - 1]
    keep = (labels == before).astype(f32)[:, None]
    tail = (labels == last).astype(f32)[:, None]
    through = (last == before).astype(f32)
    marks = jnp.concatenate(
        [masks[:rows], labels.astype(f32)[:, None], keep, tail, jnp.full((rows, 1), through), jnp.zeros((rows, 1), f32)],
        axis=1,
    )
    line_label = jnp.broadcast_to(labels.astype(f32)[None], (8, rows))

    prior = lax.ppermute(tokens[-HALO:], "tensor", up)
    x_ext = jnp.concatenate([prior, tokens], axis=0).astype(f32)
    rstd_ext = lax.rsqrt(jnp.mean(x_ext * x_ext, axis=1, keepdims=True) + epsilon)
    normed_ext = (x_ext * rstd_ext * gain[None, :]).astype(bf16)
    x, rstd_in, normed = x_ext[HALO:], rstd_ext[HALO:], normed_ext[HALO:]
    back = cotangent.astype(f32)
    masked = (back * valid).astype(bf16)
    if paired:
        order = dp_me ^ jnp.array([0, 2, 4, 6, 1, 3, 5, 7], jnp.int32)
        turn = me[None].astype(jnp.int32)
        dw_shapes = [((n_t, width // 2 + EXTRA, local), jnp.int16)] * 2
    else:
        order = jnp.arange(n_dp, dtype=jnp.int32)
        turn = jnp.zeros((1,), jnp.int32)
        dw_shapes = [((n_t, width, local), f32)]

    def turned(a):
        return a.T.reshape(n_dp, -1, rows)[order].reshape(width, rows)

    normed_t, masked_t = turned(normed), turned(masked)

    heads_pad = jnp.pad(heads, ((0, 6), (0, 0)))
    bcp, bc_pre, step_raw, step, in_mat, read_mat, in_t, read_t, cols, cols_n, lines, scores, through_all = kernel_call(
        small_kernel,
        1,
        [
            (a, None, None)
            for a in (
                normed_ext,
                bc_low,
                dt_low,
                jnp.pad(conv_full, ((0, 3), (0, 0))),
                marks,
                line_label,
                heads_pad,
            )
        ],
        [
            (s, f32, None, None)
            for s in (
                (rows + HALO, 2 * STATE),
                (rows, 2 * STATE),
                (rows, all_heads),
                (rows, all_heads),
                (rows, STATE),
                (rows, STATE),
                (STATE, rows),
                (STATE, rows),
                (n_t, rows, 4 * hb),
                (steps_in, rows, 4 * hn),
                (all_heads, rows),
                (rows, rows),
                (8, all_heads),
            )
        ],
    )
    decay_all = through_all[0]

    def slab(i, *_):
        return (i // per, 0, i % per)

    wspec = (None, width, cb), slab
    cspec = (None, 8, cb), slab
    colspec = (None, rows, 4 * hb), lambda i, *_: (i, 0, 0)
    colnspec = (None, rows, 4 * hn), lambda i, *_: (i, 0, 0)
    linespec = (hn, rows), lambda i, *_: (i, 0)
    chnspec = (rows, narrow), lambda i, *_: (0, i)
    chspec = (rows, cb), lambda i, *_: (0, i)
    stspec = (STATE, cb), lambda i, *_: (0, i)
    st_shape = (STATE, inner)
    decay_row = jnp.broadcast_to(jnp.repeat(decay_all, PWIDTH)[None], (8, inner))
    def dw_at(i, m):
        return (m[0] ^ (i // per), 0, i % per)

    dw_specs = [(s, d, (None, s[1], cb), dw_at) for s, d in dw_shapes]
    full = (None, None)
    big = 2 * rows * width * inner

    ps, xc, added = kernel_call(
        functools.partial(stream_kernel, hb),
        blocks,
        [(normed_ext, *full), (w_s, *wspec), (chan, *cspec), (marks, *full), (cols, *colspec), (in_t, *full)],
        [
            ((rows + HALO, inner), f32, (rows + HALO, cb), lambda i, *_: (0, i)),
            ((rows, inner), f32, *chspec),
            (st_shape, f32, *stspec),
        ],
        flops=big,
        bytes_=4 * width * inner,
    )

    inside, state = kernel_call(
        functools.partial(inside_kernel, hn, n_t),
        steps_in,
        [
            (xc, *chnspec),
            (cols_n, *colnspec),
            (lines, *linespec),
            (scores, *full),
            (added, *full),
            (decay_row, *full),
        ],
        [((rows, inner), f32, *chnspec), (st_shape, f32, *full)],
        scratch=carry_scratch(steps_in, narrow),
        ident=1,
        flops=4 * big,
        bytes_=8 * width * inner,
    )
    z, y, squares = kernel_call(
        functools.partial(carry_kernel, hb),
        blocks,
        [
            (normed_ext, *full),
            (w_z, *wspec),
            (inside, *chspec),
            (xc, *chspec),
            (cols, *colspec),
            (read_mat, *full),
            (state, *stspec),
            (chan, *cspec),
        ],
        [
            ((rows, inner), f32, *chspec),
            ((rows, inner), f32, *chspec),
            ((rows, 128), f32, *full),
        ],
        flops=2 * big,
        bytes_=8 * width * inner,
    )
    rstd = lax.rsqrt(jnp.sum(squares, axis=1, keepdims=True) / inner + epsilon)

    mixed, d_gated, d_gain_gate, totals, *dw_o = kernel_call(
        out_kernel,
        blocks,
        [
            (z, *chspec),
            (y, *chspec),
            (xc, *chspec),
            (chan, *cspec),
            (rstd, *full),
            (w_o, *wspec),
            (masked, *full),
            (masked_t, *full),
            (tokens, *full),
            (valid, *full),
        ],
        [
            ((rows, width), bf16, *full),
            ((rows, inner), f32, *chspec),
            ((1, inner), f32, (1, cb), lambda i, *_: (0, i)),
            ((rows, 128), f32, *full),
            *dw_specs,
        ],
        scratch=[pltpu.VMEM((rows, width), f32)],
        scalar=turn,
        flops=3 * big,
        bytes_=8 * width * inner,
    )
    sum_o = PairSum(*dw_o) if paired else None
    total = jnp.sum(totals, axis=1, keepdims=True)

    dy, dh, back_added, skip_rows, *dw_z = kernel_call(
        functools.partial(gate_kernel, hb, inner),
        blocks,
        [
            (z, *chspec),
            (y, *chspec),
            (xc, *chspec),
            (chan, *cspec),
            (rstd, *full),
            (total, *full),
            (d_gated, *chspec),
            (w_z, *wspec),
            (normed_t, *full),
            (cols, *colspec),
            (read_t, *full),
        ],
        [
            ((rows, inner), f32, *chspec),
            ((rows, width), f32, *full),
            (st_shape, f32, *stspec),
            ((1, inner), f32, (1, cb), lambda i, *_: (0, i)),
            *dw_specs,
        ],
        scalar=turn,
        flops=2 * big,
        bytes_=8 * width * inner,
    )
    if paired:
        sum_z = PairSum(*dw_z)
        dy = tied(dy, *sum_o.over_xy())

    d_inside, sums, d_in_part, d_read_part, back_state = kernel_call(
        functools.partial(inside_back_kernel, hn, n_t),
        steps_in,
        [
            (dy, *chnspec),
            (xc, *chnspec),
            (y, *chnspec),
            (cols_n, *colnspec),
            (lines, *linespec),
            (scores, *full),
            (marks, *full),
            (line_label, *full),
            (in_mat, *full),
            (read_mat, *full),
            (back_added, *full),
            (decay_row, *full),
        ],
        [
            ((rows, inner), f32, *chnspec),
            ((steps_in, rows, hn), f32, (None, rows, hn), lambda i, *_: (i, 0, 0)),
            ((rows, STATE), f32, *full),
            ((rows, STATE), f32, *full),
            (st_shape, f32, *full),
        ],
        scratch=[pltpu.VMEM((rows, rows), f32), *carry_scratch(steps_in, narrow)],
        ident=2,
        flops=8 * big,
        bytes_=8 * width * inner,
    )
    if paired:
        d_inside = tied(d_inside, *sum_o.over_yx(), *sum_z.over_xy())
    d_pre, more_sums, tap_rows, d_in_mat, d_read_mat = kernel_call(
        functools.partial(carry_back_kernel, hb),
        blocks,
        [
            (dy, *chspec),
            (xc, *chspec),
            (ps, (rows + HALO, cb), lambda i, *_: (0, i)),
            (d_inside, *chspec),
            (cols, *colspec),
            (in_mat, *full),
            (back_state, *stspec),
            (state, *stspec),
            (chan, *cspec),
            (marks, *full),
            (d_in_part, *full),
            (d_read_part, *full),
        ],
        [
            ((rows, inner), f32, *chspec),
            ((blocks, rows, 2 * hb), f32, (None, rows, 2 * hb), lambda i, *_: (i, 0, 0)),
            ((8, inner), f32, (8, cb), lambda i, *_: (0, i)),
            ((rows, STATE), f32, *full),
            ((rows, STATE), f32, *full),
        ],
        flops=2 * big,
        bytes_=8 * width * inner,
    )
    halo = lax.ppermute(d_pre[:8], "tensor", down)
    conv_pad = jnp.pad(conv_full, ((0, 3), (0, 0)))
    d_bc_pre, d_dt, d_heads, d_conv = kernel_call(
        post_kernel,
        1,
        [
            (a, None, None)
            for a in (
                sums,
                more_sums,
                step_raw,
                step,
                heads_pad,
                through_all,
                tap_rows,
                d_in_mat,
                d_read_mat,
                bc_pre,
                bcp,
                marks,
            )
        ],
        [
            ((rows, 2 * STATE), f32, None, None),
            ((rows, all_heads), bf16, None, None),
            ((8, all_heads), f32, None, None),
            ((8, 2 * STATE), f32, None, None),
        ],
    )
    bc_halo = lax.ppermute(d_bc_pre[:8], "tensor", down)
    head_row = jnp.pad(d_heads[:2, :, None], ((0, 0), (0, 0), (0, PWIDTH - 1)))
    head_row = head_row[0] + jnp.roll(head_row[1], 1, axis=1)
    by_t = jnp.concatenate([tap_rows[: KW + 1], d_gain_gate, skip_rows, head_row.reshape(1, inner)], axis=0)
    by_t = by_t.reshape(8, n_t, local).swapaxes(0, 1)
    wide = (2 * STATE + all_heads + 127) // 128 * 128
    per_dp = width // n_dp
    if paired:
        halo = tied(halo, *sum_o.over_z(), *sum_z.over_yx())
        w_small = jnp.pad(jnp.concatenate([bc_low, dt_low], axis=1), ((0, 0), (0, wide - 2 * STATE - all_heads)))
        g_s, token_grad, g_small, by_t, tiny = kernel_call(
            functools.partial(tail_kernel, n_t),
            1,
            [
                (d_pre, pl.ANY, None),
                (w_s, pl.ANY, None),
                (dh, pl.ANY, None),
                *[
                    (a, None, None)
                    for a in (
                        halo,
                        chan,
                        masks,
                        normed_t,
                        d_bc_pre,
                        bc_halo,
                        conv_pad,
                        d_dt,
                        w_small,
                        by_t,
                        d_conv,
                        tokens,
                        cotangent,
                        rstd_in,
                        jnp.broadcast_to(gain[None], (8, width)),
                    )
                ],
            ],
            [
                ((per_dp, local), f32, None, None),
                ((rows, width), bf16, None, None),
                ((per_dp, wide), f32, None, None),
                ((8, local), f32, None, None),
                ((16, width), f32, None, None),
            ],
            scratch=tail_scratch(n_t, rows, width, local, wide),
            ident=3,
        )
        sum_z.over_z()
        g_o, g_z = sum_o.result(), sum_z.result()
        g_small = g_small[:, : 2 * STATE + all_heads]
        d_gain, d_conv = tiny[0], tiny[8 : 8 + KW + 1, : 2 * STATE]
    else:
        dh, *dw_s = kernel_call(
            stream_back_kernel,
            blocks,
            [
                (d_pre, *chspec),
                (halo, (8, cb), lambda i, *_: (0, i)),
                (chan, *cspec),
                (masks, *full),
                (w_s, *wspec),
                (normed_t, *full),
                (dh, *full),
            ],
            [
                ((rows, width), f32, *full),
                *dw_specs,
            ],
            scratch=[pltpu.VMEM((rows + 8, cb), f32)],
            scalar=turn,
        )
        bc_ext = jnp.concatenate([d_bc_pre, bc_halo], axis=0)
        d_bc = conv_full[KW - 1][None, :] * d_bc_pre
        for o in range(1, KW):
            d_bc = d_bc + conv_full[KW - 1 - o][None, :] * (masks[o : o + rows, o - 1 : o] * bc_ext[o : o + rows])
        d_bc = d_bc.astype(bf16)
        d_normed = dh + dot(d_bc, bc_low, NT) + dot(d_dt, dt_low, NT)
        scaled = gain[None, :] * d_normed
        token_grad = (
            back + rstd_in * scaled - x * rstd_in**3 * jnp.sum(x * scaled, axis=1, keepdims=True) / width
        ).astype(bf16)
        d_gain = lax.psum(jnp.sum(x * rstd_in * d_normed, axis=0), ("dp", "tensor"))
        d_conv = lax.psum(d_conv[: KW + 1], ("dp", "tensor"))
        g_small = dot(normed_t, jnp.concatenate([d_bc, d_dt], axis=1)).reshape(n_dp, per_dp, -1)
        g_small = lax.psum(lax.psum_scatter(g_small, "dp", scatter_dimension=0), "tensor")
        by_t = lax.psum(lax.psum_scatter(by_t, "tensor", scatter_dimension=0), "dp")
        g_o, g_z, g_s = scatter_plain(dw_o[0]), scatter_plain(dw_z[0]), scatter_plain(dw_s[0])
    place = dp_me * n_t + me
    g_bc = lax.dynamic_slice(g_small, (me * per_bc, 0), (per_bc, 2 * STATE))
    g_dt = lax.dynamic_slice(g_small, (0, 2 * STATE + me * local_heads), (per_dp, local_heads))
    g_gain = lax.dynamic_slice(d_gain, (place * per_bc,), (per_bc,))
    g_conv = lax.dynamic_slice(d_conv, (0, place * per_conv), (KW + 1, per_conv))
    g_channel = by_t[: KW + 2]
    ends = by_t[7].reshape(local_heads, PWIDTH)
    g_head = jnp.stack([ends[:, 0], ends[:, 1], jnp.sum(by_t[6].reshape(local_heads, PWIDTH), axis=1)])
    g_in = jnp.stack([g_z, g_s], axis=1)
    in_new = adam_update(in_weight, g_in, in_first, in_second, rate_matrix, decay_matrix)
    dt_new = adam_update(dt_weight, g_dt, dt_first, dt_second, rate_matrix, decay_matrix)
    bc_new = adam_update(bc_weight, g_bc, bc_first, bc_second, rate_matrix, decay_matrix)
    out_new = adam_update(out_weight, g_o.T, out_first, out_second, rate_matrix, decay_matrix)
    gain_new = adam_update(norm_gain, g_gain, gain_first, gain_second, rate_small, 0.0)
    conv_new = adam_update(bc_conv, g_conv, conv_first, conv_second, rate_small, 0.0)
    channel_new = adam_update(x_channel, g_channel, channel_first, channel_second, rate_small, 0.0)
    head_new = adam_update(head_params, g_head, head_first, head_second, rate_small, 0.0)
    return (
        mixed,
        token_grad,
        *in_new,
        *dt_new,
        *bc_new,
        *out_new,
        *gain_new,
        *conv_new,
        *channel_new,
        *head_new,
    )


def solution(mesh):
    return jax.shard_map(
        body,
        mesh=mesh,
        in_specs=(
            P(("dp", "tensor"), None),
            P(("dp", "tensor"), None),
            P("dp", None),
            P("dp", None, "tensor"),
            P("dp", None, "tensor"),
            P("dp", None, "tensor"),
            P("dp", "tensor"),
            P("dp", "tensor"),
            P("dp", "tensor"),
            P(("dp", "tensor"), None),
            P(("dp", "tensor"), None),
            P(("dp", "tensor"), None),
            P("tensor", "dp"),
            P("tensor", "dp"),
            P("tensor", "dp"),
            P(("dp", "tensor")),
            P(("dp", "tensor")),
            P(("dp", "tensor")),
            P(None, ("dp", "tensor")),
            P(None, ("dp", "tensor")),
            P(None, ("dp", "tensor")),
            P(None, "tensor"),
            P(None, "tensor"),
            P(None, "tensor"),
            P(None, "tensor"),
            P(None, "tensor"),
            P(None, "tensor"),
        ),
        out_specs=(
            P(("dp", "tensor"), None),
            P(("dp", "tensor"), None),
            P("dp", None, "tensor"),
            P("dp", None, "tensor"),
            P("dp", None, "tensor"),
            P("dp", "tensor"),
            P("dp", "tensor"),
            P("dp", "tensor"),
            P(("dp", "tensor"), None),
            P(("dp", "tensor"), None),
            P(("dp", "tensor"), None),
            P("tensor", "dp"),
            P("tensor", "dp"),
            P("tensor", "dp"),
            P(("dp", "tensor")),
            P(("dp", "tensor")),
            P(("dp", "tensor")),
            P(None, ("dp", "tensor")),
            P(None, ("dp", "tensor")),
            P(None, ("dp", "tensor")),
            P(None, "tensor"),
            P(None, "tensor"),
            P(None, "tensor"),
            P(None, "tensor"),
            P(None, "tensor"),
            P(None, "tensor"),
        ),
        check_vma=False,
    )
```

```python
import functools

import jax
import jax.numpy as jnp
from jax import lax
from jax.experimental import pallas as pl
from jax.experimental.pallas import tpu as pltpu
from jax.sharding import PartitionSpec as P

STATE = 128
KW = 4
STEP = 5
HALO = 16
BLOCK = 256
PWIDTH = 64
LOG2E = 1.4426950408889634

epsilon = 1e-05
adam_epsilon = 1e-08
beta_first = 0.9
beta_second = 0.95
rate_matrix = 0.02
rate_small = 0.2
decay_matrix = 0.1
highest = lax.Precision.HIGHEST

f32 = jnp.float32
bf16 = jnp.bfloat16
NN = (((1,), (0,)), ((), ()))
NT = (((1,), (1,)), ((), ()))
TN = (((0,), (0,)), ((), ()))


def dot(a, b, dims=NN):
    return lax.dot_general(a, b, dims, preferred_element_type=f32)


def halves(a):
    high = a.astype(bf16)
    return high, (a - high.astype(f32)).astype(bf16)


def dot3(a, b, dims=NN):
    ah, al = halves(a)
    bh, bl = halves(b)
    return dot(ah, bh, dims) + (dot(ah, bl, dims) + dot(al, bh, dims))


def sigmoid(v):
    return 1.0 / (1.0 + jnp.exp(-v))


def low_lanes(rows):
    return lax.broadcasted_iota(jnp.int32, (rows, 2 * PWIDTH), 1) < PWIDTH


def dot_exact(ones, a):
    high = a.astype(bf16)
    rest = a - high.astype(f32)
    middle = rest.astype(bf16)
    low = (rest - middle.astype(f32)).astype(bf16)
    return dot(ones, high) + (dot(ones, middle) + dot(ones, low))


EXTRA = 16
FULL = 32000.0


def column_exponent(value):
    most = jnp.max(jnp.abs(value), axis=0, keepdims=True)
    return jnp.floor(jnp.log2(jnp.maximum(most, 1e-30))) + 1.0


def put_codes(ref, start, value, exponent):
    codes = jnp.round(value * (FULL * jnp.exp2(-exponent)))
    ref[start : start + value.shape[0], :] = codes.astype(jnp.int32).astype(jnp.int16)


def put_exponent(ref, exponent):
    rows = ref.shape[0]
    wide = jnp.broadcast_to(exponent, (EXTRA, exponent.shape[1]))
    ref[rows - EXTRA : rows, :] = wide.astype(jnp.int32).astype(jnp.int16)


def exponent_in(ref):
    rows = ref.shape[0]
    return ref[rows - EXTRA : rows, :].astype(jnp.int32).astype(f32)[:1]


def codes_in(ref, start, rows, exponent):
    codes = ref[start : start + rows, :].astype(jnp.int32).astype(f32)
    return codes * (jnp.exp2(exponent) / FULL)


def put_packed(ref, *parts):
    exponent = column_exponent(parts[0])
    for part in parts[1:]:
        exponent = jnp.maximum(exponent, column_exponent(part))
    start = 0
    for part in parts:
        put_codes(ref, start, part, exponent)
        start += part.shape[0]
    put_exponent(ref, exponent)


def core_sum(keep, got, x_out, y_out, keep_out):
    rows = keep.shape[0] // 4
    half = rows // 2
    there = exponent_in(got)

    def total(part, second):
        start = part * rows + second * half
        return keep[start : start + half, :] + codes_in(got, start, half, there)

    put_packed(x_out, total(1, 0), total(3, 0))
    put_packed(y_out, total(2, 1), total(3, 1))
    for at, (part, second) in enumerate(((0, 0), (2, 0), (0, 1), (1, 1))):
        keep_out[at * half : (at + 1) * half, :] = total(part, second)


def cross_sum(keep, x_got, y_got, y_out, x_out, keep_out):
    half = y_out.shape[0] - EXTRA
    x_there, y_there = exponent_in(x_got), exponent_in(y_got)
    put_packed(y_out, keep[half : 2 * half, :] + codes_in(x_got, half, half, x_there))
    put_packed(x_out, keep[3 * half : 4 * half, :] + codes_in(y_got, half, half, y_there))
    keep_out[0:half, :] = keep[0:half, :] + codes_in(x_got, 0, half, x_there)
    keep_out[half : 2 * half, :] = keep[2 * half : 3 * half, :] + codes_in(y_got, 0, half, y_there)


def plane_sum(keep, y_got, x_got):
    half = keep.shape[0] // 2
    own_a = keep[0:half, :] + codes_in(y_got, 0, half, exponent_in(y_got))
    own_b = keep[half : 2 * half, :] + codes_in(x_got, 0, half, exponent_in(x_got))
    return own_a, own_b


def plane_sum_kernel(me, keep, y_got, x_got, own_out, z_out):
    own_a, own_b = plane_sum(keep, y_got, x_got)
    put_packed(z_out, own_a, own_b)

    @pl.when(pl.program_id(0) == 0)
    def _():
        half = own_a.shape[0]
        own_out[0:half, :] = own_a
        own_out[half : 2 * half, :] = own_b


def spread(cols, field, heads):
    rows = cols.shape[0]
    low = low_lanes(rows)
    parts = []
    for pair in range(heads // 2):
        at = field * heads + 2 * pair
        parts.append(jnp.where(low, cols[:, at : at + 1], cols[:, at + 1 : at + 2]))
    return parts[0] if len(parts) == 1 else jnp.concatenate(parts, axis=1)


def shifted(stream_ref, rows, offset):
    return stream_ref[pl.ds(HALO - offset, rows), :]


def conv_of(stream_ref, chan, masks, rows):
    pre = chan[KW : KW + 1, :] + chan[KW - 1 : KW, :] * shifted(stream_ref, rows, 0)
    for offset in range(1, KW):
        tap = chan[KW - 1 - offset : KW - offset, :]
        pre = pre + tap * (masks[:, offset - 1 : offset] * shifted(stream_ref, rows, offset))
    return pre


def tiles_of(rows):
    size = min(BLOCK, rows)
    return size, rows // size


def decay_tile(cols, lines, heads, head, i, j, size):
    gap = cols[i * size : (i + 1) * size, heads + head : heads + head + 1]
    gap = gap - lines[head : head + 1, j * size : (j + 1) * size]
    if i == j:
        gap = jnp.minimum(gap, 0.0)
    return jnp.exp2(gap)


def field_columns(fields, groups):
    size = fields[0].shape[1] // groups
    return [jnp.concatenate([f[:, g * size : (g + 1) * size] for f in fields], axis=1) for g in range(groups)]


def small_kernel(nh, wbc, wdt, conv, marks, line_label, heads, *outs):
    raw = dot(nh[pl.ds(HALO, marks.shape[0]), :], wdt[...])
    small_core(nh, wbc[...], raw, conv[...], marks, line_label, heads[...], *outs)


def small_core(nh, wbc, raw, conv, marks, line_label, heads, bcp_out, pre_out, raw_out, step_out, in_out, read_out,
               in_t_out, read_t_out, wide_out, narrow_out, lines_out, scores_out, through_out):
    rows = step_out.shape[0]
    bcp_out[...] = dot(nh[...], wbc)
    masks = marks[...]
    pre = conv_of(bcp_out, conv, masks, rows)
    pre_out[...] = pre
    bcc = pre * sigmoid(pre)
    in_mat, read_mat = bcc[:, :STATE], bcc[:, STATE:]
    in_out[...] = in_mat
    read_out[...] = read_mat
    in_t_out[...] = in_mat.T
    read_t_out[...] = read_mat.T
    raw = raw + heads[0:1, :]
    raw_out[...] = raw
    step = jnp.maximum(raw, 0.0) + jnp.log1p(jnp.exp(-jnp.abs(raw)))
    step_out[...] = step
    log_decay = step * (-jnp.exp(heads[1:2, :]))
    label, keep, tail, through = masks[:, 3:4], masks[:, 4:5], masks[:, 5:6], masks[0:1, 6:7]
    row_at = lax.broadcasted_iota(jnp.int32, (rows, rows), 0)
    col_at = lax.broadcasted_iota(jnp.int32, (rows, rows), 1)
    lower = row_at >= col_at
    cum = dot_exact(jnp.where(lower, 1.0, 0.0).astype(bf16), log_decay)
    end = cum[rows - 1 : rows, :]
    through_out[...] = jnp.broadcast_to(through * jnp.exp(end), through_out.shape)
    cum2 = cum * LOG2E
    fields = [step, cum2, keep * jnp.exp(cum), tail * jnp.exp(end - cum)]
    for at, group in enumerate(field_columns(fields, wide_out.shape[0])):
        wide_out[at] = group
    for at, group in enumerate(field_columns(fields, narrow_out.shape[0])):
        narrow_out[at] = group
    padded = jnp.concatenate([cum2, jnp.zeros((rows, 128 - cum2.shape[1]), f32)], axis=1)
    lines_out[...] = padded.T[: lines_out.shape[0]]
    same = jnp.logical_and(lower, label == line_label[0:1, :])
    scores_out[...] = jnp.where(same, dot3(read_mat, in_mat, NT), 0.0)


def stream_core(heads, nh, w, chan, masks, col, in_t, ps_out):
    rows = in_t.shape[1]
    ps_out[...] = dot(nh[...], w)
    pre = conv_of(ps_out, chan, masks, rows)
    xc = pre * sigmoid(pre)
    weight = spread(col, 0, heads) * spread(col, 3, heads)
    return xc, dot3(in_t, xc * weight)


def stream_kernel(heads, nh, w, chan, masks, cols, in_t, ps_out, xc_out, add_out):
    xc_out[...], add_out[...] = stream_core(heads, nh, w[...], chan[...], masks[...], cols[...], in_t[...], ps_out)


CARRY_LAG = 3


class Carry:
    def __init__(self, n_t, upward, added, decay, enters, out_codes, in_codes, send_sem, recv_sem, lag=CARRY_LAG):
        self.lag = lag
        self.n_t, self.added, self.decay, self.enters = n_t, added, decay, enters
        self.out_codes, self.in_codes, self.send_sem, self.recv_sem = out_codes, in_codes, send_sem, recv_sem
        me = lax.axis_index("tensor")
        self.dp, self.me = lax.axis_index("dp"), me
        self.at = me if upward else n_t - 1 - me
        self.following = lax.rem(me + (1 if upward else n_t - 1), n_t)
        self.chunks, _, self.size = out_codes.shape
        self.ticks = self.chunks + lag * (n_t - 1)

    def meet(self):
        barrier = pltpu.get_barrier_semaphore()
        for there in (1, self.n_t - 1):
            pl.semaphore_signal(
                barrier, inc=1, device_id=(self.dp, lax.rem(self.me + there, self.n_t)), device_id_type=pl.DeviceIdType.MESH
            )
        pl.semaphore_wait(barrier, 2)

    def copy(self, chunk):
        return pltpu.make_async_remote_copy(
            src_ref=self.out_codes.at[chunk], dst_ref=self.in_codes.at[chunk],
            send_sem=self.send_sem.at[chunk], recv_sem=self.recv_sem.at[chunk],
            device_id=(self.dp, self.following), device_id_type=pl.DeviceIdType.MESH,
        )

    def tick(self, number):
        chunk = number - self.lag * self.at

        @pl.when(jnp.logical_and(chunk >= 0, chunk < self.chunks))
        def _():
            lanes = pl.ds(pl.multiple_of(chunk * self.size, 128), self.size)

            @pl.when(self.at == 0)
            def _():
                self.enters[:, lanes] = jnp.zeros((STATE, self.size), f32)

            @pl.when(self.at > 0)
            def _():
                self.copy(chunk).wait_recv()
                came = self.in_codes.at[chunk]
                self.enters[:, lanes] = codes_in(came, 0, STATE, exponent_in(came))

            @pl.when(self.at < self.n_t - 1)
            def _():
                value = self.added[:, lanes] + self.decay[0:1, lanes] * self.enters[:, lanes]
                exponent = column_exponent(value)
                put_codes(self.out_codes.at[chunk], 0, value, exponent)
                put_exponent(self.out_codes.at[chunk], exponent)
                self.copy(chunk).start()

    def drain(self, done):
        @pl.loop(done, max(done, self.ticks))
        def _(number):
            self.tick(number)

        @pl.when(self.at < self.n_t - 1)
        def _():
            for chunk in range(self.chunks):
                self.copy(chunk).wait_send()


def carry_scratch(chunks, size):
    return [
        pltpu.VMEM((chunks, STATE + EXTRA, size), jnp.int16),
        pltpu.VMEM((chunks, STATE + EXTRA, size), jnp.int16),
        pltpu.SemaphoreType.DMA((chunks,)),
        pltpu.SemaphoreType.DMA((chunks,)),
    ]


def inside_core(heads, xc, col, line, scores, y_out, between=None):
    rows = xc.shape[0]
    size, count = tiles_of(rows)
    scaled = xc * spread(col, 0, heads)
    low = low_lanes(size)
    for pair in range(heads // 2):
        if between is not None and pair == heads // 4:
            between()
        xh, xl = halves(scaled[:, pair * 128 : (pair + 1) * 128])
        both = jnp.concatenate([xh, xl], axis=1)
        for i in range(count):
            outs = []
            for half in range(2):
                acc = jnp.zeros((size, 256), f32)
                for j in range(i + 1):
                    decay = decay_tile(col, line, heads, 2 * pair + half, i, j, size)
                    mix = decay * scores[i * size : (i + 1) * size, j * size : (j + 1) * size]
                    mh, ml = halves(mix)
                    part = both[j * size : (j + 1) * size]
                    acc = acc + dot(mh, part) + dot(ml, part)
                outs.append(acc[:, :128] + acc[:, 128:])
            y_out[i * size : (i + 1) * size, pair * 128 : (pair + 1) * 128] = jnp.where(low, outs[0], outs[1])


def inside_kernel(heads, n_t, xc, cols, lines, scores, added, decay, y_out, enters, *scratch):
    step, steps = pl.program_id(0), pl.num_programs(0)
    carry = Carry(n_t, True, added, decay, enters, *scratch)

    @pl.when(step == 0)
    def _():
        carry.meet()

    carry.tick(2 * step)
    inside_core(heads, xc[...], cols[...], lines[...], scores, y_out, lambda: carry.tick(2 * step + 1))

    @pl.when(step == steps - 1)
    def _():
        carry.drain(2 * carry.chunks)


def carry_kernel(heads, nh, w, inside, xc, cols, read_mat, state, chan, z_out, y_out, sq_out):
    rows = xc.shape[0]
    step = pl.program_id(0)
    z = dot(nh[pl.ds(HALO, rows), :], w[...])
    z_out[...] = z
    y = inside[...] + dot3(read_mat[...], state[...]) * spread(cols[...], 2, heads)
    y_out[...] = y
    g = (y + chan[KW + 2 : KW + 3, :] * xc[...]) * (z * sigmoid(z))
    sq = g * g
    total = sq[:, :128]
    for at in range(128, sq.shape[1], 128):
        total = total + sq[:, at : at + 128]

    @pl.when(step == 0)
    def _():
        sq_out[...] = total

    @pl.when(step > 0)
    def _():
        sq_out[...] += total


def gate_parts(z, y, xc, chan):
    full = y[...] + chan[KW + 2 : KW + 3, :] * xc[...]
    zv = z[...]
    sig = sigmoid(zv)
    return full, zv, sig


class CorePair:
    def __init__(self, x_out, y_out, keep_out, kept, codes, got, send_sem, recv_sem):
        self.outs = (x_out, y_out, keep_out)
        self.kept, self.codes, self.got, self.send_sem, self.recv_sem = kept, codes, got, send_sem, recv_sem
        self.dp, self.me = lax.axis_index("dp"), lax.axis_index("tensor")
        self.core = self.dp + 1 - 2 * lax.rem(self.dp, 2)

    def meet(self):
        barrier = pltpu.get_barrier_semaphore()
        pl.semaphore_signal(barrier, inc=1, device_id=(self.core, self.me), device_id_type=pl.DeviceIdType.MESH)
        pl.semaphore_wait(barrier, 1)

    def copy(self, step):
        slot = lax.rem(step, 2)
        return pltpu.make_async_remote_copy(
            src_ref=self.codes.at[slot], dst_ref=self.got.at[step], send_sem=self.send_sem.at[step],
            recv_sem=self.recv_sem.at[step], device_id=(self.core, self.me), device_id_type=pl.DeviceIdType.MESH,
        )

    def give(self, step, value):
        @pl.when(step >= 2)
        def _():
            self.copy(step - 2).wait_send()

        slot = lax.rem(step, 2)
        half = value.shape[0] // 2
        self.kept[slot] = value[:half]
        put_packed(self.codes.at[slot], value[half:])
        self.copy(step).start()

    def take(self, step, count):
        self.copy(step).wait_recv()
        core_sum(self.kept.at[lax.rem(step, 2)], self.got.at[step], *self.outs)

        @pl.when(step == count - 1)
        def _():
            for last in range(max(0, count - 2), count):
                self.copy(last).wait_send()


def core_pair_scratch(count, rows, columns):
    return [
        pltpu.VMEM((2, rows, columns), f32),
        pltpu.VMEM((2, rows + EXTRA, columns), jnp.int16),
        pltpu.VMEM((count, rows + EXTRA, columns), jnp.int16),
        pltpu.SemaphoreType.DMA((count,)),
        pltpu.SemaphoreType.DMA((count,)),
    ]


def in_steps(pair, count, make):
    step = pl.program_id(0)
    if pair is None:
        make(step)
        return

    @pl.when(step == 0)
    def _():
        pair.meet()

    @pl.when(step < count)
    def _():
        pair.give(step, make(step))

    @pl.when(step > 0)
    def _():
        pair.take(step - 1, count)


class LineSum:
    def __init__(self, n_t, pay, got, send_sem, recv_sem):
        self.n_t, self.pay, self.got, self.send_sem, self.recv_sem = n_t, pay, got, send_sem, recv_sem
        self.dp, self.me = lax.axis_index("dp"), lax.axis_index("tensor")

    def meet(self):
        barrier = pltpu.get_barrier_semaphore()
        for r in range(1, self.n_t):
            pl.semaphore_signal(
                barrier, inc=1, device_id=(self.dp, flip_all(self.me, r)), device_id_type=pl.DeviceIdType.MESH
            )
        pl.semaphore_wait(barrier, self.n_t - 1)

    def copy(self, r):
        return pltpu.make_async_remote_copy(
            src_ref=self.pay.at[r], dst_ref=self.got.at[r - 1], send_sem=self.send_sem.at[r - 1],
            recv_sem=self.recv_sem.at[r - 1], device_id=(self.dp, flip_all(self.me, r)),
            device_id_type=pl.DeviceIdType.MESH,
        )

    def start(self):
        for r in range(self.n_t - 1, 0, -1):
            self.copy(r).start()

    def total(self):
        value = None
        for r in range(1, self.n_t):
            self.copy(r).wait_recv()
            came = self.got.at[r - 1]
            part = codes_in(came, 0, came.shape[0] - EXTRA, exponent_in(came))
            value = part if value is None else value + part
        for r in range(1, self.n_t):
            self.copy(r).wait_send()
        return value


def line_scratch(n_t, rows, columns):
    return [
        pltpu.VMEM((n_t - 1, rows + EXTRA, columns), jnp.int16),
        pltpu.SemaphoreType.DMA((n_t - 1,)),
        pltpu.SemaphoreType.DMA((n_t - 1,)),
    ]


def out_kernel(count, z, y, xc, chan, rstd, w, e, et, x, valid, mixed_out, dg_out, gain_out, s_out, *rest):
    paired = len(rest) > 2
    pair = CorePair(*rest[:3], *rest[4:]) if paired else None
    acc = rest[3] if paired else rest[1]

    def make(step):
        full, zv, sig = gate_parts(z, y, xc, chan)
        g = full * (zv * sig)
        gain = chan[KW + 1 : KW + 2, :]
        scaled = g * rstd[...]
        gated = (scaled * gain).astype(bf16)
        d_w = dot(et[...], gated)
        if not paired:
            rest[0][...] = d_w
        wv = w[...]
        part = dot(gated, wv, NT)
        d_gated = dot(e[...], wv)
        dg_out[...] = d_gated
        gain_out[...] = jnp.sum(scaled * d_gated, axis=0, keepdims=True)
        prod = g * gain * d_gated
        total = prod[:, :128]
        for at in range(128, prod.shape[1], 128):
            total = total + prod[:, at : at + 128]

        @pl.when(step == 0)
        def _():
            acc[...] = part
            s_out[...] = total

        @pl.when(step > 0)
        def _():
            acc[...] += part
            s_out[...] += total

        @pl.when(step == count - 1)
        def _():
            mixed_out[...] = (x[...].astype(f32) + valid[...] * acc[...]).astype(bf16)

        return d_w

    in_steps(pair, count, make)


def gate_kernel(count, heads, inner, z, y, xc, chan, rstd, s, dgat, w, nt, cols, read_t, dy_out, dh_out, add_out, skip_out, *rest):
    paired = len(rest) > 1
    pair = CorePair(*rest) if paired else None

    def make(step):
        full, zv, sig = gate_parts(z, y, xc, chan)
        gate = zv * sig
        r = rstd[...]
        d_g = r * chan[KW + 1 : KW + 2, :] * dgat[...] - full * gate * (r * r * r * (s[...] / inner))
        dy = d_g * gate
        dy_out[...] = dy
        dz = (d_g * full * (sig * (1.0 + zv * (1.0 - sig)))).astype(bf16)
        d_w = dot(nt[...], dz)
        if not paired:
            rest[0][...] = d_w
        part = dot(dz, w[...], NT)
        add_out[...] = dot3(read_t[...], dy * spread(cols[...], 2, heads))
        skip_out[...] = jnp.sum(dy * xc[...], axis=0, keepdims=True)

        @pl.when(step == 0)
        def _():
            dh_out[...] = part

        @pl.when(step > 0)
        def _():
            dh_out[...] += part

        return d_w

    in_steps(pair, count, make)


def head_sums(prod, heads):
    width = prod.shape[1]
    owner = lax.broadcasted_iota(jnp.int32, (width, 128), 0) // PWIDTH
    pick = (owner == lax.broadcasted_iota(jnp.int32, (width, 128), 1)).astype(bf16)
    high, low = halves(prod)
    return dot(high, pick) + dot(low, pick)


def inside_back_kernel(heads, n_t, dy, xc, y, cols, lines, scores, marks, line_label, in_mat, read_mat, added, decay_row,
                       dx_out, sums_out, db_out, dc_out, enters, dsc, *scratch):
    rows = xc.shape[0]
    size, count = tiles_of(rows)
    step, steps = pl.program_id(0), pl.num_programs(0)
    carry = Carry(n_t, False, added, decay_row, enters, *scratch)

    @pl.when(step == 0)
    def _():
        dsc[...] = jnp.zeros_like(dsc)
        carry.meet()

    carry.tick(2 * step)

    col = cols[...]
    line = lines[...]
    d_y = dy[...]
    d_yt = d_y.T
    scaled = xc[...] * spread(col, 0, heads)
    low = low_lanes(rows)
    pieces = []
    for pair in range(heads // 2):
        if pair == heads // 4:
            carry.tick(2 * step + 1)
        at = slice(pair * 128, (pair + 1) * 128)
        xv, dv = scaled[:, at], d_y[:, at]
        th, tl = halves(d_yt[at])
        xh_f, dh_f = xv.astype(bf16).astype(f32), dv.astype(bf16).astype(f32)
        xl_f, dl_f = xv - xh_f, dv - dh_f
        xh_r, dl_r = pltpu.roll(xh_f, PWIDTH, 1), pltpu.roll(dl_f, PWIDTH, 1)
        for half in range(2):
            if half == 0:
                left = [jnp.where(low, dh_f, dl_r), jnp.where(low, dh_f, 0.0)]
                right = [jnp.where(low, xh_f, xh_r), jnp.where(low, xl_f, 0.0)]
            else:
                left = [jnp.where(low, dl_r, dh_f), jnp.where(low, 0.0, dh_f)]
                right = [jnp.where(low, xh_r, xh_f), jnp.where(low, 0.0, xl_f)]
            left = jnp.concatenate(left, axis=1).astype(bf16)
            right = jnp.concatenate(right, axis=1).astype(bf16)
            own = slice(half * PWIDTH, (half + 1) * PWIDTH)
            turned = jnp.concatenate([th[own], tl[own]], axis=0)
            tiles = []
            for j in range(count):
                acc = jnp.zeros((2 * PWIDTH, size), f32)
                for i in range(j, count):
                    ti, tj = slice(i * size, (i + 1) * size), slice(j * size, (j + 1) * size)
                    decay = decay_tile(col, line, heads, 2 * pair + half, i, j, size)
                    mh, ml = halves(decay * scores[ti, tj])
                    dsc[ti, tj] += dot(left[ti], right[tj], NT) * decay
                    acc = acc + dot(turned[:, ti], mh) + dot(turned[:, ti], ml)
                tiles.append(acc[:PWIDTH] + acc[PWIDTH:])
            pieces.append(jnp.concatenate(tiles, axis=1) if count > 1 else tiles[0])
    inside = jnp.concatenate(pieces, axis=0).T
    dx_out[...] = inside
    sums_out[...] = head_sums(d_y * y[...] - scaled * inside, heads)[:, :heads]

    @pl.when(step == steps - 1)
    def _():
        row_at = lax.broadcasted_iota(jnp.int32, (rows, rows), 0)
        col_at = lax.broadcasted_iota(jnp.int32, (rows, rows), 1)
        same = jnp.logical_and(row_at >= col_at, marks[:, 3:4] == line_label[0:1, :])
        d_scores = jnp.where(same, dsc[...], 0.0)
        dc_out[...] = dot3(d_scores, in_mat[...])
        db_out[...] = dot3(d_scores.T, read_mat[...])

        carry.drain(2 * carry.chunks)


def carry_back_kernel(heads, n_t, dy, xc, ps, inside, cols, in_mat, back_state, state, chan, masks, db_in, dc_in, *rest):
    if len(rest) > 5:
        pay, own, pre_out, sums_out, rows_out, db_out, dc_out, line_out, *scratch = rest
        line = LineSum(n_t, pay, *scratch)
    else:
        pre_out, sums_out, rows_out, db_out, dc_out = rest
        line = None
    rows = xc.shape[0]
    step, steps = pl.program_id(0), pl.num_programs(0)
    if line is not None:

        @pl.when(step == 0)
        def _():
            line.meet()
            line.start()

    @pl.when(step == 0)
    def _():
        db_out[...] = db_in[...]
        dc_out[...] = dc_in[...]

    col = cols[...]
    x = xc[...]
    d_y = dy[...]
    steps_wide, out_wide = spread(col, 0, heads), spread(col, 3, heads)
    scaled = x * steps_wide
    tail = dot3(in_mat[...], back_state[...]) * out_wide
    d_scaled = inside[...] + tail
    u = head_sums(scaled * tail, heads)
    r = head_sums(x * d_scaled, heads)
    sums_out[...] = jnp.concatenate([u[:, :heads], r[:, :heads]], axis=1)
    db_out[...] += dot3(scaled * out_wide, back_state[...], NT)
    dc_out[...] += dot3(d_y * spread(col, 2, heads), state[...], NT)
    d_x = d_scaled * steps_wide + chan[KW + 2 : KW + 3, :] * d_y
    chan_v, masks_v = chan[...], masks[...]
    pre = conv_of(ps, chan_v, masks_v, rows)
    sig = sigmoid(pre)
    d_pre = d_x * (sig * (1.0 + pre * (1.0 - sig)))
    pre_out[...] = d_pre
    taps = []
    for k in range(KW):
        offset = KW - 1 - k
        moved = shifted(ps, rows, offset)
        if offset:
            moved = moved * masks_v[:, offset - 1 : offset]
        taps.append(jnp.sum(d_pre * moved, axis=0, keepdims=True))
    taps.append(jnp.sum(d_pre, axis=0, keepdims=True))
    taps.append(jnp.sum(back_state[...] * state[...], axis=0, keepdims=True))
    taps.append(jnp.zeros((8 - KW - 2, d_pre.shape[1]), f32))
    rows_out[...] = jnp.concatenate(taps, axis=0)
    if line is not None:

        @pl.when(step == steps - 1)
        def _():
            line_out[...] = own[...] + line.total()


def stream_back_kernel(pre, halo, chan, masks, w, nt, dh_in, dh_out, dw_out, ext):
    rows = pre.shape[0]
    step = pl.program_id(0)
    ext[pl.ds(0, rows), :] = pre[...]
    ext[pl.ds(rows, 8), :] = halo[...]
    chan_v = chan[...]
    d_ps = chan_v[KW - 1 : KW, :] * pre[...]
    for offset in range(1, KW):
        tap = chan_v[KW - 1 - offset : KW - offset, :]
        moved = ext[pl.ds(offset, rows), :] * masks[pl.ds(offset, rows), offset - 1 : offset]
        d_ps = d_ps + tap * moved
    d_ps = d_ps.astype(bf16)
    dw_out[...] = dot(nt[...], d_ps)
    part = dot(d_ps, w[...], NT)

    @pl.when(step == 0)
    def _():
        dh_out[...] = dh_in[...] + part

    @pl.when(step > 0)
    def _():
        dh_out[...] += part


def gather_columns(ref, field, fields):
    size = ref.shape[2] // fields
    return jnp.concatenate([ref[g][:, field * size : (field + 1) * size] for g in range(ref.shape[0])], axis=1)


def post_kernel(sums, more, raw, step, heads, through, taps, db, dc, pre, bcp, masks, pre_out, dt_out, head_out, conv_out):
    rows, count = raw.shape
    row_at = lax.broadcasted_iota(jnp.int32, (rows, rows), 0)
    col_at = lax.broadcasted_iota(jnp.int32, (rows, rows), 1)
    upper = jnp.where(col_at >= row_at, 1.0, 0.0).astype(bf16)
    below = jnp.where(col_at < row_at, 1.0, 0.0).astype(bf16)
    q, u, r = gather_columns(sums, 0, 1), gather_columns(more, 0, 2), gather_columns(more, 1, 2)
    crossing = head_sums(taps[...], count)[KW + 1 : KW + 2, :count] * through[0:1, :]
    d_log = dot_exact(upper, q) + dot_exact(below, u) + crossing
    rates = -jnp.exp(heads[1:2, :])
    d_raw = (rates * d_log + r) * sigmoid(raw[...])
    dt_out[...] = d_raw.astype(bf16)
    head_out[...] = jnp.concatenate(
        [
            jnp.sum(d_raw, axis=0, keepdims=True),
            jnp.sum(d_log * step[...], axis=0, keepdims=True) * rates,
            jnp.zeros((6, count), f32),
        ],
        axis=0,
    )
    prev = pre[...]
    sig = sigmoid(prev)
    d_pre = jnp.concatenate([db[...], dc[...]], axis=1) * (sig * (1.0 + prev * (1.0 - sig)))
    pre_out[...] = d_pre
    out = []
    for tap in range(KW):
        offset = KW - 1 - tap
        moved = shifted(bcp, rows, offset)
        if offset:
            moved = moved * masks[:, offset - 1 : offset]
        out.append(jnp.sum(d_pre * moved, axis=0, keepdims=True))
    out.append(jnp.sum(d_pre, axis=0, keepdims=True))
    out.append(jnp.zeros((8 - KW - 1, d_pre.shape[1]), f32))
    conv_out[...] = jnp.concatenate(out, axis=0)


def conv_back(ext, chan, masks, rows):
    total = chan[KW - 1 : KW, :] * ext[pl.ds(0, rows), :]
    for offset in range(1, KW):
        tap = chan[KW - 1 - offset : KW - offset, :]
        total = total + tap * (ext[pl.ds(offset, rows), :] * masks[pl.ds(offset, rows), offset - 1 : offset])
    return total


def tail_kernel(n_t, pre, w, dh_in, line_pay, halo, chan, masks, nt, small_pre, small_halo, conv, d_dt, w_small, by_t, conv_rows_in,
                x, back, rstd, gain,
                g_out, token_out, bc_out, dt_sum_out, by_t_out, tiny_out, line_out,
                pre_ring, w_slot, acc, ext, small_ext, d_ps_all, load_sem, acc_sem,
                p_send, p_got, x_pay, y_pay, x_got, y_got, keep1, y_pay2, x_pay2, y_got2, x_got2, keep2,
                z_pay, z_got,
                s_send, s_keep, s_core, s_x, s_xgot, s_y, s_ygot, s_z, s_zbc, s_zdt,
                t_acc, t_got, b_acc, b_zgot, b_got,
                send_sem, recv_sem, line_got, line_send, line_recv):
    rows, columns = pre_ring.shape[1:]
    dp, me = lax.axis_index("dp"), lax.axis_index("tensor")
    core, xn, yn = flip(dp, 1), flip(dp, 2), flip(dp, 4)
    others = [flip_all(me, r) for r in range(1, n_t)]
    order = list(range(n_t - 1, -1, -1))
    slabs = [flip_all(me, r) for r in order]
    barrier = pltpu.get_barrier_semaphore()
    for there in (core, xn, yn):
        pl.semaphore_signal(barrier, inc=1, device_id=(there, me), device_id_type=MESH)
    for there in others:
        pl.semaphore_signal(barrier, inc=1, device_id=(dp, there), device_id_type=MESH)
    pl.semaphore_wait(barrier, 3 + len(others))
    used, started = [0], []

    def send(src, dst, device):
        at = used[0]
        used[0] += 1
        copy = pltpu.make_async_remote_copy(
            src_ref=src, dst_ref=dst, send_sem=send_sem.at[at], recv_sem=recv_sem.at[at],
            device_id=device, device_id_type=MESH,
        )
        copy.start()
        started.append(copy)
        return copy

    def load_pre(i):
        lanes = pl.ds(pl.multiple_of(slabs[i] * columns, 128), columns)
        copy = pltpu.make_async_copy(pre.at[:, lanes], pre_ring.at[i % 2], load_sem.at[0, i])
        copy.start()
        return copy

    def load_w(i):
        copy = pltpu.make_async_copy(w.at[slabs[i]], w_slot, load_sem.at[1, i])
        copy.start()
        return copy

    dh_copy = pltpu.make_async_copy(dh_in, acc, acc_sem)
    dh_copy.start()
    waiting = {0: load_pre(0)}
    w_copy = [load_w(0)]

    wide = w_small.shape[1]
    half = nt.shape[0] // 2
    part = half // 4
    state = {}

    def small_start():
        small_ext[pl.ds(0, rows), :] = small_pre[...]
        small_ext[pl.ds(rows, 8), :] = small_halo[...]
        d_bc = conv_back(small_ext, conv, masks, rows).astype(bf16)
        d_small = jnp.concatenate([d_bc.astype(f32), d_dt[...].astype(f32)], axis=1)
        d_small = jnp.concatenate([d_small, jnp.zeros((rows, wide - d_small.shape[1]), f32)], axis=1).astype(bf16)
        put_packed(s_send, dot(nt[pl.ds(half, half), :], d_small))
        state["s"] = send(s_send, s_core, (core, me))
        s_keep[...] = dot(nt[pl.ds(0, half), :], d_small)
        return d_small

    b_first = [send(by_t.at[there], b_zgot.at[r], (dp, there)) for r, there in enumerate(others)]
    line = LineSum(n_t, line_pay, line_got, line_send, line_recv)
    line.start()

    def small_x():
        state["s"].wait_recv()
        s_keep[...] += codes_in(s_core, 0, half, exponent_in(s_core))
        put_packed(s_x, s_keep[pl.ds(part, part), :], s_keep[pl.ds(3 * part, part), :])
        state["sx"] = send(s_x, s_xgot, (xn, me))

    def small_y():
        state["sx"].wait_recv()
        there = exponent_in(s_xgot)
        put_packed(s_y, s_keep[pl.ds(2 * part, part), :] + codes_in(s_xgot, part, part, there))
        s_keep[pl.ds(0, part), :] += codes_in(s_xgot, 0, part, there)
        state["sy"] = send(s_y, s_ygot, (yn, me))

    states, piece = 2 * STATE, part // n_t

    def small_z():
        state["sy"].wait_recv()
        s_keep[pl.ds(0, part), :] += codes_in(s_ygot, 0, part, exponent_in(s_ygot))
        s_z[...] = s_keep[pl.ds(0, part), pl.ds(states, wide - states)]
        state["sz"] = []
        for r, there in enumerate(others):
            rows_there = pl.ds(pl.multiple_of(there * piece, 8), piece)
            state["sz"].append(
                (
                    send(s_keep.at[rows_there, pl.ds(0, states)], s_zbc.at[r], (dp, there)),
                    send(s_z, s_zdt.at[r], (dp, there)),
                )
            )

    def small_end():
        rows_here = pl.ds(pl.multiple_of(me * piece, 8), piece)
        total_bc, total_dt = s_keep[rows_here, pl.ds(0, states)], s_z[...]
        for r, copies in enumerate(state["sz"]):
            for copy in copies:
                copy.wait_recv()
            total_bc = total_bc + s_zbc[r]
            total_dt = total_dt + s_zdt[r]
        bc_out[...] = total_bc
        dt_sum_out[...] = total_dt

    def by_t_first():
        total = by_t[me]
        for r, copy in enumerate(b_first):
            copy.wait_recv()
            total = total + b_zgot[r]
        b_acc[0] = total
        state["b"] = send(b_acc.at[0], b_got.at[0], (core, me))

    def by_t_hop(at):
        state["b"].wait_recv()
        total = b_acc[at] + b_got[at]
        if at == 2:
            by_t_out[...] = total
            return
        b_acc[at + 1] = total
        state["b"] = send(b_acc.at[at + 1], b_got.at[at + 1], ((xn, yn)[at], me))

    tiny_peers = [(core, me), (xn, me), (yn, me)]
    bit = 1
    while bit < n_t:
        tiny_peers.append((dp, flip(me, bit)))
        bit *= 2

    def tiny_hop(at):
        if at:
            state["t"].wait_recv()
            total = t_acc[at - 1] + t_got[at - 1]
            if at == len(tiny_peers):
                tiny_out[...] = total
                return
            t_acc[at] = total
        state["t"] = send(t_acc.at[at], t_got.at[at], tiny_peers[at])

    def product(i):
        waiting[i].wait()
        if i + 1 < n_t:
            waiting[i + 1] = load_pre(i + 1)
        ext[pl.ds(0, rows), :] = pre_ring[i % 2]
        ext[pl.ds(rows, 8), :] = halo[:, pl.ds(pl.multiple_of(slabs[i] * columns, 128), columns)]
        d_ps = conv_back(ext, chan[slabs[i]], masks, rows).astype(bf16)
        d_ps_all[i] = d_ps
        if i >= 2:
            state["p", i - 2].wait_send()
        put_packed(p_send.at[i % 2], dot(nt[pl.ds(half, half), :], d_ps))
        state["p", i] = send(p_send.at[i % 2], p_got.at[i], (core, me))

    def normed(i):
        w_copy[i].wait()
        if i == 0:
            dh_copy.wait()
        acc[...] += dot(d_ps_all[i], w_slot[...], NT)
        if i + 1 < n_t:
            w_copy.append(load_w(i + 1))

    def first(i):
        value = dot(nt[pl.ds(0, half), :], d_ps_all[i])
        state["p", i].wait_recv()
        if i >= 2:
            state["x", i - 2].wait_send()
            state["y", i - 2].wait_send()
        core_sum(value, p_got.at[i], x_pay.at[i % 2], y_pay.at[i % 2], keep1.at[i])
        state["x", i] = send(x_pay.at[i % 2], x_got.at[i], (xn, me))
        state["y", i] = send(y_pay.at[i % 2], y_got.at[i], (yn, me))

    def second(i):
        state["x", i].wait_recv()
        state["y", i].wait_recv()
        if i >= 2:
            state["x2", i - 2].wait_send()
            state["y2", i - 2].wait_send()
        cross_sum(keep1.at[i], x_got.at[i], y_got.at[i], y_pay2.at[i % 2], x_pay2.at[i % 2], keep2.at[i])
        state["y2", i] = send(y_pay2.at[i % 2], y_got2.at[i], (yn, me))
        state["x2", i] = send(x_pay2.at[i % 2], x_got2.at[i], (xn, me))

    def third(i):
        state["y2", i].wait_recv()
        state["x2", i].wait_recv()
        own_a, own_b = plane_sum(keep2.at[i], y_got2.at[i], x_got2.at[i])
        if order[i] == 0:
            g_out[0 : own_a.shape[0], :] = own_a
            g_out[own_a.shape[0] :, :] = own_b
            return
        put_packed(z_pay.at[i], own_a, own_b)
        state["z", i] = send(z_pay.at[i], z_got.at[i], (dp, slabs[i]))

    def token():
        d_normed = acc[...] + dot(d_small, w_small[...], NT)
        x_v = x[...].astype(f32)
        scaled = gain[0:1, :] * d_normed
        r = rstd[...]
        inner = jnp.sum(x_v * scaled, axis=1, keepdims=True) * (1.0 / x_v.shape[1])
        token_out[...] = (back[...].astype(f32) + r * scaled - x_v * (r * r * r) * inner).astype(bf16)
        d_gain = jnp.sum(x_v * r * d_normed, axis=0, keepdims=True)
        t_acc[0, 0:8, :] = jnp.concatenate([d_gain, jnp.zeros((7, d_gain.shape[1]), f32)], axis=0)
        t_acc[0, 8:16, :] = jnp.concatenate(
            [conv_rows_in[...], jnp.zeros((8, d_gain.shape[1] - conv_rows_in.shape[1]), f32)], axis=1
        )

    last = n_t - 1
    d_small = small_start()
    product(0)
    small_x()
    by_t_first()
    product(1)
    first(0)
    small_y()
    by_t_hop(0)
    for i in range(2, n_t):
        product(i)
        first(i - 1)
        if i == 2:
            small_z()
            by_t_hop(1)
    if n_t < 3:
        small_z()
        by_t_hop(1)
    by_t_hop(2)
    first(last)
    for i in range(n_t):
        normed(i)
    token()
    for i in range(n_t):
        if i <= len(tiny_peers):
            tiny_hop(i)
        second(i)
        if i:
            third(i - 1)
    for at in range(n_t, len(tiny_peers) + 1):
        if at == len(tiny_peers):
            third(last)
        tiny_hop(at)
    small_end()
    line_out[...] = line.total()
    for i in range(n_t - 1):
        state["z", i].wait_recv()
        ref = z_got.at[i]
        g_out[...] += codes_in(ref, 0, g_out.shape[0], exponent_in(ref))
    waited = [state[what, i] for what in ("p", "x", "y", "x2", "y2") for i in range(n_t - 2)]
    for copy in started:
        if not any(copy is other for other in waited):
            copy.wait_send()


def tail_scratch(n_t, rows, width, columns, wide):
    i16 = jnp.int16
    half = width // 2
    part = half // 4
    hops = 3 + (n_t.bit_length() - 1)
    return [
        pltpu.VMEM((2, rows, columns), f32),
        pltpu.VMEM((width, columns), bf16),
        pltpu.VMEM((rows, width), f32),
        pltpu.VMEM((rows + 8, columns), f32),
        pltpu.VMEM((rows + 8, 2 * STATE), f32),
        pltpu.VMEM((n_t, rows, columns), bf16),
        pltpu.SemaphoreType.DMA((2, n_t)),
        pltpu.SemaphoreType.DMA,
        pltpu.VMEM((2, half + EXTRA, columns), i16),
        pltpu.VMEM((n_t, half + EXTRA, columns), i16),
        pltpu.VMEM((2, part + EXTRA, columns), i16),
        pltpu.VMEM((2, part + EXTRA, columns), i16),
        pltpu.VMEM((n_t, part + EXTRA, columns), i16),
        pltpu.VMEM((n_t, part + EXTRA, columns), i16),
        pltpu.VMEM((n_t, 2 * part, columns), f32),
        pltpu.VMEM((2, part // 2 + EXTRA, columns), i16),
        pltpu.VMEM((2, part // 2 + EXTRA, columns), i16),
        pltpu.VMEM((n_t, part // 2 + EXTRA, columns), i16),
        pltpu.VMEM((n_t, part // 2 + EXTRA, columns), i16),
        pltpu.VMEM((n_t, part, columns), f32),
        pltpu.VMEM((n_t - 1, part + EXTRA, columns), i16),
        pltpu.VMEM((n_t - 1, part + EXTRA, columns), i16),
        pltpu.VMEM((half + EXTRA, wide), i16),
        pltpu.VMEM((half, wide), f32),
        pltpu.VMEM((half + EXTRA, wide), i16),
        pltpu.VMEM((2 * part + EXTRA, wide), i16),
        pltpu.VMEM((2 * part + EXTRA, wide), i16),
        pltpu.VMEM((part + EXTRA, wide), i16),
        pltpu.VMEM((part + EXTRA, wide), i16),
        pltpu.VMEM((part, wide - 2 * STATE), f32),
        pltpu.VMEM((n_t - 1, part // n_t, 2 * STATE), f32),
        pltpu.VMEM((n_t - 1, part, wide - 2 * STATE), f32),
        pltpu.VMEM((hops, 16, width), f32),
        pltpu.VMEM((hops, 16, width), f32),
        pltpu.VMEM((3, 8, columns), f32),
        pltpu.VMEM((n_t - 1, 8, columns), f32),
        pltpu.VMEM((3, 8, columns), f32),
        pltpu.SemaphoreType.DMA((6 * n_t + 8 * n_t,)),
        pltpu.SemaphoreType.DMA((6 * n_t + 8 * n_t,)),
        *line_scratch(n_t, part, columns),
    ]


def kernel_call(kernel, grid, ins, outs, scratch=(), scalar=None, flops=0, bytes_=0, ident=None):
    def spec(shape, block, index):
        if block is pl.ANY:
            return pl.BlockSpec(memory_space=pl.ANY)
        if block is None:
            rank = len(shape)
            return pl.BlockSpec(shape, lambda i, *_, rank=rank: (0,) * rank)
        return pl.BlockSpec(block, index)

    return pl.pallas_call(
        kernel,
        grid_spec=pltpu.PrefetchScalarGridSpec(
            num_scalar_prefetch=0 if scalar is None else 1,
            grid=(grid,),
            in_specs=[spec(a.shape, b, m) for a, b, m in ins],
            out_specs=[spec(s, b, m) for s, _, b, m in outs],
            scratch_shapes=list(scratch),
        ),
        out_shape=[jax.ShapeDtypeStruct(s, d) for s, d, _, _ in outs],
        compiler_params=pltpu.CompilerParams(
            dimension_semantics=("arbitrary",),
            vmem_limit_bytes=62 * 1024 * 1024,
            **({} if ident is None else {"collective_id": ident, "has_side_effects": True}),
        ),
        cost_estimate=pl.CostEstimate(flops=flops, bytes_accessed=bytes_, transcendentals=0),
    )(*([] if scalar is None else [scalar]), *[a for a, _, _ in ins])


MESH = pl.DeviceIdType.MESH


def flip(index, bit):
    return index + bit - 2 * bit * ((index // bit) % 2)


def flip_all(index, mask):
    bit = 1
    while bit <= mask:
        if mask & bit:
            index = flip(index, bit)
        bit *= 2
    return index


class Gather:
    def __init__(self, n_t, kinds, shards, outs, local_sem, send_sem, recv_sem):
        self.n_t, self.kinds, self.shards, self.outs = n_t, kinds, shards, outs
        self.local_sem, self.send_sem, self.recv_sem = local_sem, send_sem, recv_sem
        self.dp, self.me = lax.axis_index("dp"), lax.axis_index("tensor")
        self.core, self.xn, self.yn = flip(self.dp, 1), flip(self.dp, 2), flip(self.dp, 4)
        self.diagonal = flip(self.xn, 4)
        self.others = [flip_all(self.me, r) for r in range(1, n_t)]
        self.slots, self.started = {}, []
        self.following = {}
        self.units = []
        for k, kind in enumerate(kinds):
            if kind == "flat":
                self.units.append((k, None))
            elif kind == "slab":
                self.units += [(k, r) for r in range(n_t)]
        self.late = (0, 3, 4, 5)
        self.ticks = len(self.units) + self.late[-1]

    def arrival(self, unit):
        return self.units.index(unit) + self.late[-1]

    def meet(self):
        barrier = pltpu.get_barrier_semaphore()
        for there in (self.core, self.xn, self.yn):
            pl.semaphore_signal(barrier, inc=1, device_id=(there, self.me), device_id_type=MESH)
        for there in self.others:
            pl.semaphore_signal(barrier, inc=1, device_id=(self.dp, there), device_id_type=MESH)
        pl.semaphore_wait(barrier, 3 + len(self.others))

    def place(self, k, there, slab, part=None):
        rows = self.shards[k].shape[0]
        out = self.outs[k]
        if self.kinds[k] == "line":
            return out.at[slab]
        if self.kinds[k] == "flat":
            if slab is not None:
                return out.at[there, pl.ds(pl.multiple_of(slab * rows, 8), rows)]
            if part is None:
                return out.at[there]
            return out.at[there, pl.ds(part * (self.n_t * rows // 2), self.n_t * rows // 2)]
        start, size = there * rows, rows
        if part is not None:
            start, size = start + part * (rows // 2), rows // 2
        return out.at[slab, pl.ds(pl.multiple_of(start, 16), size)]

    def slab_of(self, unit):
        return None if unit[1] is None else flip_all(self.me, unit[1])

    def copy(self, name):
        what, k, r = name
        at = self.slots.setdefault(name, len(self.slots))
        slab = self.slab_of((k, r))
        mine, there = (self.dp, self.me), None
        if what == "far":
            src, dst, there = self.shards[k], self.place(k, self.dp, self.me), (self.dp, self.others[r - 1])
        elif what in ("x", "y", "core"):
            src = self.shards[k] if r == 0 else self.place(k, self.dp, slab)
            dst, there = self.place(k, self.dp, slab), ({"x": self.xn, "y": self.yn, "core": self.core}[what], self.me)
        elif what == "xy":
            src, there = self.place(k, self.xn, slab, 0), (self.yn, self.me)
        elif what == "yx":
            src, there = self.place(k, self.yn, slab, 1), (self.xn, self.me)
        else:
            src, there = self.place(k, {"cx": self.xn, "cy": self.yn, "cd": self.diagonal}[what], slab), (self.core, self.me)
        if what not in ("far", "x", "y", "core"):
            dst = src
        return pltpu.make_async_remote_copy(
            src_ref=src, dst_ref=dst, send_sem=self.send_sem.at[at], recv_sem=self.recv_sem.at[at],
            device_id=there, device_id_type=MESH,
        )

    def start(self, *name):
        self.copy(name).start()
        self.started.append(name)

    def keep(self, k):
        return pltpu.make_async_copy(self.shards[k], self.place(k, self.dp, self.me), self.local_sem.at[k])

    def begin(self):
        for k in range(len(self.kinds)):
            self.keep(k).start()
        later = list(self.following.values())
        for k in range(len(self.kinds)):
            if k not in later:
                self.begin_far(k)

    def begin_far(self, k):
        for r in range(1, self.n_t):
            self.start("far", k, r)

    def first(self, k, r):
        if r is None:
            self.keep(k).wait()
            for other in range(1, self.n_t):
                self.copy(("far", k, other)).wait_recv()
        elif r:
            self.copy(("far", k, r)).wait_recv()
        for what in ("x", "y", "core"):
            self.start(what, k, r)
        if (k, r) in self.following:
            self.begin_far(self.following[k, r])

    def second(self, k, r):
        self.copy(("x", k, r)).wait_recv()
        self.start("xy", k, r)
        self.start("cx", k, r)
        self.copy(("y", k, r)).wait_recv()
        self.start("yx", k, r)
        self.start("cy", k, r)

    def third(self, k, r):
        self.copy(("xy", k, r)).wait_recv()
        self.copy(("yx", k, r)).wait_recv()
        self.start("cd", k, r)

    def fourth(self, k, r):
        if r == 0:
            self.keep(k).wait()
        for what in ("core", "cx", "cy", "cd"):
            self.copy((what, k, r)).wait_recv()

    def tick(self, number):
        for late, stage in zip(self.late, (self.first, self.second, self.third, self.fourth)):
            if 0 <= number - late < len(self.units):
                stage(*self.units[number - late])

    def wait_line(self, k):
        self.keep(k).wait()
        for r in range(1, self.n_t):
            self.copy(("far", k, r)).wait_recv()

    def finish(self):
        for name in self.started:
            self.copy(name).wait_send()


def gather_shape(a, kind, n_dp, n_t):
    rows, columns = a.shape
    lead = {"line": (n_t, rows), "flat": (n_dp, n_t * rows), "slab": (n_t, n_dp * rows)}[kind]
    return (*lead, columns)


def gather_scratch(kinds, n_t):
    copies = len(kinds) * (n_t - 1) + 8 * sum({"line": 0, "flat": 1, "slab": n_t}[kind] for kind in kinds)
    return [
        pltpu.SemaphoreType.DMA((len(kinds),)),
        pltpu.SemaphoreType.DMA((copies,)),
        pltpu.SemaphoreType.DMA((copies,)),
    ]


def row_of_pieces(pieces, first, size, columns):
    lane = lax.broadcasted_iota(jnp.int32, (128, columns), 0)
    place = lax.broadcasted_iota(jnp.int32, (128, columns), 1)
    pick = jnp.where(lane == first + lax.rem(place, size), 1.0, 0.0).astype(bf16)
    high = pieces.astype(bf16)
    rest = pieces - high.astype(f32)
    middle = rest.astype(bf16)
    low = (rest - middle.astype(f32)).astype(bf16)
    wide = dot(high, pick) + (dot(middle, pick) + dot(low, pick))
    row = lax.broadcasted_iota(jnp.int32, wide.shape, 0) // 8
    place = lax.broadcasted_iota(jnp.int32, wide.shape, 1) // size
    return jnp.sum(jnp.where(row == place, wide, 0.0), axis=0, keepdims=True)


FRONT_KINDS = ("line", "flat", "flat", "flat", "slab", "slab", "slab")


def front_kernel(n_t, local_heads, per_bc, per_conv, tokens, marks, line_label, *refs):
    shards, refs = refs[:7], refs[7:]
    (chan, tiny, bc, dt, w_s, w_z, w_o, nh, rstd_out, gain_out, conv_out, heads_out), refs = refs[:12], refs[12:]
    small_outs, refs = refs[:13], refs[13:]
    (ps_out, xc_out, y_out, enters, prior, ps_slot, xc_slot, y_slot, w_slot, added, decay, slab_lines), refs = refs[:12], refs[12:]
    (prior_sem, load_sem, store_sem), refs = refs[:3], refs[3:]
    carry_refs, gather_refs = refs[:4], refs[4:]
    rows, width = tokens.shape
    local = chan.shape[2]
    gather = Gather(n_t, FRONT_KINDS, shards, (chan, tiny, bc, dt, w_s, w_z, w_o), *gather_refs)
    me = gather.me
    stream_units, gate_units, out_units = ([(at, r) for r in range(n_t)] for at in (4, 5, 6))
    gather.units = gather.units[:3] + stream_units[:1] + gate_units[:1] + stream_units[1:] + out_units[:1] + gate_units[1:] + out_units[1:]
    gather.following = {(4, n_t - 2): 5, (5, n_t - 2): 6}
    gather.meet()
    gather.begin()

    def prior_copy():
        return pltpu.make_async_remote_copy(
            src_ref=tokens.at[pl.ds(rows - HALO, HALO)], dst_ref=prior, send_sem=prior_sem.at[0], recv_sem=prior_sem.at[1],
            device_id=(gather.dp, lax.rem(me + 1, n_t)), device_id_type=MESH,
        )

    @pl.when(me < n_t - 1)
    def _():
        prior_copy().start()

    done = gather.arrival((3, None)) + 1
    for number in range(done):
        gather.tick(number)

    gather.wait_line(0)

    pieces = tiny[...].reshape(-1, 128)
    gain = row_of_pieces(pieces, 0, per_bc, width)
    gain_out[...] = jnp.broadcast_to(gain, gain_out.shape)
    conv_rows = [row_of_pieces(pieces, per_bc + per_conv * tap, per_conv, 2 * STATE) for tap in range(KW + 1)]
    conv_out[...] = jnp.concatenate([*conv_rows, jnp.zeros((8 - KW - 1, 2 * STATE), f32)], axis=0)

    @pl.when(me > 0)
    def _():
        prior_copy().wait_recv()

    @pl.when(me == 0)
    def _():
        prior[...] = jnp.zeros_like(prior)

    for ref, start, size in ((prior, 0, HALO), (tokens, HALO, rows)):
        x = ref[...].astype(f32)
        r = lax.rsqrt(jnp.sum(x * x, axis=1, keepdims=True) * (1.0 / width) + epsilon)
        nh[pl.ds(start, size), :] = (x * r * gain).astype(bf16)
    rstd_out[...] = r

    own = nh[pl.ds(HALO, rows), :]
    each = shards[3].shape[0]
    raw = [dot(own, dt[:, t * each : (t + 1) * each, :].reshape(width, local_heads)) for t in range(n_t)]
    heads = [
        jnp.concatenate([chan[t, 7:8, field * local_heads : (field + 1) * local_heads] for t in range(n_t)], axis=1)
        for field in range(2)
    ]
    heads = jnp.concatenate([*heads, jnp.zeros((6, heads[0].shape[1]), f32)], axis=0)
    heads_out[...] = heads
    small_core(
        nh, bc[...].reshape(width, 2 * STATE), jnp.concatenate(raw, axis=1), conv_out[...], marks, line_label, heads, *small_outs
    )
    in_t, wide, lines, scores, through = small_outs[6], small_outs[8], small_outs[10], small_outs[11], small_outs[12]
    low = low_lanes(8)
    for t in range(n_t):
        at = t * local_heads
        slab_lines[t, 0:local_heads, :] = lines[at : at + local_heads, :]
        for pair in range(local_heads // 2):
            left = through[:, at + 2 * pair : at + 2 * pair + 1]
            right = through[:, at + 2 * pair + 1 : at + 2 * pair + 2]
            lanes = t * local + pair * 128
            decay[:, lanes : lanes + 128] = jnp.where(low, left, right)

    def lanes_of(slab):
        return pl.ds(pl.multiple_of(slab * local, 128), local)

    def load(r):
        return pltpu.make_async_copy(w_s.at[flip_all(me, r)], w_slot, load_sem)

    def stores(r):
        lanes = lanes_of(flip_all(me, r))
        pairs = ((ps_slot, ps_out), (xc_slot, xc_out), (y_slot, y_out))
        return [pltpu.make_async_copy(a.at[r % 2], o.at[:, lanes], store_sem.at[at, r]) for at, (a, o) in enumerate(pairs)]

    def stream(r):
        slab = flip_all(me, r)
        load(r).wait()
        if r >= 2:
            for copy in stores(r - 2)[:2]:
                copy.wait()
        xc, add = stream_core(
            local_heads, nh, w_slot[...], chan[slab], marks[...], wide[slab], in_t[...], ps_slot.at[r % 2]
        )
        xc_slot[r % 2] = xc
        added[:, lanes_of(slab)] = add
        for copy in stores(r)[:2]:
            copy.start()

    def inside(r):
        slab = flip_all(me, r)
        if r >= 2:
            stores(r - 2)[2].wait()
        inside_core(local_heads, xc_slot[r % 2], wide[slab], slab_lines[slab], scores, y_slot.at[r % 2])
        stores(r)[2].start()

    carry = Carry(n_t, True, added, decay, enters, *carry_refs, lag=3)
    for r in range(n_t):
        while done <= gather.arrival((4, r)):
            gather.tick(done)
            done += 1
        load(r).start()
        stream(r)
        if r + 1 < n_t:
            inside(r)
    carried = 0

    def carry_on(count):
        for number in range(carried, min(carried + count, carry.ticks)):
            carry.tick(number)
        return min(carried + count, carry.ticks)

    carried = carry_on(3)
    inside(n_t - 1)
    while done < gather.ticks or carried < carry.ticks:
        if done < gather.ticks:
            gather.tick(done)
            done += 1
        carried = carry_on(3)
    carry.drain(carry.ticks)
    for r in range(max(0, n_t - 2), n_t):
        for copy in stores(r):
            copy.wait()

    @pl.when(me < n_t - 1)
    def _():
        prior_copy().wait_send()

    gather.finish()


def front_scratch(n_t, rows, width, local, local_heads, chunks, chunk):
    return [
        pltpu.VMEM((HALO, width), bf16),
        pltpu.VMEM((2, rows + HALO, local), f32),
        pltpu.VMEM((2, rows, local), f32),
        pltpu.VMEM((2, rows, local), f32),
        pltpu.VMEM((width, local), bf16),
        pltpu.VMEM((STATE, n_t * local), f32),
        pltpu.VMEM((8, n_t * local), f32),
        pltpu.VMEM((n_t, (local_heads + 7) // 8 * 8, rows), f32),
        pltpu.SemaphoreType.DMA((2,)),
        pltpu.SemaphoreType.DMA,
        pltpu.SemaphoreType.DMA((3, n_t)),
        *carry_scratch(chunks, chunk),
        *gather_scratch(FRONT_KINDS, n_t),
    ]


def adam_update(weight, grad, first, second, rate, decay):
    first_new = beta_first * first + (1.0 - beta_first) * grad
    second_new = beta_second * second + (1.0 - beta_second) * grad * grad
    first_hat = first_new / (1.0 - beta_first**STEP)
    second_hat = second_new / (1.0 - beta_second**STEP)
    weight_new = weight * (1.0 - rate * decay) - rate * first_hat / (
        jnp.sqrt(second_hat) + adam_epsilon
    )
    return (weight_new, first_new, second_new)


def xor_pairs(size, mask):
    return [(i, i ^ mask) for i in range(size)]


def tied(value, *others):
    return lax.optimization_barrier((value, *others))[0]


class PairSum:
    def __init__(self, x, y, keep, me):
        self.count, rows, self.columns = keep.shape
        self.rows = rows // 2
        self.keep, self.me = keep, me
        self.x = lax.ppermute(x, "dp", xor_pairs(8, 2))
        self.y = lax.ppermute(y, "dp", xor_pairs(8, 4))

    def call(self, kernel, ins, outs, scalar=None):
        def each(rows):
            return (None, rows, self.columns), lambda i, *_: (i, 0, 0)

        def at(rows):
            return (None, rows, self.columns), (lambda i, m: (m[0] ^ i, 0, 0)) if scalar is not None else each(rows)[1]

        return kernel_call(
            kernel,
            self.count,
            [(a, *at(a.shape[1])) for a in ins],
            [
                ((self.count, rows, self.columns), dtype, *each(rows))
                if lead is None
                else ((rows, self.columns), dtype, None, None)
                for rows, dtype, lead in outs
            ],
            scalar=scalar,
        )

    def over_yx(self):
        i16, rows = jnp.int16, self.rows
        outs = [(rows // 2 + EXTRA, i16, None), (rows // 2 + EXTRA, i16, None), (rows, f32, None)]
        y, x, self.keep = self.call(cross_sum, [self.keep, self.x, self.y], outs)
        self.y = lax.ppermute(y, "dp", xor_pairs(8, 4))
        self.x = lax.ppermute(x, "dp", xor_pairs(8, 2))
        return x, y

    def over_z(self):
        rows = self.rows
        self.own, z = self.call(
            plane_sum_kernel,
            [self.keep, self.y, self.x],
            [(rows, f32, 0), (rows + EXTRA, jnp.int16, None)],
            scalar=self.me,
        )
        return self.own, z


def gather_plain(shard, kind):
    if kind == "flat":
        return lax.all_gather(lax.all_gather(shard, "tensor", axis=0, tiled=True), "dp", axis=0)
    lines = lax.all_gather(shard, "tensor", axis=0)
    return lines if kind == "line" else lax.all_gather(lines, "dp", axis=1, tiled=True)


def scatter_plain(part):
    own = lax.psum_scatter(part, "dp", scatter_dimension=1, tiled=True)
    return lax.psum_scatter(own, "tensor", scatter_dimension=0, tiled=True)[0]


def body(
    tokens,
    cotangent,
    lengths,
    in_weight,
    in_first,
    in_second,
    dt_weight,
    dt_first,
    dt_second,
    bc_weight,
    bc_first,
    bc_second,
    out_weight,
    out_first,
    out_second,
    norm_gain,
    gain_first,
    gain_second,
    bc_conv,
    conv_first,
    conv_second,
    x_channel,
    channel_first,
    channel_second,
    head_params,
    head_first,
    head_second,
):
    n_dp, n_t = lax.axis_size("dp"), lax.axis_size("tensor")
    me = lax.axis_index("tensor")
    rows, width = tokens.shape
    local = x_channel.shape[1]
    inner = local * n_t
    local_heads = head_params.shape[1]
    all_heads = local_heads * n_t
    cb = local
    per, blocks, hb = 1, n_t, local_heads
    narrow = 512
    steps_in, hn = inner // narrow, narrow // PWIDTH
    own = me * rows
    up = [(i, i + 1) for i in range(n_t - 1)]
    down = [(i + 1, i) for i in range(n_t - 1)]

    paired = n_dp == 8 and n_t & (n_t - 1) == 0
    dp_me = lax.axis_index("dp")
    per_bc, per_conv = bc_weight.shape[0], bc_conv.shape[1]

    ends_of = jnp.cumsum(lengths[0])

    def labels_at(places):
        found = jnp.sum((places[:, None] >= ends_of[None, :]).astype(jnp.int32), axis=1)
        return jnp.where(places < 0, -1, found)

    span = labels_at(own + jnp.arange(-HALO, rows + 8, dtype=jnp.int32))
    labels = span[HALO : HALO + rows]
    valid = (own + jnp.arange(rows, dtype=jnp.int32) < ends_of[-1]).astype(f32)[:, None]
    masks = jnp.stack(
        [(span[HALO - o : HALO - o + rows + 8] == span[HALO:]).astype(f32) for o in (1, 2, 3)], axis=1
    )
    before, last = span[HALO - 1], labels[rows - 1]
    keep = (labels == before).astype(f32)[:, None]
    tail = (labels == last).astype(f32)[:, None]
    through = (last == before).astype(f32)
    marks = jnp.concatenate(
        [masks[:rows], labels.astype(f32)[:, None], keep, tail, jnp.full((rows, 1), through), jnp.zeros((rows, 1), f32)],
        axis=1,
    )
    line_label = jnp.broadcast_to(labels.astype(f32)[None], (8, rows))

    line = jnp.concatenate(
        [
            x_channel,
            jnp.repeat(head_params[2], PWIDTH)[None],
            jnp.pad(head_params[:2].reshape(1, -1), ((0, 0), (0, local - 2 * local_heads))),
        ],
        axis=0,
    )
    tiny = jnp.concatenate([norm_gain, bc_conv.reshape(-1)])
    tiny = jnp.pad(tiny[None], ((0, 7), (0, 128 - tiny.size)))
    shards = [
        (line, "line"),
        (tiny, "flat"),
        (bc_weight.astype(bf16), "flat"),
        (dt_weight.astype(bf16), "flat"),
        (in_weight[:, 1].astype(bf16), "slab"),
        (in_weight[:, 0].astype(bf16), "slab"),
        (out_weight.T.astype(bf16), "slab"),
    ]
    small_shapes = (
        (rows + HALO, 2 * STATE),
        (rows, 2 * STATE),
        (rows, all_heads),
        (rows, all_heads),
        (rows, STATE),
        (rows, STATE),
        (STATE, rows),
        (STATE, rows),
        (n_t, rows, 4 * local_heads),
        (steps_in, rows, 4 * hn),
        (all_heads, rows),
        (rows, rows),
        (8, all_heads),
    )
    if paired:
        gathers = [(gather_shape(a, kind, n_dp, n_t), a.dtype) for a, kind in shards]
        got = kernel_call(
            functools.partial(front_kernel, n_t, local_heads, per_bc, per_conv),
            1,
            [
                (tokens, None, None),
                (marks, None, None),
                (line_label, None, None),
                *[(a, pl.ANY, None) for a, _ in shards],
            ],
            [
                *[(s, d, None, None) for s, d in gathers[:4]],
                *[(s, d, pl.ANY, None) for s, d in gathers[4:]],
                ((rows + HALO, width), bf16, None, None),
                ((rows, 1), f32, None, None),
                ((8, width), f32, None, None),
                ((8, 2 * STATE), f32, None, None),
                ((8, all_heads), f32, None, None),
                *[(s, f32, None, None) for s in small_shapes],
                ((rows + HALO, inner), f32, pl.ANY, None),
                ((rows, inner), f32, pl.ANY, None),
                ((rows, inner), f32, pl.ANY, None),
                ((STATE, inner), f32, None, None),
            ],
            scratch=front_scratch(n_t, rows, width, local, local_heads, steps_in, narrow),
            ident=0,
        )
        chan, _, bc_low, dt_low, w_s, w_z, w_o, normed_ext, rstd_in, gain_rows, conv_pad, heads_pad, *got = got
        bcp, bc_pre, step_raw, step, in_mat, read_mat, in_t, read_t, cols, cols_n, lines, scores, through_all, *got = got
        ps, xc, inside, state = got
        bc_low = bc_low.reshape(width, -1)
        dt_low = dt_low.reshape(n_dp, n_t, -1, local_heads).swapaxes(1, 2).reshape(width, all_heads)
        normed = normed_ext[HALO:]
        gain, conv_full = gain_rows[0], conv_pad[: KW + 1]
    else:
        chan, tiny, bc_low, dt_low, w_s, w_z, w_o = [gather_plain(a, kind) for a, kind in shards]
        bc_low = bc_low.reshape(width, -1)
        dt_low = dt_low.reshape(n_dp, n_t, -1, local_heads).swapaxes(1, 2).reshape(width, all_heads)
        tiny = tiny.reshape(n_dp * n_t, 8, 128)[:, 0]
        gain = tiny[:, :per_bc].reshape(width)
        conv_full = tiny[:, per_bc : per_bc + (KW + 1) * per_conv].reshape(-1, KW + 1, per_conv)
        conv_full = conv_full.swapaxes(0, 1).reshape(KW + 1, -1)
        conv_pad = jnp.pad(conv_full, ((0, 3), (0, 0)))
        heads = chan[:, 7, : 2 * local_heads].reshape(n_t, 2, local_heads).swapaxes(0, 1).reshape(2, all_heads)
        heads_pad = jnp.pad(heads, ((0, 6), (0, 0)))
        gain_rows = jnp.broadcast_to(gain[None], (8, width))
        prior = lax.ppermute(tokens[-HALO:], "tensor", up)
        x_ext = jnp.concatenate([prior, tokens], axis=0).astype(f32)
        rstd_ext = lax.rsqrt(jnp.mean(x_ext * x_ext, axis=1, keepdims=True) + epsilon)
        normed_ext = (x_ext * rstd_ext * gain[None, :]).astype(bf16)
        rstd_in, normed = rstd_ext[HALO:], normed_ext[HALO:]
        got = kernel_call(
            small_kernel,
            1,
            [(a, None, None) for a in (normed_ext, bc_low, dt_low, conv_pad, marks, line_label, heads_pad)],
            [(s, f32, None, None) for s in small_shapes],
        )
        bcp, bc_pre, step_raw, step, in_mat, read_mat, in_t, read_t, cols, cols_n, lines, scores, through_all = got
    back = cotangent.astype(f32)
    masked = (back * valid).astype(bf16)
    if paired:
        order = dp_me ^ jnp.array([0, 2, 4, 6, 1, 3, 5, 7], jnp.int32)
    else:
        order = jnp.arange(n_dp, dtype=jnp.int32)

    def turned(a):
        return a.T.reshape(n_dp, -1, rows)[order].reshape(width, rows)

    normed_t, masked_t = turned(normed), turned(masked)

    decay_all = through_all[0]

    def slab(i, *_):
        return (i // per, 0, i % per)

    wspec = (None, width, cb), slab
    cspec = (None, 8, cb), slab
    colspec = (None, rows, 4 * hb), lambda i, *_: (i, 0, 0)
    colnspec = (None, rows, 4 * hn), lambda i, *_: (i, 0, 0)
    linespec = (hn, rows), lambda i, *_: (i, 0)
    chnspec = (rows, narrow), lambda i, *_: (0, i)
    chspec = (rows, cb), lambda i, *_: (0, i)
    stspec = (STATE, cb), lambda i, *_: (0, i)
    st_shape = (STATE, inner)
    decay_row = jnp.broadcast_to(jnp.repeat(decay_all, PWIDTH)[None], (8, inner))
    steps = blocks
    if paired:
        steps = blocks + 1

        def now(spec):
            return spec[0], lambda i, *_: spec[1](jnp.minimum(i, blocks - 1))

        def late(rows):
            return (None, rows, local), lambda i, *_: (jnp.maximum(i - 1, 0), 0, 0)

        part = width // 8
        dw_specs = [
            ((n_t, part + EXTRA, local), jnp.int16, *late(part + EXTRA)),
            ((n_t, part + EXTRA, local), jnp.int16, *late(part + EXTRA)),
            ((n_t, 2 * part, local), f32, *late(2 * part)),
        ]
        dw_scratch = core_pair_scratch(n_t, width // 2, local)
    else:
        now = tuple
        dw_specs = [((n_t, width, local), f32, *wspec)]
        dw_scratch = []
    full = (None, None)
    big = 2 * rows * width * inner

    if not paired:
        ps, xc, added = kernel_call(
            functools.partial(stream_kernel, hb),
            blocks,
            [(normed_ext, *full), (w_s, *wspec), (chan, *cspec), (marks, *full), (cols, *colspec), (in_t, *full)],
            [
                ((rows + HALO, inner), f32, (rows + HALO, cb), lambda i, *_: (0, i)),
                ((rows, inner), f32, *chspec),
                (st_shape, f32, *stspec),
            ],
        )
        inside, state = kernel_call(
            functools.partial(inside_kernel, hn, n_t),
            steps_in,
            [
                (xc, *chnspec),
                (cols_n, *colnspec),
                (lines, *linespec),
                (scores, *full),
                (added, *full),
                (decay_row, *full),
            ],
            [((rows, inner), f32, *chnspec), (st_shape, f32, *full)],
            scratch=carry_scratch(steps_in, narrow),
            ident=1,
        )
    z, y, squares = kernel_call(
        functools.partial(carry_kernel, hb),
        blocks,
        [
            (normed_ext, *full),
            (w_z, *wspec),
            (inside, *chspec),
            (xc, *chspec),
            (cols, *colspec),
            (read_mat, *full),
            (state, *stspec),
            (chan, *cspec),
        ],
        [
            ((rows, inner), f32, *chspec),
            ((rows, inner), f32, *chspec),
            ((rows, 128), f32, *full),
        ],
        flops=2 * big,
        bytes_=8 * width * inner,
    )
    rstd = lax.rsqrt(jnp.sum(squares, axis=1, keepdims=True) / inner + epsilon)

    rowspec = (1, cb), lambda i, *_: (0, i)
    mixed, d_gated, d_gain_gate, totals, *dw_o = kernel_call(
        functools.partial(out_kernel, blocks),
        steps,
        [
            (z, *now(chspec)),
            (y, *now(chspec)),
            (xc, *now(chspec)),
            (chan, *now(cspec)),
            (rstd, *full),
            (w_o, *now(wspec)),
            (masked, *full),
            (masked_t, *full),
            (tokens, *full),
            (valid, *full),
        ],
        [
            ((rows, width), bf16, *full),
            ((rows, inner), f32, *now(chspec)),
            ((1, inner), f32, *now(rowspec)),
            ((rows, 128), f32, *full),
            *dw_specs,
        ],
        scratch=[pltpu.VMEM((rows, width), f32), *dw_scratch],
        ident=5 if paired else None,
        flops=3 * big,
        bytes_=8 * width * inner,
    )
    turn = me[None].astype(jnp.int32)
    sum_o = PairSum(*dw_o, turn) if paired else None
    total = jnp.sum(totals, axis=1, keepdims=True)

    dy, dh, back_added, skip_rows, *dw_z = kernel_call(
        functools.partial(gate_kernel, blocks, hb, inner),
        steps,
        [
            (z, *now(chspec)),
            (y, *now(chspec)),
            (xc, *now(chspec)),
            (chan, *now(cspec)),
            (rstd, *full),
            (total, *full),
            (d_gated, *now(chspec)),
            (w_z, *now(wspec)),
            (normed_t, *full),
            (cols, *now(colspec)),
            (read_t, *full),
        ],
        [
            ((rows, inner), f32, *now(chspec)),
            ((rows, width), f32, *full),
            (st_shape, f32, *now(stspec)),
            ((1, inner), f32, *now(rowspec)),
            *dw_specs,
        ],
        scratch=dw_scratch,
        ident=6 if paired else None,
        flops=2 * big,
        bytes_=8 * width * inner,
    )
    if paired:
        sum_z = PairSum(*dw_z, turn)
        dy = tied(dy, *sum_o.over_yx())

    d_inside, sums, d_in_part, d_read_part, back_state = kernel_call(
        functools.partial(inside_back_kernel, hn, n_t),
        steps_in,
        [
            (dy, *chnspec),
            (xc, *chnspec),
            (y, *chnspec),
            (cols_n, *colnspec),
            (lines, *linespec),
            (scores, *full),
            (marks, *full),
            (line_label, *full),
            (in_mat, *full),
            (read_mat, *full),
            (back_added, *full),
            (decay_row, *full),
        ],
        [
            ((rows, inner), f32, *chnspec),
            ((steps_in, rows, hn), f32, (None, rows, hn), lambda i, *_: (i, 0, 0)),
            ((rows, STATE), f32, *full),
            ((rows, STATE), f32, *full),
            (st_shape, f32, *full),
        ],
        scratch=[pltpu.VMEM((rows, rows), f32), *carry_scratch(steps_in, narrow)],
        ident=2,
        flops=8 * big,
        bytes_=8 * width * inner,
    )
    if paired:
        sum_o.keep, sum_z.keep = tied(sum_o.keep, d_inside), tied(sum_z.keep, d_inside)
        own_o, pay_o = sum_o.over_z()
        d_inside = tied(d_inside, own_o, pay_o, *sum_z.over_yx())
        line_in = [(pay_o, *full), (own_o, *full)]
        line_get = [(own_o.shape, f32, *full)]
        line_refs = line_scratch(n_t, width // n_dp, local)
    else:
        line_in = line_get = line_refs = []
    d_pre, more_sums, tap_rows, d_in_mat, d_read_mat, *g_o = kernel_call(
        functools.partial(carry_back_kernel, hb, n_t),
        blocks,
        [
            (dy, *chspec),
            (xc, *chspec),
            (ps, (rows + HALO, cb), lambda i, *_: (0, i)),
            (d_inside, *chspec),
            (cols, *colspec),
            (in_mat, *full),
            (back_state, *stspec),
            (state, *stspec),
            (chan, *cspec),
            (marks, *full),
            (d_in_part, *full),
            (d_read_part, *full),
            *line_in,
        ],
        [
            ((rows, inner), f32, *chspec),
            ((blocks, rows, 2 * hb), f32, (None, rows, 2 * hb), lambda i, *_: (i, 0, 0)),
            ((8, inner), f32, (8, cb), lambda i, *_: (0, i)),
            ((rows, STATE), f32, *full),
            ((rows, STATE), f32, *full),
            *line_get,
        ],
        scratch=line_refs,
        ident=7 if paired else None,
        flops=2 * big,
        bytes_=8 * width * inner,
    )
    halo = lax.ppermute(d_pre[:8], "tensor", down)
    d_bc_pre, d_dt, d_heads, d_conv = kernel_call(
        post_kernel,
        1,
        [
            (a, None, None)
            for a in (
                sums,
                more_sums,
                step_raw,
                step,
                heads_pad,
                through_all,
                tap_rows,
                d_in_mat,
                d_read_mat,
                bc_pre,
                bcp,
                marks,
            )
        ],
        [
            ((rows, 2 * STATE), f32, None, None),
            ((rows, all_heads), bf16, None, None),
            ((8, all_heads), f32, None, None),
            ((8, 2 * STATE), f32, None, None),
        ],
    )
    bc_halo = lax.ppermute(d_bc_pre[:8], "tensor", down)
    head_row = jnp.pad(d_heads[:2, :, None], ((0, 0), (0, 0), (0, PWIDTH - 1)))
    head_row = head_row[0] + jnp.roll(head_row[1], 1, axis=1)
    by_t = jnp.concatenate([tap_rows[: KW + 1], d_gain_gate, skip_rows, head_row.reshape(1, inner)], axis=0)
    by_t = by_t.reshape(8, n_t, local).swapaxes(0, 1)
    wide = (2 * STATE + all_heads + 127) // 128 * 128
    per_dp = width // n_dp
    if paired:
        sum_z.keep = tied(sum_z.keep, d_pre)
        own_z, pay_z = sum_z.over_z()
        w_small = jnp.pad(jnp.concatenate([bc_low, dt_low], axis=1), ((0, 0), (0, wide - 2 * STATE - all_heads)))
        g_s, token_grad, g_bc, g_dt, by_t, tiny, far_z = kernel_call(
            functools.partial(tail_kernel, n_t),
            1,
            [
                (d_pre, pl.ANY, None),
                (w_s, pl.ANY, None),
                (dh, pl.ANY, None),
                (pay_z, pl.ANY, None),
                *[
                    (a, None, None)
                    for a in (
                        halo,
                        chan,
                        masks,
                        normed_t,
                        d_bc_pre,
                        bc_halo,
                        conv_pad,
                        d_dt,
                        w_small,
                        by_t,
                        d_conv,
                        tokens,
                        cotangent,
                        rstd_in,
                        gain_rows,
                    )
                ],
            ],
            [
                ((per_dp, local), f32, None, None),
                ((rows, width), bf16, None, None),
                ((per_bc, 2 * STATE), f32, None, None),
                ((per_dp, wide - 2 * STATE), f32, None, None),
                ((8, local), f32, None, None),
                ((16, width), f32, None, None),
                ((per_dp, local), f32, None, None),
            ],
            scratch=tail_scratch(n_t, rows, width, local, wide),
            ident=3,
            flops=10 * big,
            bytes_=30 * width * inner,
        )
        g_o, g_z = g_o[0], own_z + far_z
        d_gain, d_conv = tiny[0], tiny[8 : 8 + KW + 1, : 2 * STATE]
    else:
        dh, *dw_s = kernel_call(
            stream_back_kernel,
            blocks,
            [
                (d_pre, *chspec),
                (halo, (8, cb), lambda i, *_: (0, i)),
                (chan, *cspec),
                (masks, *full),
                (w_s, *wspec),
                (normed_t, *full),
                (dh, *full),
            ],
            [
                ((rows, width), f32, *full),
                *dw_specs,
            ],
            scratch=[pltpu.VMEM((rows + 8, cb), f32)],
        )
        bc_ext = jnp.concatenate([d_bc_pre, bc_halo], axis=0)
        d_bc = conv_full[KW - 1][None, :] * d_bc_pre
        for o in range(1, KW):
            d_bc = d_bc + conv_full[KW - 1 - o][None, :] * (masks[o : o + rows, o - 1 : o] * bc_ext[o : o + rows])
        d_bc = d_bc.astype(bf16)
        d_normed = dh + dot(d_bc, bc_low, NT) + dot(d_dt, dt_low, NT)
        scaled = gain[None, :] * d_normed
        token_grad = (
            back + rstd_in * scaled - x_ext[HALO:] * rstd_in**3 * jnp.sum(x_ext[HALO:] * scaled, axis=1, keepdims=True) / width
        ).astype(bf16)
        d_gain = lax.psum(jnp.sum(x_ext[HALO:] * rstd_in * d_normed, axis=0), ("dp", "tensor"))
        d_conv = lax.psum(d_conv[: KW + 1], ("dp", "tensor"))
        g_small = dot(normed_t, jnp.concatenate([d_bc, d_dt], axis=1)).reshape(n_dp, per_dp, -1)
        g_small = lax.psum(lax.psum_scatter(g_small, "dp", scatter_dimension=0), "tensor")
        by_t = lax.psum(lax.psum_scatter(by_t, "tensor", scatter_dimension=0), "dp")
        g_bc = lax.dynamic_slice(g_small, (me * per_bc, 0), (per_bc, 2 * STATE))
        g_dt = g_small[:, 2 * STATE :]
        g_o, g_z, g_s = scatter_plain(dw_o[0]), scatter_plain(dw_z[0]), scatter_plain(dw_s[0])
    place = dp_me * n_t + me
    g_dt = lax.dynamic_slice(g_dt, (0, me * local_heads), (per_dp, local_heads))
    g_gain = lax.dynamic_slice(d_gain, (place * per_bc,), (per_bc,))
    g_conv = lax.dynamic_slice(d_conv, (0, place * per_conv), (KW + 1, per_conv))
    g_channel = by_t[: KW + 2]
    ends = by_t[7].reshape(local_heads, PWIDTH)
    g_head = jnp.stack([ends[:, 0], ends[:, 1], jnp.sum(by_t[6].reshape(local_heads, PWIDTH), axis=1)])
    g_in = jnp.stack([g_z, g_s], axis=1)
    in_new = adam_update(in_weight, g_in, in_first, in_second, rate_matrix, decay_matrix)
    dt_new = adam_update(dt_weight, g_dt, dt_first, dt_second, rate_matrix, decay_matrix)
    bc_new = adam_update(bc_weight, g_bc, bc_first, bc_second, rate_matrix, decay_matrix)
    out_new = adam_update(out_weight, g_o.T, out_first, out_second, rate_matrix, decay_matrix)
    gain_new = adam_update(norm_gain, g_gain, gain_first, gain_second, rate_small, 0.0)
    conv_new = adam_update(bc_conv, g_conv, conv_first, conv_second, rate_small, 0.0)
    channel_new = adam_update(x_channel, g_channel, channel_first, channel_second, rate_small, 0.0)
    head_new = adam_update(head_params, g_head, head_first, head_second, rate_small, 0.0)
    return (
        mixed,
        token_grad,
        *in_new,
        *dt_new,
        *bc_new,
        *out_new,
        *gain_new,
        *conv_new,
        *channel_new,
        *head_new,
    )


def solution(mesh):
    return jax.shard_map(
        body,
        mesh=mesh,
        in_specs=(
            P(("dp", "tensor"), None),
            P(("dp", "tensor"), None),
            P("dp", None),
            P("dp", None, "tensor"),
            P("dp", None, "tensor"),
            P("dp", None, "tensor"),
            P("dp", "tensor"),
            P("dp", "tensor"),
            P("dp", "tensor"),
            P(("dp", "tensor"), None),
            P(("dp", "tensor"), None),
            P(("dp", "tensor"), None),
            P("tensor", "dp"),
            P("tensor", "dp"),
            P("tensor", "dp"),
            P(("dp", "tensor")),
            P(("dp", "tensor")),
            P(("dp", "tensor")),
            P(None, ("dp", "tensor")),
            P(None, ("dp", "tensor")),
            P(None, ("dp", "tensor")),
            P(None, "tensor"),
            P(None, "tensor"),
            P(None, "tensor"),
            P(None, "tensor"),
            P(None, "tensor"),
            P(None, "tensor"),
        ),
        out_specs=(
            P(("dp", "tensor"), None),
            P(("dp", "tensor"), None),
            P("dp", None, "tensor"),
            P("dp", None, "tensor"),
            P("dp", None, "tensor"),
            P("dp", "tensor"),
            P("dp", "tensor"),
            P("dp", "tensor"),
            P(("dp", "tensor"), None),
            P(("dp", "tensor"), None),
            P(("dp", "tensor"), None),
            P("tensor", "dp"),
            P("tensor", "dp"),
            P("tensor", "dp"),
            P(("dp", "tensor")),
            P(("dp", "tensor")),
            P(("dp", "tensor")),
            P(None, ("dp", "tensor")),
            P(None, ("dp", "tensor")),
            P(None, ("dp", "tensor")),
            P(None, "tensor"),
            P(None, "tensor"),
            P(None, "tensor"),
            P(None, "tensor"),
            P(None, "tensor"),
            P(None, "tensor"),
        ),
        check_vma=False,
    )
```

```python
import functools

import jax
import jax.numpy as jnp
from jax import lax
from jax.experimental import pallas as pl
from jax.experimental.pallas import tpu as pltpu
from jax.sharding import PartitionSpec as P

STATE = 128
KW = 4
STEP = 5
HALO = 16
BLOCK = 256
PWIDTH = 64
LOG2E = 1.4426950408889634

epsilon = 1e-05
adam_epsilon = 1e-08
beta_first = 0.9
beta_second = 0.95
rate_matrix = 0.02
rate_small = 0.2
decay_matrix = 0.1
highest = lax.Precision.HIGHEST

f32 = jnp.float32
bf16 = jnp.bfloat16
NN = (((1,), (0,)), ((), ()))
NT = (((1,), (1,)), ((), ()))
TN = (((0,), (0,)), ((), ()))


def dot(a, b, dims=NN):
    return lax.dot_general(a, b, dims, preferred_element_type=f32)


def halves(a):
    high = a.astype(bf16)
    return high, (a - high.astype(f32)).astype(bf16)


def dot3(a, b, dims=NN):
    ah, al = halves(a)
    bh, bl = halves(b)
    return dot(ah, bh, dims) + (dot(ah, bl, dims) + dot(al, bh, dims))


def sigmoid(v):
    return 1.0 / (1.0 + jnp.exp(-v))


def low_lanes(rows):
    return lax.broadcasted_iota(jnp.int32, (rows, 2 * PWIDTH), 1) < PWIDTH


def dot_exact(ones, a):
    high = a.astype(bf16)
    rest = a - high.astype(f32)
    middle = rest.astype(bf16)
    low = (rest - middle.astype(f32)).astype(bf16)
    return dot(ones, high) + (dot(ones, middle) + dot(ones, low))


EXTRA = 16
FULL = 32000.0


def column_exponent(value):
    most = jnp.max(jnp.abs(value), axis=0, keepdims=True)
    return jnp.floor(jnp.log2(jnp.maximum(most, 1e-30))) + 1.0


def put_codes(ref, start, value, exponent):
    codes = jnp.round(value * (FULL * jnp.exp2(-exponent)))
    ref[start : start + value.shape[0], :] = codes.astype(jnp.int32).astype(jnp.int16)


def put_exponent(ref, exponent):
    rows = ref.shape[0]
    wide = jnp.broadcast_to(exponent, (EXTRA, exponent.shape[1]))
    ref[rows - EXTRA : rows, :] = wide.astype(jnp.int32).astype(jnp.int16)


def exponent_in(ref):
    rows = ref.shape[0]
    return ref[rows - EXTRA : rows, :].astype(jnp.int32).astype(f32)[:1]


def codes_in(ref, start, rows, exponent):
    codes = ref[start : start + rows, :].astype(jnp.int32).astype(f32)
    return codes * (jnp.exp2(exponent) / FULL)


def put_packed(ref, *parts):
    exponent = column_exponent(parts[0])
    for part in parts[1:]:
        exponent = jnp.maximum(exponent, column_exponent(part))
    start = 0
    for part in parts:
        put_codes(ref, start, part, exponent)
        start += part.shape[0]
    put_exponent(ref, exponent)


def core_sum(keep, got, x_out, y_out, keep_out):
    rows = keep.shape[0] // 4
    half = rows // 2
    there = exponent_in(got)

    def total(part, second):
        start = part * rows + second * half
        return keep[start : start + half, :] + codes_in(got, start, half, there)

    put_packed(x_out, total(1, 0), total(3, 0))
    put_packed(y_out, total(2, 1), total(3, 1))
    for at, (part, second) in enumerate(((0, 0), (2, 0), (0, 1), (1, 1))):
        keep_out[at * half : (at + 1) * half, :] = total(part, second)


def cross_sum(keep, x_got, y_got, y_out, x_out, keep_out):
    half = y_out.shape[0] - EXTRA
    x_there, y_there = exponent_in(x_got), exponent_in(y_got)
    put_packed(y_out, keep[half : 2 * half, :] + codes_in(x_got, half, half, x_there))
    put_packed(x_out, keep[3 * half : 4 * half, :] + codes_in(y_got, half, half, y_there))
    keep_out[0:half, :] = keep[0:half, :] + codes_in(x_got, 0, half, x_there)
    keep_out[half : 2 * half, :] = keep[2 * half : 3 * half, :] + codes_in(y_got, 0, half, y_there)


def plane_sum(keep, y_got, x_got):
    half = keep.shape[0] // 2
    own_a = keep[0:half, :] + codes_in(y_got, 0, half, exponent_in(y_got))
    own_b = keep[half : 2 * half, :] + codes_in(x_got, 0, half, exponent_in(x_got))
    return own_a, own_b


def plane_sum_kernel(me, keep, y_got, x_got, own_out, z_out):
    own_a, own_b = plane_sum(keep, y_got, x_got)
    put_packed(z_out, own_a, own_b)

    @pl.when(pl.program_id(0) == 0)
    def _():
        half = own_a.shape[0]
        own_out[0:half, :] = own_a
        own_out[half : 2 * half, :] = own_b


def spread(cols, field, heads):
    rows = cols.shape[0]
    low = low_lanes(rows)
    parts = []
    for pair in range(heads // 2):
        at = field * heads + 2 * pair
        parts.append(jnp.where(low, cols[:, at : at + 1], cols[:, at + 1 : at + 2]))
    return parts[0] if len(parts) == 1 else jnp.concatenate(parts, axis=1)


def shifted(stream_ref, rows, offset):
    return stream_ref[pl.ds(HALO - offset, rows), :]


def conv_of(stream_ref, chan, masks, rows):
    pre = chan[KW : KW + 1, :] + chan[KW - 1 : KW, :] * shifted(stream_ref, rows, 0)
    for offset in range(1, KW):
        tap = chan[KW - 1 - offset : KW - offset, :]
        pre = pre + tap * (masks[:, offset - 1 : offset] * shifted(stream_ref, rows, offset))
    return pre


def tiles_of(rows):
    size = min(BLOCK, rows)
    return size, rows // size


def decay_tile(cols, lines, heads, head, i, j, size):
    gap = cols[i * size : (i + 1) * size, heads + head : heads + head + 1]
    gap = gap - lines[head : head + 1, j * size : (j + 1) * size]
    if i == j:
        gap = jnp.minimum(gap, 0.0)
    return jnp.exp2(gap)


def field_columns(fields, groups):
    size = fields[0].shape[1] // groups
    return [jnp.concatenate([f[:, g * size : (g + 1) * size] for f in fields], axis=1) for g in range(groups)]


def small_kernel(nh, wbc, wdt, conv, marks, line_label, heads, *outs):
    raw = dot(nh[pl.ds(HALO, marks.shape[0]), :], wdt[...])
    small_core(nh, wbc[...], raw, conv[...], marks, line_label, heads[...], *outs)


def small_core(nh, wbc, raw, conv, marks, line_label, heads, bcp_out, pre_out, raw_out, step_out, in_out, read_out,
               in_t_out, read_t_out, wide_out, narrow_out, lines_out, scores_out, through_out):
    rows = step_out.shape[0]
    bcp_out[...] = dot(nh[...], wbc)
    masks = marks[...]
    pre = conv_of(bcp_out, conv, masks, rows)
    pre_out[...] = pre
    bcc = pre * sigmoid(pre)
    in_mat, read_mat = bcc[:, :STATE], bcc[:, STATE:]
    in_out[...] = in_mat
    read_out[...] = read_mat
    in_t_out[...] = in_mat.T
    read_t_out[...] = read_mat.T
    raw = raw + heads[0:1, :]
    raw_out[...] = raw
    step = jnp.maximum(raw, 0.0) + jnp.log1p(jnp.exp(-jnp.abs(raw)))
    step_out[...] = step
    log_decay = step * (-jnp.exp(heads[1:2, :]))
    label, keep, tail, through = masks[:, 3:4], masks[:, 4:5], masks[:, 5:6], masks[0:1, 6:7]
    row_at = lax.broadcasted_iota(jnp.int32, (rows, rows), 0)
    col_at = lax.broadcasted_iota(jnp.int32, (rows, rows), 1)
    lower = row_at >= col_at
    cum = dot_exact(jnp.where(lower, 1.0, 0.0).astype(bf16), log_decay)
    end = cum[rows - 1 : rows, :]
    through_out[...] = jnp.broadcast_to(through * jnp.exp(end), through_out.shape)
    cum2 = cum * LOG2E
    fields = [step, cum2, keep * jnp.exp(cum), tail * jnp.exp(end - cum)]
    for at, group in enumerate(field_columns(fields, wide_out.shape[0])):
        wide_out[at] = group
    for at, group in enumerate(field_columns(fields, narrow_out.shape[0])):
        narrow_out[at] = group
    padded = jnp.concatenate([cum2, jnp.zeros((rows, 128 - cum2.shape[1]), f32)], axis=1)
    lines_out[...] = padded.T[: lines_out.shape[0]]
    same = jnp.logical_and(lower, label == line_label[0:1, :])
    scores_out[...] = jnp.where(same, dot3(read_mat, in_mat, NT), 0.0)


def stream_core(heads, nh, w, chan, masks, col, in_t, ps_out):
    rows = in_t.shape[1]
    ps_out[...] = dot(nh[...], w)
    pre = conv_of(ps_out, chan, masks, rows)
    xc = pre * sigmoid(pre)
    weight = spread(col, 0, heads) * spread(col, 3, heads)
    return xc, dot3(in_t, xc * weight)


def stream_kernel(heads, nh, w, chan, masks, cols, in_t, ps_out, xc_out, add_out):
    xc_out[...], add_out[...] = stream_core(heads, nh, w[...], chan[...], masks[...], cols[...], in_t[...], ps_out)


CARRY_LAG = 3


class Carry:
    def __init__(self, n_t, upward, added, decay, enters, out_codes, in_codes, send_sem, recv_sem, lag=CARRY_LAG):
        self.lag = lag
        self.n_t, self.added, self.decay, self.enters = n_t, added, decay, enters
        self.out_codes, self.in_codes, self.send_sem, self.recv_sem = out_codes, in_codes, send_sem, recv_sem
        me = lax.axis_index("tensor")
        self.dp, self.me = lax.axis_index("dp"), me
        self.at = me if upward else n_t - 1 - me
        self.following = lax.rem(me + (1 if upward else n_t - 1), n_t)
        self.chunks, _, self.size = out_codes.shape
        self.ticks = self.chunks + lag * (n_t - 1)

    def meet(self):
        barrier = pltpu.get_barrier_semaphore()
        for there in (1, self.n_t - 1):
            pl.semaphore_signal(
                barrier, inc=1, device_id=(self.dp, lax.rem(self.me + there, self.n_t)), device_id_type=pl.DeviceIdType.MESH
            )
        pl.semaphore_wait(barrier, 2)

    def copy(self, chunk):
        return pltpu.make_async_remote_copy(
            src_ref=self.out_codes.at[chunk], dst_ref=self.in_codes.at[chunk],
            send_sem=self.send_sem.at[chunk], recv_sem=self.recv_sem.at[chunk],
            device_id=(self.dp, self.following), device_id_type=pl.DeviceIdType.MESH,
        )

    def tick(self, number):
        chunk = number - self.lag * self.at

        @pl.when(jnp.logical_and(chunk >= 0, chunk < self.chunks))
        def _():
            lanes = pl.ds(pl.multiple_of(chunk * self.size, 128), self.size)

            @pl.when(self.at == 0)
            def _():
                self.enters[:, lanes] = jnp.zeros((STATE, self.size), f32)

            @pl.when(self.at > 0)
            def _():
                self.copy(chunk).wait_recv()
                came = self.in_codes.at[chunk]
                self.enters[:, lanes] = codes_in(came, 0, STATE, exponent_in(came))

            @pl.when(self.at < self.n_t - 1)
            def _():
                value = self.added[:, lanes] + self.decay[0:1, lanes] * self.enters[:, lanes]
                exponent = column_exponent(value)
                put_codes(self.out_codes.at[chunk], 0, value, exponent)
                put_exponent(self.out_codes.at[chunk], exponent)
                self.copy(chunk).start()

    def drain(self, done):
        @pl.loop(done, max(done, self.ticks))
        def _(number):
            self.tick(number)

        @pl.when(self.at < self.n_t - 1)
        def _():
            for chunk in range(self.chunks):
                self.copy(chunk).wait_send()


def carry_scratch(chunks, size):
    return [
        pltpu.VMEM((chunks, STATE + EXTRA, size), jnp.int16),
        pltpu.VMEM((chunks, STATE + EXTRA, size), jnp.int16),
        pltpu.SemaphoreType.DMA((chunks,)),
        pltpu.SemaphoreType.DMA((chunks,)),
    ]


def inside_core(heads, xc, col, line, scores, y_out, between=None):
    rows = xc.shape[0]
    size, count = tiles_of(rows)
    scaled = xc * spread(col, 0, heads)
    low = low_lanes(size)
    for pair in range(heads // 2):
        if between is not None and pair == heads // 4:
            between()
        xh, xl = halves(scaled[:, pair * 128 : (pair + 1) * 128])
        both = jnp.concatenate([xh, xl], axis=1)
        for i in range(count):
            outs = []
            for half in range(2):
                acc = jnp.zeros((size, 256), f32)
                for j in range(i + 1):
                    decay = decay_tile(col, line, heads, 2 * pair + half, i, j, size)
                    mix = decay * scores[i * size : (i + 1) * size, j * size : (j + 1) * size]
                    mh, ml = halves(mix)
                    part = both[j * size : (j + 1) * size]
                    acc = acc + dot(mh, part) + dot(ml, part)
                outs.append(acc[:, :128] + acc[:, 128:])
            y_out[i * size : (i + 1) * size, pair * 128 : (pair + 1) * 128] = jnp.where(low, outs[0], outs[1])


def inside_kernel(heads, n_t, xc, cols, lines, scores, added, decay, y_out, enters, *scratch):
    step, steps = pl.program_id(0), pl.num_programs(0)
    carry = Carry(n_t, True, added, decay, enters, *scratch)

    @pl.when(step == 0)
    def _():
        carry.meet()

    carry.tick(2 * step)
    inside_core(heads, xc[...], cols[...], lines[...], scores, y_out, lambda: carry.tick(2 * step + 1))

    @pl.when(step == steps - 1)
    def _():
        carry.drain(2 * carry.chunks)


def carry_kernel(heads, nh, w, inside, xc, cols, read_mat, state, chan, z_out, y_out, sq_out):
    rows = xc.shape[0]
    step = pl.program_id(0)
    z = dot(nh[pl.ds(HALO, rows), :], w[...])
    z_out[...] = z
    y = inside[...] + dot3(read_mat[...], state[...]) * spread(cols[...], 2, heads)
    y_out[...] = y
    g = (y + chan[KW + 2 : KW + 3, :] * xc[...]) * (z * sigmoid(z))
    sq = g * g
    total = sq[:, :128]
    for at in range(128, sq.shape[1], 128):
        total = total + sq[:, at : at + 128]

    @pl.when(step == 0)
    def _():
        sq_out[...] = total

    @pl.when(step > 0)
    def _():
        sq_out[...] += total


def gate_parts(z, y, xc, chan):
    full = y[...] + chan[KW + 2 : KW + 3, :] * xc[...]
    zv = z[...]
    sig = sigmoid(zv)
    return full, zv, sig


class CorePair:
    def __init__(self, x_out, y_out, keep_out, kept, codes, got, send_sem, recv_sem):
        self.outs = (x_out, y_out, keep_out)
        self.kept, self.codes, self.got, self.send_sem, self.recv_sem = kept, codes, got, send_sem, recv_sem
        self.dp, self.me = lax.axis_index("dp"), lax.axis_index("tensor")
        self.core = self.dp + 1 - 2 * lax.rem(self.dp, 2)

    def meet(self):
        barrier = pltpu.get_barrier_semaphore()
        pl.semaphore_signal(barrier, inc=1, device_id=(self.core, self.me), device_id_type=pl.DeviceIdType.MESH)
        pl.semaphore_wait(barrier, 1)

    def copy(self, step):
        slot = lax.rem(step, 2)
        return pltpu.make_async_remote_copy(
            src_ref=self.codes.at[slot], dst_ref=self.got.at[step], send_sem=self.send_sem.at[step],
            recv_sem=self.recv_sem.at[step], device_id=(self.core, self.me), device_id_type=pl.DeviceIdType.MESH,
        )

    def give(self, step, value):
        @pl.when(step >= 2)
        def _():
            self.copy(step - 2).wait_send()

        slot = lax.rem(step, 2)
        half = value.shape[0] // 2
        self.kept[slot] = value[:half]
        put_packed(self.codes.at[slot], value[half:])
        self.copy(step).start()

    def take(self, step, count):
        self.copy(step).wait_recv()
        core_sum(self.kept.at[lax.rem(step, 2)], self.got.at[step], *self.outs)

        @pl.when(step == count - 1)
        def _():
            for last in range(max(0, count - 2), count):
                self.copy(last).wait_send()


def core_pair_scratch(count, rows, columns):
    return [
        pltpu.VMEM((2, rows, columns), f32),
        pltpu.VMEM((2, rows + EXTRA, columns), jnp.int16),
        pltpu.VMEM((count, rows + EXTRA, columns), jnp.int16),
        pltpu.SemaphoreType.DMA((count,)),
        pltpu.SemaphoreType.DMA((count,)),
    ]


def in_steps(pair, count, make):
    step = pl.program_id(0)
    if pair is None:
        make(step)
        return

    @pl.when(step == 0)
    def _():
        pair.meet()

    @pl.when(step < count)
    def _():
        pair.give(step, make(step))

    @pl.when(step > 0)
    def _():
        pair.take(step - 1, count)


class LineSum:
    def __init__(self, n_t, pay, got, send_sem, recv_sem):
        self.n_t, self.pay, self.got, self.send_sem, self.recv_sem = n_t, pay, got, send_sem, recv_sem
        self.dp, self.me = lax.axis_index("dp"), lax.axis_index("tensor")

    def meet(self):
        barrier = pltpu.get_barrier_semaphore()
        for r in range(1, self.n_t):
            pl.semaphore_signal(
                barrier, inc=1, device_id=(self.dp, flip_all(self.me, r)), device_id_type=pl.DeviceIdType.MESH
            )
        pl.semaphore_wait(barrier, self.n_t - 1)

    def copy(self, r):
        return pltpu.make_async_remote_copy(
            src_ref=self.pay.at[r], dst_ref=self.got.at[r - 1], send_sem=self.send_sem.at[r - 1],
            recv_sem=self.recv_sem.at[r - 1], device_id=(self.dp, flip_all(self.me, r)),
            device_id_type=pl.DeviceIdType.MESH,
        )

    def start(self):
        for r in range(self.n_t - 1, 0, -1):
            self.copy(r).start()

    def total(self):
        value = None
        for r in range(1, self.n_t):
            self.copy(r).wait_recv()
            came = self.got.at[r - 1]
            part = codes_in(came, 0, came.shape[0] - EXTRA, exponent_in(came))
            value = part if value is None else value + part
        for r in range(1, self.n_t):
            self.copy(r).wait_send()
        return value


def line_scratch(n_t, rows, columns):
    return [
        pltpu.VMEM((n_t - 1, rows + EXTRA, columns), jnp.int16),
        pltpu.SemaphoreType.DMA((n_t - 1,)),
        pltpu.SemaphoreType.DMA((n_t - 1,)),
    ]


def out_kernel(count, z, y, xc, chan, rstd, w, e, et, x, valid, mixed_out, dg_out, gain_out, s_out, *rest):
    paired = len(rest) > 2
    pair = CorePair(*rest[:3], *rest[4:]) if paired else None
    acc = rest[3] if paired else rest[1]

    def make(step):
        full, zv, sig = gate_parts(z, y, xc, chan)
        g = full * (zv * sig)
        gain = chan[KW + 1 : KW + 2, :]
        scaled = g * rstd[...]
        gated = (scaled * gain).astype(bf16)
        d_w = dot(et[...], gated)
        if not paired:
            rest[0][...] = d_w
        wv = w[...]
        part = dot(gated, wv, NT)
        d_gated = dot(e[...], wv)
        dg_out[...] = d_gated
        gain_out[...] = jnp.sum(scaled * d_gated, axis=0, keepdims=True)
        prod = g * gain * d_gated
        total = prod[:, :128]
        for at in range(128, prod.shape[1], 128):
            total = total + prod[:, at : at + 128]

        @pl.when(step == 0)
        def _():
            acc[...] = part
            s_out[...] = total

        @pl.when(step > 0)
        def _():
            acc[...] += part
            s_out[...] += total

        @pl.when(step == count - 1)
        def _():
            mixed_out[...] = (x[...].astype(f32) + valid[...] * acc[...]).astype(bf16)

        return d_w

    in_steps(pair, count, make)


def gate_kernel(count, heads, inner, z, y, xc, chan, rstd, s, dgat, w, nt, cols, read_t, dy_out, dh_out, add_out, skip_out, *rest):
    paired = len(rest) > 1
    pair = CorePair(*rest) if paired else None

    def make(step):
        full, zv, sig = gate_parts(z, y, xc, chan)
        gate = zv * sig
        r = rstd[...]
        d_g = r * chan[KW + 1 : KW + 2, :] * dgat[...] - full * gate * (r * r * r * (s[...] / inner))
        dy = d_g * gate
        dy_out[...] = dy
        dz = (d_g * full * (sig * (1.0 + zv * (1.0 - sig)))).astype(bf16)
        d_w = dot(nt[...], dz)
        if not paired:
            rest[0][...] = d_w
        part = dot(dz, w[...], NT)
        add_out[...] = dot3(read_t[...], dy * spread(cols[...], 2, heads))
        skip_out[...] = jnp.sum(dy * xc[...], axis=0, keepdims=True)

        @pl.when(step == 0)
        def _():
            dh_out[...] = part

        @pl.when(step > 0)
        def _():
            dh_out[...] += part

        return d_w

    in_steps(pair, count, make)


def head_sums(prod, heads):
    width = prod.shape[1]
    owner = lax.broadcasted_iota(jnp.int32, (width, 128), 0) // PWIDTH
    pick = (owner == lax.broadcasted_iota(jnp.int32, (width, 128), 1)).astype(bf16)
    high, low = halves(prod)
    return dot(high, pick) + dot(low, pick)


def inside_back_kernel(heads, n_t, dy, xc, y, cols, lines, scores, marks, line_label, in_mat, read_mat, added, decay_row,
                       dx_out, sums_out, db_out, dc_out, enters, dsc, *scratch):
    rows = xc.shape[0]
    size, count = tiles_of(rows)
    step, steps = pl.program_id(0), pl.num_programs(0)
    carry = Carry(n_t, False, added, decay_row, enters, *scratch)

    @pl.when(step == 0)
    def _():
        dsc[...] = jnp.zeros_like(dsc)
        carry.meet()

    carry.tick(2 * step)

    col = cols[...]
    line = lines[...]
    d_y = dy[...]
    d_yt = d_y.T
    scaled = xc[...] * spread(col, 0, heads)
    low = low_lanes(rows)
    pieces = []
    for pair in range(heads // 2):
        if pair == heads // 4:
            carry.tick(2 * step + 1)
        at = slice(pair * 128, (pair + 1) * 128)
        xv, dv = scaled[:, at], d_y[:, at]
        th, tl = halves(d_yt[at])
        xh_f, dh_f = xv.astype(bf16).astype(f32), dv.astype(bf16).astype(f32)
        xl_f, dl_f = xv - xh_f, dv - dh_f
        xh_r, dl_r = pltpu.roll(xh_f, PWIDTH, 1), pltpu.roll(dl_f, PWIDTH, 1)
        for half in range(2):
            if half == 0:
                left = [jnp.where(low, dh_f, dl_r), jnp.where(low, dh_f, 0.0)]
                right = [jnp.where(low, xh_f, xh_r), jnp.where(low, xl_f, 0.0)]
            else:
                left = [jnp.where(low, dl_r, dh_f), jnp.where(low, 0.0, dh_f)]
                right = [jnp.where(low, xh_r, xh_f), jnp.where(low, 0.0, xl_f)]
            left = jnp.concatenate(left, axis=1).astype(bf16)
            right = jnp.concatenate(right, axis=1).astype(bf16)
            own = slice(half * PWIDTH, (half + 1) * PWIDTH)
            turned = jnp.concatenate([th[own], tl[own]], axis=0)
            tiles = []
            for j in range(count):
                acc = jnp.zeros((2 * PWIDTH, size), f32)
                for i in range(j, count):
                    ti, tj = slice(i * size, (i + 1) * size), slice(j * size, (j + 1) * size)
                    decay = decay_tile(col, line, heads, 2 * pair + half, i, j, size)
                    mh, ml = halves(decay * scores[ti, tj])
                    dsc[ti, tj] += dot(left[ti], right[tj], NT) * decay
                    acc = acc + dot(turned[:, ti], mh) + dot(turned[:, ti], ml)
                tiles.append(acc[:PWIDTH] + acc[PWIDTH:])
            pieces.append(jnp.concatenate(tiles, axis=1) if count > 1 else tiles[0])
    inside = jnp.concatenate(pieces, axis=0).T
    dx_out[...] = inside
    sums_out[...] = head_sums(d_y * y[...] - scaled * inside, heads)[:, :heads]

    @pl.when(step == steps - 1)
    def _():
        row_at = lax.broadcasted_iota(jnp.int32, (rows, rows), 0)
        col_at = lax.broadcasted_iota(jnp.int32, (rows, rows), 1)
        same = jnp.logical_and(row_at >= col_at, marks[:, 3:4] == line_label[0:1, :])
        d_scores = jnp.where(same, dsc[...], 0.0)
        dc_out[...] = dot3(d_scores, in_mat[...])
        db_out[...] = dot3(d_scores.T, read_mat[...])

        carry.drain(2 * carry.chunks)


def carry_back_kernel(heads, n_t, dy, xc, ps, inside, cols, in_mat, back_state, state, chan, masks, db_in, dc_in, *rest):
    if len(rest) > 5:
        pay, own, pre_out, sums_out, rows_out, db_out, dc_out, line_out, *scratch = rest
        line = LineSum(n_t, pay, *scratch)
    else:
        pre_out, sums_out, rows_out, db_out, dc_out = rest
        line = None
    rows = xc.shape[0]
    step, steps = pl.program_id(0), pl.num_programs(0)
    if line is not None:

        @pl.when(step == 0)
        def _():
            line.meet()
            line.start()

    @pl.when(step == 0)
    def _():
        db_out[...] = db_in[...]
        dc_out[...] = dc_in[...]

    col = cols[...]
    x = xc[...]
    d_y = dy[...]
    steps_wide, out_wide = spread(col, 0, heads), spread(col, 3, heads)
    scaled = x * steps_wide
    tail = dot3(in_mat[...], back_state[...]) * out_wide
    d_scaled = inside[...] + tail
    u = head_sums(scaled * tail, heads)
    r = head_sums(x * d_scaled, heads)
    sums_out[...] = jnp.concatenate([u[:, :heads], r[:, :heads]], axis=1)
    db_out[...] += dot3(scaled * out_wide, back_state[...], NT)
    dc_out[...] += dot3(d_y * spread(col, 2, heads), state[...], NT)
    d_x = d_scaled * steps_wide + chan[KW + 2 : KW + 3, :] * d_y
    chan_v, masks_v = chan[...], masks[...]
    pre = conv_of(ps, chan_v, masks_v, rows)
    sig = sigmoid(pre)
    d_pre = d_x * (sig * (1.0 + pre * (1.0 - sig)))
    pre_out[...] = d_pre
    taps = []
    for k in range(KW):
        offset = KW - 1 - k
        moved = shifted(ps, rows, offset)
        if offset:
            moved = moved * masks_v[:, offset - 1 : offset]
        taps.append(jnp.sum(d_pre * moved, axis=0, keepdims=True))
    taps.append(jnp.sum(d_pre, axis=0, keepdims=True))
    taps.append(jnp.sum(back_state[...] * state[...], axis=0, keepdims=True))
    taps.append(jnp.zeros((8 - KW - 2, d_pre.shape[1]), f32))
    rows_out[...] = jnp.concatenate(taps, axis=0)
    if line is not None:

        @pl.when(step == steps - 1)
        def _():
            line_out[...] = own[...] + line.total()


def stream_back_kernel(pre, halo, chan, masks, w, nt, dh_in, dh_out, dw_out, ext):
    rows = pre.shape[0]
    step = pl.program_id(0)
    ext[pl.ds(0, rows), :] = pre[...]
    ext[pl.ds(rows, 8), :] = halo[...]
    chan_v = chan[...]
    d_ps = chan_v[KW - 1 : KW, :] * pre[...]
    for offset in range(1, KW):
        tap = chan_v[KW - 1 - offset : KW - offset, :]
        moved = ext[pl.ds(offset, rows), :] * masks[pl.ds(offset, rows), offset - 1 : offset]
        d_ps = d_ps + tap * moved
    d_ps = d_ps.astype(bf16)
    dw_out[...] = dot(nt[...], d_ps)
    part = dot(d_ps, w[...], NT)

    @pl.when(step == 0)
    def _():
        dh_out[...] = dh_in[...] + part

    @pl.when(step > 0)
    def _():
        dh_out[...] += part


def gather_columns(ref, field, fields):
    size = ref.shape[2] // fields
    return jnp.concatenate([ref[g][:, field * size : (field + 1) * size] for g in range(ref.shape[0])], axis=1)


def post_kernel(sums, more, raw, step, heads, through, taps, db, dc, pre, bcp, masks, pre_out, dt_out, head_out, conv_out):
    rows, count = raw.shape
    row_at = lax.broadcasted_iota(jnp.int32, (rows, rows), 0)
    col_at = lax.broadcasted_iota(jnp.int32, (rows, rows), 1)
    upper = jnp.where(col_at >= row_at, 1.0, 0.0).astype(bf16)
    below = jnp.where(col_at < row_at, 1.0, 0.0).astype(bf16)
    q, u, r = gather_columns(sums, 0, 1), gather_columns(more, 0, 2), gather_columns(more, 1, 2)
    crossing = head_sums(taps[...], count)[KW + 1 : KW + 2, :count] * through[0:1, :]
    d_log = dot_exact(upper, q) + dot_exact(below, u) + crossing
    rates = -jnp.exp(heads[1:2, :])
    d_raw = (rates * d_log + r) * sigmoid(raw[...])
    dt_out[...] = d_raw.astype(bf16)
    head_out[...] = jnp.concatenate(
        [
            jnp.sum(d_raw, axis=0, keepdims=True),
            jnp.sum(d_log * step[...], axis=0, keepdims=True) * rates,
            jnp.zeros((6, count), f32),
        ],
        axis=0,
    )
    prev = pre[...]
    sig = sigmoid(prev)
    d_pre = jnp.concatenate([db[...], dc[...]], axis=1) * (sig * (1.0 + prev * (1.0 - sig)))
    pre_out[...] = d_pre
    out = []
    for tap in range(KW):
        offset = KW - 1 - tap
        moved = shifted(bcp, rows, offset)
        if offset:
            moved = moved * masks[:, offset - 1 : offset]
        out.append(jnp.sum(d_pre * moved, axis=0, keepdims=True))
    out.append(jnp.sum(d_pre, axis=0, keepdims=True))
    out.append(jnp.zeros((8 - KW - 1, d_pre.shape[1]), f32))
    conv_out[...] = jnp.concatenate(out, axis=0)


def conv_back(ext, chan, masks, rows):
    total = chan[KW - 1 : KW, :] * ext[pl.ds(0, rows), :]
    for offset in range(1, KW):
        tap = chan[KW - 1 - offset : KW - offset, :]
        total = total + tap * (ext[pl.ds(offset, rows), :] * masks[pl.ds(offset, rows), offset - 1 : offset])
    return total


def tail_kernel(n_t, pre, w, dh_in, line_pay, halo, chan, masks, nt, small_pre, small_halo, conv, d_dt, w_small, by_t, conv_rows_in,
                x, back, rstd, gain,
                g_out, token_out, bc_out, dt_sum_out, by_t_out, tiny_out, line_out,
                pre_ring, w_slot, acc, ext, small_ext, d_ps_all, load_sem, acc_sem,
                p_send, p_got, x_pay, y_pay, x_got, y_got, keep1, y_pay2, x_pay2, y_got2, x_got2, keep2,
                z_pay, z_got,
                s_send, s_keep, s_core, s_x, s_xgot, s_y, s_ygot, s_z, s_zbc, s_zdt,
                t_acc, t_got, b_acc, b_zgot, b_got,
                send_sem, recv_sem, line_got, line_send, line_recv):
    rows, columns = pre_ring.shape[1:]
    dp, me = lax.axis_index("dp"), lax.axis_index("tensor")
    core, xn, yn = flip(dp, 1), flip(dp, 2), flip(dp, 4)
    others = [flip_all(me, r) for r in range(1, n_t)]
    order = list(range(n_t - 1, -1, -1))
    slabs = [flip_all(me, r) for r in order]
    barrier = pltpu.get_barrier_semaphore()
    for there in (core, xn, yn):
        pl.semaphore_signal(barrier, inc=1, device_id=(there, me), device_id_type=MESH)
    for there in others:
        pl.semaphore_signal(barrier, inc=1, device_id=(dp, there), device_id_type=MESH)
    pl.semaphore_wait(barrier, 3 + len(others))
    used, started = [0], []

    def send(src, dst, device):
        at = used[0]
        used[0] += 1
        copy = pltpu.make_async_remote_copy(
            src_ref=src, dst_ref=dst, send_sem=send_sem.at[at], recv_sem=recv_sem.at[at],
            device_id=device, device_id_type=MESH,
        )
        copy.start()
        started.append(copy)
        return copy

    def load_pre(i):
        lanes = pl.ds(pl.multiple_of(slabs[i] * columns, 128), columns)
        copy = pltpu.make_async_copy(pre.at[:, lanes], pre_ring.at[i % 2], load_sem.at[0, i])
        copy.start()
        return copy

    def load_w(i):
        copy = pltpu.make_async_copy(w.at[slabs[i]], w_slot, load_sem.at[1, i])
        copy.start()
        return copy

    dh_copy = pltpu.make_async_copy(dh_in, acc, acc_sem)
    dh_copy.start()
    waiting = {0: load_pre(0)}
    w_copy = [load_w(0)]

    wide = w_small.shape[1]
    half = nt.shape[0] // 2
    part = half // 4
    state = {}

    def small_start():
        small_ext[pl.ds(0, rows), :] = small_pre[...]
        small_ext[pl.ds(rows, 8), :] = small_halo[...]
        d_bc = conv_back(small_ext, conv, masks, rows).astype(bf16)
        d_small = jnp.concatenate([d_bc.astype(f32), d_dt[...].astype(f32)], axis=1)
        d_small = jnp.concatenate([d_small, jnp.zeros((rows, wide - d_small.shape[1]), f32)], axis=1).astype(bf16)
        put_packed(s_send, dot(nt[pl.ds(half, half), :], d_small))
        state["s"] = send(s_send, s_core, (core, me))
        s_keep[...] = dot(nt[pl.ds(0, half), :], d_small)
        return d_small

    b_first = [send(by_t.at[there], b_zgot.at[r], (dp, there)) for r, there in enumerate(others)]
    line = LineSum(n_t, line_pay, line_got, line_send, line_recv)
    line.start()

    def small_x():
        state["s"].wait_recv()
        s_keep[...] += codes_in(s_core, 0, half, exponent_in(s_core))
        put_packed(s_x, s_keep[pl.ds(part, part), :], s_keep[pl.ds(3 * part, part), :])
        state["sx"] = send(s_x, s_xgot, (xn, me))

    def small_y():
        state["sx"].wait_recv()
        there = exponent_in(s_xgot)
        put_packed(s_y, s_keep[pl.ds(2 * part, part), :] + codes_in(s_xgot, part, part, there))
        s_keep[pl.ds(0, part), :] += codes_in(s_xgot, 0, part, there)
        state["sy"] = send(s_y, s_ygot, (yn, me))

    states, piece = 2 * STATE, part // n_t

    def small_z():
        state["sy"].wait_recv()
        s_keep[pl.ds(0, part), :] += codes_in(s_ygot, 0, part, exponent_in(s_ygot))
        s_z[...] = s_keep[pl.ds(0, part), pl.ds(states, wide - states)]
        state["sz"] = []
        for r, there in enumerate(others):
            rows_there = pl.ds(pl.multiple_of(there * piece, 8), piece)
            state["sz"].append(
                (
                    send(s_keep.at[rows_there, pl.ds(0, states)], s_zbc.at[r], (dp, there)),
                    send(s_z, s_zdt.at[r], (dp, there)),
                )
            )

    def small_end():
        rows_here = pl.ds(pl.multiple_of(me * piece, 8), piece)
        total_bc, total_dt = s_keep[rows_here, pl.ds(0, states)], s_z[...]
        for r, copies in enumerate(state["sz"]):
            for copy in copies:
                copy.wait_recv()
            total_bc = total_bc + s_zbc[r]
            total_dt = total_dt + s_zdt[r]
        bc_out[...] = total_bc
        dt_sum_out[...] = total_dt

    def by_t_first():
        total = by_t[me]
        for r, copy in enumerate(b_first):
            copy.wait_recv()
            total = total + b_zgot[r]
        b_acc[0] = total
        state["b"] = send(b_acc.at[0], b_got.at[0], (core, me))

    def by_t_hop(at):
        state["b"].wait_recv()
        total = b_acc[at] + b_got[at]
        if at == 2:
            by_t_out[...] = total
            return
        b_acc[at + 1] = total
        state["b"] = send(b_acc.at[at + 1], b_got.at[at + 1], ((xn, yn)[at], me))

    tiny_peers = [(core, me), (xn, me), (yn, me)]
    bit = 1
    while bit < n_t:
        tiny_peers.append((dp, flip(me, bit)))
        bit *= 2

    def tiny_hop(at):
        if at:
            state["t"].wait_recv()
            total = t_acc[at - 1] + t_got[at - 1]
            if at == len(tiny_peers):
                tiny_out[...] = total
                return
            t_acc[at] = total
        state["t"] = send(t_acc.at[at], t_got.at[at], tiny_peers[at])

    def product(i):
        waiting[i].wait()
        if i + 1 < n_t:
            waiting[i + 1] = load_pre(i + 1)
        ext[pl.ds(0, rows), :] = pre_ring[i % 2]
        ext[pl.ds(rows, 8), :] = halo[:, pl.ds(pl.multiple_of(slabs[i] * columns, 128), columns)]
        d_ps = conv_back(ext, chan[slabs[i]], masks, rows).astype(bf16)
        d_ps_all[i] = d_ps
        if i >= 2:
            state["p", i - 2].wait_send()
        put_packed(p_send.at[i % 2], dot(nt[pl.ds(half, half), :], d_ps))
        state["p", i] = send(p_send.at[i % 2], p_got.at[i], (core, me))

    def normed(i):
        w_copy[i].wait()
        if i == 0:
            dh_copy.wait()
        acc[...] += dot(d_ps_all[i], w_slot[...], NT)
        if i + 1 < n_t:
            w_copy.append(load_w(i + 1))

    def first(i):
        value = dot(nt[pl.ds(0, half), :], d_ps_all[i])
        state["p", i].wait_recv()
        if i >= 2:
            state["x", i - 2].wait_send()
            state["y", i - 2].wait_send()
        core_sum(value, p_got.at[i], x_pay.at[i % 2], y_pay.at[i % 2], keep1.at[i])
        state["x", i] = send(x_pay.at[i % 2], x_got.at[i], (xn, me))
        state["y", i] = send(y_pay.at[i % 2], y_got.at[i], (yn, me))

    def second(i):
        state["x", i].wait_recv()
        state["y", i].wait_recv()
        if i >= 2:
            state["x2", i - 2].wait_send()
            state["y2", i - 2].wait_send()
        cross_sum(keep1.at[i], x_got.at[i], y_got.at[i], y_pay2.at[i % 2], x_pay2.at[i % 2], keep2.at[i])
        state["y2", i] = send(y_pay2.at[i % 2], y_got2.at[i], (yn, me))
        state["x2", i] = send(x_pay2.at[i % 2], x_got2.at[i], (xn, me))

    def third(i):
        state["y2", i].wait_recv()
        state["x2", i].wait_recv()
        own_a, own_b = plane_sum(keep2.at[i], y_got2.at[i], x_got2.at[i])
        if order[i] == 0:
            g_out[0 : own_a.shape[0], :] = own_a
            g_out[own_a.shape[0] :, :] = own_b
            return
        put_packed(z_pay.at[i], own_a, own_b)
        state["z", i] = send(z_pay.at[i], z_got.at[i], (dp, slabs[i]))

    def token():
        d_normed = acc[...] + dot(d_small, w_small[...], NT)
        x_v = x[...].astype(f32)
        scaled = gain[0:1, :] * d_normed
        r = rstd[...]
        inner = jnp.sum(x_v * scaled, axis=1, keepdims=True) * (1.0 / x_v.shape[1])
        token_out[...] = (back[...].astype(f32) + r * scaled - x_v * (r * r * r) * inner).astype(bf16)
        d_gain = jnp.sum(x_v * r * d_normed, axis=0, keepdims=True)
        t_acc[0, 0:8, :] = jnp.concatenate([d_gain, jnp.zeros((7, d_gain.shape[1]), f32)], axis=0)
        t_acc[0, 8:16, :] = jnp.concatenate(
            [conv_rows_in[...], jnp.zeros((8, d_gain.shape[1] - conv_rows_in.shape[1]), f32)], axis=1
        )

    d_small = small_start()
    product(0)
    small_x()
    by_t_first()
    product(1)
    first(0)
    small_y()
    by_t_hop(0)
    product(2)
    first(1)
    second(0)
    normed(0)
    product(3)
    first(2)
    small_z()
    by_t_hop(1)
    third(0)
    second(1)
    normed(1)
    first(3)
    by_t_hop(2)
    normed(2)
    normed(3)
    token()
    tiny_hop(0)
    second(2)
    third(1)
    tiny_hop(1)
    second(3)
    third(2)
    tiny_hop(2)
    third(3)
    tiny_hop(3)
    tiny_hop(4)
    tiny_hop(5)
    small_end()
    line_out[...] = line.total()
    for i in range(n_t - 1):
        state["z", i].wait_recv()
        ref = z_got.at[i]
        g_out[...] += codes_in(ref, 0, g_out.shape[0], exponent_in(ref))
    waited = [state[what, i] for what in ("p", "x", "y", "x2", "y2") for i in range(n_t - 2)]
    for copy in started:
        if not any(copy is other for other in waited):
            copy.wait_send()


def tail_scratch(n_t, rows, width, columns, wide):
    i16 = jnp.int16
    half = width // 2
    part = half // 4
    hops = 3 + (n_t.bit_length() - 1)
    return [
        pltpu.VMEM((2, rows, columns), f32),
        pltpu.VMEM((width, columns), bf16),
        pltpu.VMEM((rows, width), f32),
        pltpu.VMEM((rows + 8, columns), f32),
        pltpu.VMEM((rows + 8, 2 * STATE), f32),
        pltpu.VMEM((n_t, rows, columns), bf16),
        pltpu.SemaphoreType.DMA((2, n_t)),
        pltpu.SemaphoreType.DMA,
        pltpu.VMEM((2, half + EXTRA, columns), i16),
        pltpu.VMEM((n_t, half + EXTRA, columns), i16),
        pltpu.VMEM((2, part + EXTRA, columns), i16),
        pltpu.VMEM((2, part + EXTRA, columns), i16),
        pltpu.VMEM((n_t, part + EXTRA, columns), i16),
        pltpu.VMEM((n_t, part + EXTRA, columns), i16),
        pltpu.VMEM((n_t, 2 * part, columns), f32),
        pltpu.VMEM((2, part // 2 + EXTRA, columns), i16),
        pltpu.VMEM((2, part // 2 + EXTRA, columns), i16),
        pltpu.VMEM((n_t, part // 2 + EXTRA, columns), i16),
        pltpu.VMEM((n_t, part // 2 + EXTRA, columns), i16),
        pltpu.VMEM((n_t, part, columns), f32),
        pltpu.VMEM((n_t - 1, part + EXTRA, columns), i16),
        pltpu.VMEM((n_t - 1, part + EXTRA, columns), i16),
        pltpu.VMEM((half + EXTRA, wide), i16),
        pltpu.VMEM((half, wide), f32),
        pltpu.VMEM((half + EXTRA, wide), i16),
        pltpu.VMEM((2 * part + EXTRA, wide), i16),
        pltpu.VMEM((2 * part + EXTRA, wide), i16),
        pltpu.VMEM((part + EXTRA, wide), i16),
        pltpu.VMEM((part + EXTRA, wide), i16),
        pltpu.VMEM((part, wide - 2 * STATE), f32),
        pltpu.VMEM((n_t - 1, part // n_t, 2 * STATE), f32),
        pltpu.VMEM((n_t - 1, part, wide - 2 * STATE), f32),
        pltpu.VMEM((hops, 16, width), f32),
        pltpu.VMEM((hops, 16, width), f32),
        pltpu.VMEM((3, 8, columns), f32),
        pltpu.VMEM((n_t - 1, 8, columns), f32),
        pltpu.VMEM((3, 8, columns), f32),
        pltpu.SemaphoreType.DMA((6 * n_t + 8 * n_t,)),
        pltpu.SemaphoreType.DMA((6 * n_t + 8 * n_t,)),
        *line_scratch(n_t, part, columns),
    ]


def kernel_call(kernel, grid, ins, outs, scratch=(), scalar=None, flops=0, bytes_=0, ident=None):
    def spec(shape, block, index):
        if block is pl.ANY:
            return pl.BlockSpec(memory_space=pl.ANY)
        if block is None:
            rank = len(shape)
            return pl.BlockSpec(shape, lambda i, *_, rank=rank: (0,) * rank)
        return pl.BlockSpec(block, index)

    return pl.pallas_call(
        kernel,
        grid_spec=pltpu.PrefetchScalarGridSpec(
            num_scalar_prefetch=0 if scalar is None else 1,
            grid=(grid,),
            in_specs=[spec(a.shape, b, m) for a, b, m in ins],
            out_specs=[spec(s, b, m) for s, _, b, m in outs],
            scratch_shapes=list(scratch),
        ),
        out_shape=[jax.ShapeDtypeStruct(s, d) for s, d, _, _ in outs],
        compiler_params=pltpu.CompilerParams(
            dimension_semantics=("arbitrary",),
            vmem_limit_bytes=62 * 1024 * 1024,
            **({} if ident is None else {"collective_id": ident, "has_side_effects": True}),
        ),
        cost_estimate=pl.CostEstimate(flops=flops, bytes_accessed=bytes_, transcendentals=0),
    )(*([] if scalar is None else [scalar]), *[a for a, _, _ in ins])


MESH = pl.DeviceIdType.MESH


def flip(index, bit):
    return index + bit - 2 * bit * ((index // bit) % 2)


def flip_all(index, mask):
    bit = 1
    while bit <= mask:
        if mask & bit:
            index = flip(index, bit)
        bit *= 2
    return index


class Gather:
    def __init__(self, n_t, kinds, shards, outs, local_sem, send_sem, recv_sem):
        self.n_t, self.kinds, self.shards, self.outs = n_t, kinds, shards, outs
        self.local_sem, self.send_sem, self.recv_sem = local_sem, send_sem, recv_sem
        self.dp, self.me = lax.axis_index("dp"), lax.axis_index("tensor")
        self.core, self.xn, self.yn = flip(self.dp, 1), flip(self.dp, 2), flip(self.dp, 4)
        self.diagonal = flip(self.xn, 4)
        self.others = [flip_all(self.me, r) for r in range(1, n_t)]
        self.slots, self.started = {}, []
        self.following = {}
        self.units = []
        for k, kind in enumerate(kinds):
            if kind == "flat":
                self.units.append((k, None))
            elif kind == "slab":
                self.units += [(k, r) for r in range(n_t)]
        self.late = (0, 3, 4, 5)
        self.ticks = len(self.units) + self.late[-1]

    def arrival(self, unit):
        return self.units.index(unit) + self.late[-1]

    def meet(self):
        barrier = pltpu.get_barrier_semaphore()
        for there in (self.core, self.xn, self.yn):
            pl.semaphore_signal(barrier, inc=1, device_id=(there, self.me), device_id_type=MESH)
        for there in self.others:
            pl.semaphore_signal(barrier, inc=1, device_id=(self.dp, there), device_id_type=MESH)
        pl.semaphore_wait(barrier, 3 + len(self.others))

    def place(self, k, there, slab, part=None):
        rows = self.shards[k].shape[0]
        out = self.outs[k]
        if self.kinds[k] == "line":
            return out.at[slab]
        if self.kinds[k] == "flat":
            if slab is not None:
                return out.at[there, pl.ds(pl.multiple_of(slab * rows, 8), rows)]
            if part is None:
                return out.at[there]
            return out.at[there, pl.ds(part * (self.n_t * rows // 2), self.n_t * rows // 2)]
        start, size = there * rows, rows
        if part is not None:
            start, size = start + part * (rows // 2), rows // 2
        return out.at[slab, pl.ds(pl.multiple_of(start, 16), size)]

    def slab_of(self, unit):
        return None if unit[1] is None else flip_all(self.me, unit[1])

    def copy(self, name):
        what, k, r = name
        at = self.slots.setdefault(name, len(self.slots))
        slab = self.slab_of((k, r))
        mine, there = (self.dp, self.me), None
        if what == "far":
            src, dst, there = self.shards[k], self.place(k, self.dp, self.me), (self.dp, self.others[r - 1])
        elif what in ("x", "y", "core"):
            src = self.shards[k] if r == 0 else self.place(k, self.dp, slab)
            dst, there = self.place(k, self.dp, slab), ({"x": self.xn, "y": self.yn, "core": self.core}[what], self.me)
        elif what == "xy":
            src, there = self.place(k, self.xn, slab, 0), (self.yn, self.me)
        elif what == "yx":
            src, there = self.place(k, self.yn, slab, 1), (self.xn, self.me)
        else:
            src, there = self.place(k, {"cx": self.xn, "cy": self.yn, "cd": self.diagonal}[what], slab), (self.core, self.me)
        if what not in ("far", "x", "y", "core"):
            dst = src
        return pltpu.make_async_remote_copy(
            src_ref=src, dst_ref=dst, send_sem=self.send_sem.at[at], recv_sem=self.recv_sem.at[at],
            device_id=there, device_id_type=MESH,
        )

    def start(self, *name):
        self.copy(name).start()
        self.started.append(name)

    def keep(self, k):
        return pltpu.make_async_copy(self.shards[k], self.place(k, self.dp, self.me), self.local_sem.at[k])

    def begin(self):
        for k in range(len(self.kinds)):
            self.keep(k).start()
        later = list(self.following.values())
        for k in range(len(self.kinds)):
            if k not in later:
                self.begin_far(k)

    def begin_far(self, k):
        for r in range(1, self.n_t):
            self.start("far", k, r)

    def first(self, k, r):
        if r is None:
            self.keep(k).wait()
            for other in range(1, self.n_t):
                self.copy(("far", k, other)).wait_recv()
        elif r:
            self.copy(("far", k, r)).wait_recv()
        for what in ("x", "y", "core"):
            self.start(what, k, r)
        if (k, r) in self.following:
            self.begin_far(self.following[k, r])

    def second(self, k, r):
        self.copy(("x", k, r)).wait_recv()
        self.start("xy", k, r)
        self.start("cx", k, r)
        self.copy(("y", k, r)).wait_recv()
        self.start("yx", k, r)
        self.start("cy", k, r)

    def third(self, k, r):
        self.copy(("xy", k, r)).wait_recv()
        self.copy(("yx", k, r)).wait_recv()
        self.start("cd", k, r)

    def fourth(self, k, r):
        if r == 0:
            self.keep(k).wait()
        for what in ("core", "cx", "cy", "cd"):
            self.copy((what, k, r)).wait_recv()

    def tick(self, number):
        for late, stage in zip(self.late, (self.first, self.second, self.third, self.fourth)):
            if 0 <= number - late < len(self.units):
                stage(*self.units[number - late])

    def wait_line(self, k):
        self.keep(k).wait()
        for r in range(1, self.n_t):
            self.copy(("far", k, r)).wait_recv()

    def finish(self):
        for name in self.started:
            self.copy(name).wait_send()


def gather_shape(a, kind, n_dp, n_t):
    rows, columns = a.shape
    lead = {"line": (n_t, rows), "flat": (n_dp, n_t * rows), "slab": (n_t, n_dp * rows)}[kind]
    return (*lead, columns)


def gather_scratch(kinds, n_t):
    copies = len(kinds) * (n_t - 1) + 8 * sum({"line": 0, "flat": 1, "slab": n_t}[kind] for kind in kinds)
    return [
        pltpu.SemaphoreType.DMA((len(kinds),)),
        pltpu.SemaphoreType.DMA((copies,)),
        pltpu.SemaphoreType.DMA((copies,)),
    ]


def row_of_pieces(pieces, first, size, columns):
    lane = lax.broadcasted_iota(jnp.int32, (128, columns), 0)
    place = lax.broadcasted_iota(jnp.int32, (128, columns), 1)
    pick = jnp.where(lane == first + lax.rem(place, size), 1.0, 0.0).astype(bf16)
    high = pieces.astype(bf16)
    rest = pieces - high.astype(f32)
    middle = rest.astype(bf16)
    low = (rest - middle.astype(f32)).astype(bf16)
    wide = dot(high, pick) + (dot(middle, pick) + dot(low, pick))
    row = lax.broadcasted_iota(jnp.int32, wide.shape, 0) // 8
    place = lax.broadcasted_iota(jnp.int32, wide.shape, 1) // size
    return jnp.sum(jnp.where(row == place, wide, 0.0), axis=0, keepdims=True)


FRONT_KINDS = ("line", "flat", "flat", "flat", "slab", "slab", "slab")


def front_kernel(n_t, local_heads, per_bc, per_conv, tokens, marks, line_label, *refs):
    shards, refs = refs[:7], refs[7:]
    (chan, tiny, bc, dt, w_s, w_z, w_o, nh, rstd_out, gain_out, conv_out, heads_out), refs = refs[:12], refs[12:]
    small_outs, refs = refs[:13], refs[13:]
    (ps_out, xc_out, y_out, enters, prior, ps_slot, xc_slot, y_slot, w_slot, added, decay, slab_lines), refs = refs[:12], refs[12:]
    (prior_sem, load_sem, store_sem), refs = refs[:3], refs[3:]
    carry_refs, gather_refs = refs[:4], refs[4:]
    rows, width = tokens.shape
    local = chan.shape[2]
    gather = Gather(n_t, FRONT_KINDS, shards, (chan, tiny, bc, dt, w_s, w_z, w_o), *gather_refs)
    me = gather.me
    stream_units, gate_units, out_units = ([(at, r) for r in range(n_t)] for at in (4, 5, 6))
    gather.units = gather.units[:3] + stream_units[:1] + gate_units[:1] + stream_units[1:] + out_units[:1] + gate_units[1:] + out_units[1:]
    gather.following = {(4, n_t - 2): 5, (5, n_t - 2): 6}
    gather.meet()
    gather.begin()

    def prior_copy():
        return pltpu.make_async_remote_copy(
            src_ref=tokens.at[pl.ds(rows - HALO, HALO)], dst_ref=prior, send_sem=prior_sem.at[0], recv_sem=prior_sem.at[1],
            device_id=(gather.dp, lax.rem(me + 1, n_t)), device_id_type=MESH,
        )

    @pl.when(me < n_t - 1)
    def _():
        prior_copy().start()

    done = gather.arrival((3, None)) + 1
    for number in range(done):
        gather.tick(number)

    gather.wait_line(0)

    pieces = tiny[...].reshape(-1, 128)
    gain = row_of_pieces(pieces, 0, per_bc, width)
    gain_out[...] = jnp.broadcast_to(gain, gain_out.shape)
    conv_rows = [row_of_pieces(pieces, per_bc + per_conv * tap, per_conv, 2 * STATE) for tap in range(KW + 1)]
    conv_out[...] = jnp.concatenate([*conv_rows, jnp.zeros((8 - KW - 1, 2 * STATE), f32)], axis=0)

    @pl.when(me > 0)
    def _():
        prior_copy().wait_recv()

    @pl.when(me == 0)
    def _():
        prior[...] = jnp.zeros_like(prior)

    for ref, start, size in ((prior, 0, HALO), (tokens, HALO, rows)):
        x = ref[...].astype(f32)
        r = lax.rsqrt(jnp.sum(x * x, axis=1, keepdims=True) * (1.0 / width) + epsilon)
        nh[pl.ds(start, size), :] = (x * r * gain).astype(bf16)
    rstd_out[...] = r

    own = nh[pl.ds(HALO, rows), :]
    each = shards[3].shape[0]
    raw = [dot(own, dt[:, t * each : (t + 1) * each, :].reshape(width, local_heads)) for t in range(n_t)]
    heads = [
        jnp.concatenate([chan[t, 7:8, field * local_heads : (field + 1) * local_heads] for t in range(n_t)], axis=1)
        for field in range(2)
    ]
    heads = jnp.concatenate([*heads, jnp.zeros((6, heads[0].shape[1]), f32)], axis=0)
    heads_out[...] = heads
    small_core(
        nh, bc[...].reshape(width, 2 * STATE), jnp.concatenate(raw, axis=1), conv_out[...], marks, line_label, heads, *small_outs
    )
    in_t, wide, lines, scores, through = small_outs[6], small_outs[8], small_outs[10], small_outs[11], small_outs[12]
    low = low_lanes(8)
    for t in range(n_t):
        at = t * local_heads
        slab_lines[t, 0:local_heads, :] = lines[at : at + local_heads, :]
        for pair in range(local_heads // 2):
            left = through[:, at + 2 * pair : at + 2 * pair + 1]
            right = through[:, at + 2 * pair + 1 : at + 2 * pair + 2]
            lanes = t * local + pair * 128
            decay[:, lanes : lanes + 128] = jnp.where(low, left, right)

    def lanes_of(slab):
        return pl.ds(pl.multiple_of(slab * local, 128), local)

    def load(r):
        return pltpu.make_async_copy(w_s.at[flip_all(me, r)], w_slot, load_sem)

    def stores(r):
        lanes = lanes_of(flip_all(me, r))
        pairs = ((ps_slot, ps_out), (xc_slot, xc_out), (y_slot, y_out))
        return [pltpu.make_async_copy(a.at[r % 2], o.at[:, lanes], store_sem.at[at, r]) for at, (a, o) in enumerate(pairs)]

    def stream(r):
        slab = flip_all(me, r)
        load(r).wait()
        if r >= 2:
            for copy in stores(r - 2)[:2]:
                copy.wait()
        xc, add = stream_core(
            local_heads, nh, w_slot[...], chan[slab], marks[...], wide[slab], in_t[...], ps_slot.at[r % 2]
        )
        xc_slot[r % 2] = xc
        added[:, lanes_of(slab)] = add
        for copy in stores(r)[:2]:
            copy.start()

    def inside(r):
        slab = flip_all(me, r)
        if r >= 2:
            stores(r - 2)[2].wait()
        inside_core(local_heads, xc_slot[r % 2], wide[slab], slab_lines[slab], scores, y_slot.at[r % 2])
        stores(r)[2].start()

    carry = Carry(n_t, True, added, decay, enters, *carry_refs, lag=3)
    for r in range(n_t):
        while done <= gather.arrival((4, r)):
            gather.tick(done)
            done += 1
        load(r).start()
        stream(r)
        if r + 1 < n_t:
            inside(r)
    carried = 0

    def carry_on(count):
        for number in range(carried, min(carried + count, carry.ticks)):
            carry.tick(number)
        return min(carried + count, carry.ticks)

    carried = carry_on(3)
    inside(n_t - 1)
    while done < gather.ticks or carried < carry.ticks:
        if done < gather.ticks:
            gather.tick(done)
            done += 1
        carried = carry_on(3)
    carry.drain(carry.ticks)
    for r in range(max(0, n_t - 2), n_t):
        for copy in stores(r):
            copy.wait()

    @pl.when(me < n_t - 1)
    def _():
        prior_copy().wait_send()

    gather.finish()


def front_scratch(n_t, rows, width, local, local_heads, chunks, chunk):
    return [
        pltpu.VMEM((HALO, width), bf16),
        pltpu.VMEM((2, rows + HALO, local), f32),
        pltpu.VMEM((2, rows, local), f32),
        pltpu.VMEM((2, rows, local), f32),
        pltpu.VMEM((width, local), bf16),
        pltpu.VMEM((STATE, n_t * local), f32),
        pltpu.VMEM((8, n_t * local), f32),
        pltpu.VMEM((n_t, (local_heads + 7) // 8 * 8, rows), f32),
        pltpu.SemaphoreType.DMA((2,)),
        pltpu.SemaphoreType.DMA,
        pltpu.SemaphoreType.DMA((3, n_t)),
        *carry_scratch(chunks, chunk),
        *gather_scratch(FRONT_KINDS, n_t),
    ]


def adam_update(weight, grad, first, second, rate, decay):
    first_new = beta_first * first + (1.0 - beta_first) * grad
    second_new = beta_second * second + (1.0 - beta_second) * grad * grad
    first_hat = first_new / (1.0 - beta_first**STEP)
    second_hat = second_new / (1.0 - beta_second**STEP)
    weight_new = weight * (1.0 - rate * decay) - rate * first_hat / (
        jnp.sqrt(second_hat) + adam_epsilon
    )
    return (weight_new, first_new, second_new)


def xor_pairs(size, mask):
    return [(i, i ^ mask) for i in range(size)]


def tied(value, *others):
    return lax.optimization_barrier((value, *others))[0]


class PairSum:
    def __init__(self, x, y, keep, me):
        self.count, rows, self.columns = keep.shape
        self.rows = rows // 2
        self.keep, self.me = keep, me
        self.x = lax.ppermute(x, "dp", xor_pairs(8, 2))
        self.y = lax.ppermute(y, "dp", xor_pairs(8, 4))

    def call(self, kernel, ins, outs, scalar=None):
        def each(rows):
            return (None, rows, self.columns), lambda i, *_: (i, 0, 0)

        def at(rows):
            return (None, rows, self.columns), (lambda i, m: (m[0] ^ i, 0, 0)) if scalar is not None else each(rows)[1]

        return kernel_call(
            kernel,
            self.count,
            [(a, *at(a.shape[1])) for a in ins],
            [
                ((self.count, rows, self.columns), dtype, *each(rows))
                if lead is None
                else ((rows, self.columns), dtype, None, None)
                for rows, dtype, lead in outs
            ],
            scalar=scalar,
        )

    def over_yx(self):
        i16, rows = jnp.int16, self.rows
        outs = [(rows // 2 + EXTRA, i16, None), (rows // 2 + EXTRA, i16, None), (rows, f32, None)]
        y, x, self.keep = self.call(cross_sum, [self.keep, self.x, self.y], outs)
        self.y = lax.ppermute(y, "dp", xor_pairs(8, 4))
        self.x = lax.ppermute(x, "dp", xor_pairs(8, 2))
        return x, y

    def over_z(self):
        rows = self.rows
        self.own, z = self.call(
            plane_sum_kernel,
            [self.keep, self.y, self.x],
            [(rows, f32, 0), (rows + EXTRA, jnp.int16, None)],
            scalar=self.me,
        )
        return self.own, z


def gather_plain(shard, kind):
    if kind == "flat":
        return lax.all_gather(lax.all_gather(shard, "tensor", axis=0, tiled=True), "dp", axis=0)
    lines = lax.all_gather(shard, "tensor", axis=0)
    return lines if kind == "line" else lax.all_gather(lines, "dp", axis=1, tiled=True)


def scatter_plain(part):
    own = lax.psum_scatter(part, "dp", scatter_dimension=1, tiled=True)
    return lax.psum_scatter(own, "tensor", scatter_dimension=0, tiled=True)[0]


def body(
    tokens,
    cotangent,
    lengths,
    in_weight,
    in_first,
    in_second,
    dt_weight,
    dt_first,
    dt_second,
    bc_weight,
    bc_first,
    bc_second,
    out_weight,
    out_first,
    out_second,
    norm_gain,
    gain_first,
    gain_second,
    bc_conv,
    conv_first,
    conv_second,
    x_channel,
    channel_first,
    channel_second,
    head_params,
    head_first,
    head_second,
):
    n_dp, n_t = lax.axis_size("dp"), lax.axis_size("tensor")
    me = lax.axis_index("tensor")
    rows, width = tokens.shape
    local = x_channel.shape[1]
    inner = local * n_t
    local_heads = head_params.shape[1]
    all_heads = local_heads * n_t
    cb = local
    per, blocks, hb = 1, n_t, local_heads
    narrow = 512
    steps_in, hn = inner // narrow, narrow // PWIDTH
    own = me * rows
    up = [(i, i + 1) for i in range(n_t - 1)]
    down = [(i + 1, i) for i in range(n_t - 1)]

    paired = n_dp == 8 and n_t == 4
    dp_me = lax.axis_index("dp")
    per_bc, per_conv = bc_weight.shape[0], bc_conv.shape[1]

    ends_of = jnp.cumsum(lengths[0])

    def labels_at(places):
        found = jnp.sum((places[:, None] >= ends_of[None, :]).astype(jnp.int32), axis=1)
        return jnp.where(places < 0, -1, found)

    span = labels_at(own + jnp.arange(-HALO, rows + 8, dtype=jnp.int32))
    labels = span[HALO : HALO + rows]
    valid = (own + jnp.arange(rows, dtype=jnp.int32) < ends_of[-1]).astype(f32)[:, None]
    masks = jnp.stack(
        [(span[HALO - o : HALO - o + rows + 8] == span[HALO:]).astype(f32) for o in (1, 2, 3)], axis=1
    )
    before, last = span[HALO - 1], labels[rows - 1]
    keep = (labels == before).astype(f32)[:, None]
    tail = (labels == last).astype(f32)[:, None]
    through = (last == before).astype(f32)
    marks = jnp.concatenate(
        [masks[:rows], labels.astype(f32)[:, None], keep, tail, jnp.full((rows, 1), through), jnp.zeros((rows, 1), f32)],
        axis=1,
    )
    line_label = jnp.broadcast_to(labels.astype(f32)[None], (8, rows))

    line = jnp.concatenate(
        [
            x_channel,
            jnp.repeat(head_params[2], PWIDTH)[None],
            jnp.pad(head_params[:2].reshape(1, -1), ((0, 0), (0, local - 2 * local_heads))),
        ],
        axis=0,
    )
    tiny = jnp.concatenate([norm_gain, bc_conv.reshape(-1)])
    tiny = jnp.pad(tiny[None], ((0, 7), (0, 128 - tiny.size)))
    shards = [
        (line, "line"),
        (tiny, "flat"),
        (bc_weight.astype(bf16), "flat"),
        (dt_weight.astype(bf16), "flat"),
        (in_weight[:, 1].astype(bf16), "slab"),
        (in_weight[:, 0].astype(bf16), "slab"),
        (out_weight.T.astype(bf16), "slab"),
    ]
    small_shapes = (
        (rows + HALO, 2 * STATE),
        (rows, 2 * STATE),
        (rows, all_heads),
        (rows, all_heads),
        (rows, STATE),
        (rows, STATE),
        (STATE, rows),
        (STATE, rows),
        (n_t, rows, 4 * local_heads),
        (steps_in, rows, 4 * hn),
        (all_heads, rows),
        (rows, rows),
        (8, all_heads),
    )
    if paired:
        gathers = [(gather_shape(a, kind, n_dp, n_t), a.dtype) for a, kind in shards]
        got = kernel_call(
            functools.partial(front_kernel, n_t, local_heads, per_bc, per_conv),
            1,
            [
                (tokens, None, None),
                (marks, None, None),
                (line_label, None, None),
                *[(a, pl.ANY, None) for a, _ in shards],
            ],
            [
                *[(s, d, None, None) for s, d in gathers[:4]],
                *[(s, d, pl.ANY, None) for s, d in gathers[4:]],
                ((rows + HALO, width), bf16, None, None),
                ((rows, 1), f32, None, None),
                ((8, width), f32, None, None),
                ((8, 2 * STATE), f32, None, None),
                ((8, all_heads), f32, None, None),
                *[(s, f32, None, None) for s in small_shapes],
                ((rows + HALO, inner), f32, pl.ANY, None),
                ((rows, inner), f32, pl.ANY, None),
                ((rows, inner), f32, pl.ANY, None),
                ((STATE, inner), f32, None, None),
            ],
            scratch=front_scratch(n_t, rows, width, local, local_heads, steps_in, narrow),
            ident=0,
        )
        chan, _, bc_low, dt_low, w_s, w_z, w_o, normed_ext, rstd_in, gain_rows, conv_pad, heads_pad, *got = got
        bcp, bc_pre, step_raw, step, in_mat, read_mat, in_t, read_t, cols, cols_n, lines, scores, through_all, *got = got
        ps, xc, inside, state = got
        bc_low = bc_low.reshape(width, -1)
        dt_low = dt_low.reshape(n_dp, n_t, -1, local_heads).swapaxes(1, 2).reshape(width, all_heads)
        normed = normed_ext[HALO:]
        gain, conv_full = gain_rows[0], conv_pad[: KW + 1]
    else:
        chan, tiny, bc_low, dt_low, w_s, w_z, w_o = [gather_plain(a, kind) for a, kind in shards]
        bc_low = bc_low.reshape(width, -1)
        dt_low = dt_low.reshape(n_dp, n_t, -1, local_heads).swapaxes(1, 2).reshape(width, all_heads)
        tiny = tiny.reshape(n_dp * n_t, 8, 128)[:, 0]
        gain = tiny[:, :per_bc].reshape(width)
        conv_full = tiny[:, per_bc : per_bc + (KW + 1) * per_conv].reshape(-1, KW + 1, per_conv)
        conv_full = conv_full.swapaxes(0, 1).reshape(KW + 1, -1)
        conv_pad = jnp.pad(conv_full, ((0, 3), (0, 0)))
        heads = chan[:, 7, : 2 * local_heads].reshape(n_t, 2, local_heads).swapaxes(0, 1).reshape(2, all_heads)
        heads_pad = jnp.pad(heads, ((0, 6), (0, 0)))
        gain_rows = jnp.broadcast_to(gain[None], (8, width))
        prior = lax.ppermute(tokens[-HALO:], "tensor", up)
        x_ext = jnp.concatenate([prior, tokens], axis=0).astype(f32)
        rstd_ext = lax.rsqrt(jnp.mean(x_ext * x_ext, axis=1, keepdims=True) + epsilon)
        normed_ext = (x_ext * rstd_ext * gain[None, :]).astype(bf16)
        rstd_in, normed = rstd_ext[HALO:], normed_ext[HALO:]
        got = kernel_call(
            small_kernel,
            1,
            [(a, None, None) for a in (normed_ext, bc_low, dt_low, conv_pad, marks, line_label, heads_pad)],
            [(s, f32, None, None) for s in small_shapes],
        )
        bcp, bc_pre, step_raw, step, in_mat, read_mat, in_t, read_t, cols, cols_n, lines, scores, through_all = got
    back = cotangent.astype(f32)
    masked = (back * valid).astype(bf16)
    if paired:
        order = dp_me ^ jnp.array([0, 2, 4, 6, 1, 3, 5, 7], jnp.int32)
    else:
        order = jnp.arange(n_dp, dtype=jnp.int32)

    def turned(a):
        return a.T.reshape(n_dp, -1, rows)[order].reshape(width, rows)

    normed_t, masked_t = turned(normed), turned(masked)

    decay_all = through_all[0]

    def slab(i, *_):
        return (i // per, 0, i % per)

    wspec = (None, width, cb), slab
    cspec = (None, 8, cb), slab
    colspec = (None, rows, 4 * hb), lambda i, *_: (i, 0, 0)
    colnspec = (None, rows, 4 * hn), lambda i, *_: (i, 0, 0)
    linespec = (hn, rows), lambda i, *_: (i, 0)
    chnspec = (rows, narrow), lambda i, *_: (0, i)
    chspec = (rows, cb), lambda i, *_: (0, i)
    stspec = (STATE, cb), lambda i, *_: (0, i)
    st_shape = (STATE, inner)
    decay_row = jnp.broadcast_to(jnp.repeat(decay_all, PWIDTH)[None], (8, inner))
    steps = blocks
    if paired:
        steps = blocks + 1

        def now(spec):
            return spec[0], lambda i, *_: spec[1](jnp.minimum(i, blocks - 1))

        def late(rows):
            return (None, rows, local), lambda i, *_: (jnp.maximum(i - 1, 0), 0, 0)

        part = width // 8
        dw_specs = [
            ((n_t, part + EXTRA, local), jnp.int16, *late(part + EXTRA)),
            ((n_t, part + EXTRA, local), jnp.int16, *late(part + EXTRA)),
            ((n_t, 2 * part, local), f32, *late(2 * part)),
        ]
        dw_scratch = core_pair_scratch(n_t, width // 2, local)
    else:
        now = tuple
        dw_specs = [((n_t, width, local), f32, *wspec)]
        dw_scratch = []
    full = (None, None)
    big = 2 * rows * width * inner

    if not paired:
        ps, xc, added = kernel_call(
            functools.partial(stream_kernel, hb),
            blocks,
            [(normed_ext, *full), (w_s, *wspec), (chan, *cspec), (marks, *full), (cols, *colspec), (in_t, *full)],
            [
                ((rows + HALO, inner), f32, (rows + HALO, cb), lambda i, *_: (0, i)),
                ((rows, inner), f32, *chspec),
                (st_shape, f32, *stspec),
            ],
        )
        inside, state = kernel_call(
            functools.partial(inside_kernel, hn, n_t),
            steps_in,
            [
                (xc, *chnspec),
                (cols_n, *colnspec),
                (lines, *linespec),
                (scores, *full),
                (added, *full),
                (decay_row, *full),
            ],
            [((rows, inner), f32, *chnspec), (st_shape, f32, *full)],
            scratch=carry_scratch(steps_in, narrow),
            ident=1,
        )
    z, y, squares = kernel_call(
        functools.partial(carry_kernel, hb),
        blocks,
        [
            (normed_ext, *full),
            (w_z, *wspec),
            (inside, *chspec),
            (xc, *chspec),
            (cols, *colspec),
            (read_mat, *full),
            (state, *stspec),
            (chan, *cspec),
        ],
        [
            ((rows, inner), f32, *chspec),
            ((rows, inner), f32, *chspec),
            ((rows, 128), f32, *full),
        ],
        flops=2 * big,
        bytes_=8 * width * inner,
    )
    rstd = lax.rsqrt(jnp.sum(squares, axis=1, keepdims=True) / inner + epsilon)

    rowspec = (1, cb), lambda i, *_: (0, i)
    mixed, d_gated, d_gain_gate, totals, *dw_o = kernel_call(
        functools.partial(out_kernel, blocks),
        steps,
        [
            (z, *now(chspec)),
            (y, *now(chspec)),
            (xc, *now(chspec)),
            (chan, *now(cspec)),
            (rstd, *full),
            (w_o, *now(wspec)),
            (masked, *full),
            (masked_t, *full),
            (tokens, *full),
            (valid, *full),
        ],
        [
            ((rows, width), bf16, *full),
            ((rows, inner), f32, *now(chspec)),
            ((1, inner), f32, *now(rowspec)),
            ((rows, 128), f32, *full),
            *dw_specs,
        ],
        scratch=[pltpu.VMEM((rows, width), f32), *dw_scratch],
        ident=5 if paired else None,
        flops=3 * big,
        bytes_=8 * width * inner,
    )
    turn = me[None].astype(jnp.int32)
    sum_o = PairSum(*dw_o, turn) if paired else None
    total = jnp.sum(totals, axis=1, keepdims=True)

    dy, dh, back_added, skip_rows, *dw_z = kernel_call(
        functools.partial(gate_kernel, blocks, hb, inner),
        steps,
        [
            (z, *now(chspec)),
            (y, *now(chspec)),
            (xc, *now(chspec)),
            (chan, *now(cspec)),
            (rstd, *full),
            (total, *full),
            (d_gated, *now(chspec)),
            (w_z, *now(wspec)),
            (normed_t, *full),
            (cols, *now(colspec)),
            (read_t, *full),
        ],
        [
            ((rows, inner), f32, *now(chspec)),
            ((rows, width), f32, *full),
            (st_shape, f32, *now(stspec)),
            ((1, inner), f32, *now(rowspec)),
            *dw_specs,
        ],
        scratch=dw_scratch,
        ident=6 if paired else None,
        flops=2 * big,
        bytes_=8 * width * inner,
    )
    if paired:
        sum_z = PairSum(*dw_z, turn)
        dy = tied(dy, *sum_o.over_yx())

    d_inside, sums, d_in_part, d_read_part, back_state = kernel_call(
        functools.partial(inside_back_kernel, hn, n_t),
        steps_in,
        [
            (dy, *chnspec),
            (xc, *chnspec),
            (y, *chnspec),
            (cols_n, *colnspec),
            (lines, *linespec),
            (scores, *full),
            (marks, *full),
            (line_label, *full),
            (in_mat, *full),
            (read_mat, *full),
            (back_added, *full),
            (decay_row, *full),
        ],
        [
            ((rows, inner), f32, *chnspec),
            ((steps_in, rows, hn), f32, (None, rows, hn), lambda i, *_: (i, 0, 0)),
            ((rows, STATE), f32, *full),
            ((rows, STATE), f32, *full),
            (st_shape, f32, *full),
        ],
        scratch=[pltpu.VMEM((rows, rows), f32), *carry_scratch(steps_in, narrow)],
        ident=2,
        flops=8 * big,
        bytes_=8 * width * inner,
    )
    if paired:
        sum_o.keep, sum_z.keep = tied(sum_o.keep, d_inside), tied(sum_z.keep, d_inside)
        own_o, pay_o = sum_o.over_z()
        d_inside = tied(d_inside, own_o, pay_o, *sum_z.over_yx())
        line_in = [(pay_o, *full), (own_o, *full)]
        line_get = [(own_o.shape, f32, *full)]
        line_refs = line_scratch(n_t, width // n_dp, local)
    else:
        line_in = line_get = line_refs = []
    d_pre, more_sums, tap_rows, d_in_mat, d_read_mat, *g_o = kernel_call(
        functools.partial(carry_back_kernel, hb, n_t),
        blocks,
        [
            (dy, *chspec),
            (xc, *chspec),
            (ps, (rows + HALO, cb), lambda i, *_: (0, i)),
            (d_inside, *chspec),
            (cols, *colspec),
            (in_mat, *full),
            (back_state, *stspec),
            (state, *stspec),
            (chan, *cspec),
            (marks, *full),
            (d_in_part, *full),
            (d_read_part, *full),
            *line_in,
        ],
        [
            ((rows, inner), f32, *chspec),
            ((blocks, rows, 2 * hb), f32, (None, rows, 2 * hb), lambda i, *_: (i, 0, 0)),
            ((8, inner), f32, (8, cb), lambda i, *_: (0, i)),
            ((rows, STATE), f32, *full),
            ((rows, STATE), f32, *full),
            *line_get,
        ],
        scratch=line_refs,
        ident=7 if paired else None,
        flops=2 * big,
        bytes_=8 * width * inner,
    )
    halo = lax.ppermute(d_pre[:8], "tensor", down)
    d_bc_pre, d_dt, d_heads, d_conv = kernel_call(
        post_kernel,
        1,
        [
            (a, None, None)
            for a in (
                sums,
                more_sums,
                step_raw,
                step,
                heads_pad,
                through_all,
                tap_rows,
                d_in_mat,
                d_read_mat,
                bc_pre,
                bcp,
                marks,
            )
        ],
        [
            ((rows, 2 * STATE), f32, None, None),
            ((rows, all_heads), bf16, None, None),
            ((8, all_heads), f32, None, None),
            ((8, 2 * STATE), f32, None, None),
        ],
    )
    bc_halo = lax.ppermute(d_bc_pre[:8], "tensor", down)
    head_row = jnp.pad(d_heads[:2, :, None], ((0, 0), (0, 0), (0, PWIDTH - 1)))
    head_row = head_row[0] + jnp.roll(head_row[1], 1, axis=1)
    by_t = jnp.concatenate([tap_rows[: KW + 1], d_gain_gate, skip_rows, head_row.reshape(1, inner)], axis=0)
    by_t = by_t.reshape(8, n_t, local).swapaxes(0, 1)
    wide = (2 * STATE + all_heads + 127) // 128 * 128
    per_dp = width // n_dp
    if paired:
        sum_z.keep = tied(sum_z.keep, d_pre)
        own_z, pay_z = sum_z.over_z()
        w_small = jnp.pad(jnp.concatenate([bc_low, dt_low], axis=1), ((0, 0), (0, wide - 2 * STATE - all_heads)))
        g_s, token_grad, g_bc, g_dt, by_t, tiny, far_z = kernel_call(
            functools.partial(tail_kernel, n_t),
            1,
            [
                (d_pre, pl.ANY, None),
                (w_s, pl.ANY, None),
                (dh, pl.ANY, None),
                (pay_z, pl.ANY, None),
                *[
                    (a, None, None)
                    for a in (
                        halo,
                        chan,
                        masks,
                        normed_t,
                        d_bc_pre,
                        bc_halo,
                        conv_pad,
                        d_dt,
                        w_small,
                        by_t,
                        d_conv,
                        tokens,
                        cotangent,
                        rstd_in,
                        gain_rows,
                    )
                ],
            ],
            [
                ((per_dp, local), f32, None, None),
                ((rows, width), bf16, None, None),
                ((per_bc, 2 * STATE), f32, None, None),
                ((per_dp, wide - 2 * STATE), f32, None, None),
                ((8, local), f32, None, None),
                ((16, width), f32, None, None),
                ((per_dp, local), f32, None, None),
            ],
            scratch=tail_scratch(n_t, rows, width, local, wide),
            ident=3,
            flops=10 * big,
            bytes_=30 * width * inner,
        )
        g_o, g_z = g_o[0], own_z + far_z
        d_gain, d_conv = tiny[0], tiny[8 : 8 + KW + 1, : 2 * STATE]
    else:
        dh, *dw_s = kernel_call(
            stream_back_kernel,
            blocks,
            [
                (d_pre, *chspec),
                (halo, (8, cb), lambda i, *_: (0, i)),
                (chan, *cspec),
                (masks, *full),
                (w_s, *wspec),
                (normed_t, *full),
                (dh, *full),
            ],
            [
                ((rows, width), f32, *full),
                *dw_specs,
            ],
            scratch=[pltpu.VMEM((rows + 8, cb), f32)],
        )
        bc_ext = jnp.concatenate([d_bc_pre, bc_halo], axis=0)
        d_bc = conv_full[KW - 1][None, :] * d_bc_pre
        for o in range(1, KW):
            d_bc = d_bc + conv_full[KW - 1 - o][None, :] * (masks[o : o + rows, o - 1 : o] * bc_ext[o : o + rows])
        d_bc = d_bc.astype(bf16)
        d_normed = dh + dot(d_bc, bc_low, NT) + dot(d_dt, dt_low, NT)
        scaled = gain[None, :] * d_normed
        token_grad = (
            back + rstd_in * scaled - x_ext[HALO:] * rstd_in**3 * jnp.sum(x_ext[HALO:] * scaled, axis=1, keepdims=True) / width
        ).astype(bf16)
        d_gain = lax.psum(jnp.sum(x_ext[HALO:] * rstd_in * d_normed, axis=0), ("dp", "tensor"))
        d_conv = lax.psum(d_conv[: KW + 1], ("dp", "tensor"))
        g_small = dot(normed_t, jnp.concatenate([d_bc, d_dt], axis=1)).reshape(n_dp, per_dp, -1)
        g_small = lax.psum(lax.psum_scatter(g_small, "dp", scatter_dimension=0), "tensor")
        by_t = lax.psum(lax.psum_scatter(by_t, "tensor", scatter_dimension=0), "dp")
        g_bc = lax.dynamic_slice(g_small, (me * per_bc, 0), (per_bc, 2 * STATE))
        g_dt = g_small[:, 2 * STATE :]
        g_o, g_z, g_s = scatter_plain(dw_o[0]), scatter_plain(dw_z[0]), scatter_plain(dw_s[0])
    place = dp_me * n_t + me
    g_dt = lax.dynamic_slice(g_dt, (0, me * local_heads), (per_dp, local_heads))
    g_gain = lax.dynamic_slice(d_gain, (place * per_bc,), (per_bc,))
    g_conv = lax.dynamic_slice(d_conv, (0, place * per_conv), (KW + 1, per_conv))
    g_channel = by_t[: KW + 2]
    ends = by_t[7].reshape(local_heads, PWIDTH)
    g_head = jnp.stack([ends[:, 0], ends[:, 1], jnp.sum(by_t[6].reshape(local_heads, PWIDTH), axis=1)])
    g_in = jnp.stack([g_z, g_s], axis=1)
    in_new = adam_update(in_weight, g_in, in_first, in_second, rate_matrix, decay_matrix)
    dt_new = adam_update(dt_weight, g_dt, dt_first, dt_second, rate_matrix, decay_matrix)
    bc_new = adam_update(bc_weight, g_bc, bc_first, bc_second, rate_matrix, decay_matrix)
    out_new = adam_update(out_weight, g_o.T, out_first, out_second, rate_matrix, decay_matrix)
    gain_new = adam_update(norm_gain, g_gain, gain_first, gain_second, rate_small, 0.0)
    conv_new = adam_update(bc_conv, g_conv, conv_first, conv_second, rate_small, 0.0)
    channel_new = adam_update(x_channel, g_channel, channel_first, channel_second, rate_small, 0.0)
    head_new = adam_update(head_params, g_head, head_first, head_second, rate_small, 0.0)
    return (
        mixed,
        token_grad,
        *in_new,
        *dt_new,
        *bc_new,
        *out_new,
        *gain_new,
        *conv_new,
        *channel_new,
        *head_new,
    )


def solution(mesh):
    return jax.shard_map(
        body,
        mesh=mesh,
        in_specs=(
            P(("dp", "tensor"), None),
            P(("dp", "tensor"), None),
            P("dp", None),
            P("dp", None, "tensor"),
            P("dp", None, "tensor"),
            P("dp", None, "tensor"),
            P("dp", "tensor"),
            P("dp", "tensor"),
            P("dp", "tensor"),
            P(("dp", "tensor"), None),
            P(("dp", "tensor"), None),
            P(("dp", "tensor"), None),
            P("tensor", "dp"),
            P("tensor", "dp"),
            P("tensor", "dp"),
            P(("dp", "tensor")),
            P(("dp", "tensor")),
            P(("dp", "tensor")),
            P(None, ("dp", "tensor")),
            P(None, ("dp", "tensor")),
            P(None, ("dp", "tensor")),
            P(None, "tensor"),
            P(None, "tensor"),
            P(None, "tensor"),
            P(None, "tensor"),
            P(None, "tensor"),
            P(None, "tensor"),
        ),
        out_specs=(
            P(("dp", "tensor"), None),
            P(("dp", "tensor"), None),
            P("dp", None, "tensor"),
            P("dp", None, "tensor"),
            P("dp", None, "tensor"),
            P("dp", "tensor"),
            P("dp", "tensor"),
            P("dp", "tensor"),
            P(("dp", "tensor"), None),
            P(("dp", "tensor"), None),
            P(("dp", "tensor"), None),
            P("tensor", "dp"),
            P("tensor", "dp"),
            P("tensor", "dp"),
            P(("dp", "tensor")),
            P(("dp", "tensor")),
            P(("dp", "tensor")),
            P(None, ("dp", "tensor")),
            P(None, ("dp", "tensor")),
            P(None, ("dp", "tensor")),
            P(None, "tensor"),
            P(None, "tensor"),
            P(None, "tensor"),
            P(None, "tensor"),
            P(None, "tensor"),
            P(None, "tensor"),
        ),
        check_vma=False,
    )
```
